32 devices in a mesh: gz: 4 (over y, x), dom: 8 (over z, core).
Axes of the slice: x: 2, y: 2, z: 4, core: 2. Of those that a mesh axis runs over, the one named last changes fastest.
Arguments:
- volume: float32 [768, 4, 384], P('gz'), may hold values from -6 to 6
- observed: bfloat16 [512, 4, 384], P(('gz', 'dom')), may hold values from -6 to 6
- ctf_table: float32 [32, 2, 384], replicated, may hold values from -1 to 1
- ctf_class: int32 [512], P(('gz', 'dom')), may hold values from 0 to 31
- bin_ids: int32 [512], P(('gz', 'dom')), may hold values from 0 to 63
Outputs:
- pose_score: float32 [512], P(('gz', 'dom'))
- backprojection: float32 [768, 4, 384], P(('gz', 'dom'))
The draws below stay inside these ranges and needn't reach their ends.
All inputs are finite; a program needn't handle non-finite values.
Results may differ from the reference program's by a relative error of at most 0.0034.
Values may be sent and summed in bfloat16 or wider, within the bound.
No kernel may reach another device: no remote copies, remote signals or barrier semaphores. Data moves between devices by JAX's collectives and lax.ppermute only.
A program may use at most 64 MiB of HBM per device.

```python
import math
import jax
import jax.numpy as jnp
import numpy as np
from jax import lax

NZ = 768
X = 384
U = 384
Y = 2
NB_DEV = 8
NCTF = 32
ITERS = 3
NB = 64
NPART = 512
N_DOM = 8


def with_ends(result, key, least, high):
    longest = result.shape.index(max(result.shape))
    spots = []
    for shift in (0, 1):
        where = [jax.random.randint(jax.random.fold_in(key, axis), (), 0, length) for axis, length in enumerate(result.shape)]
        where[longest] = (where[longest] + shift) % result.shape[longest]
        spots.append(tuple(where))
    return result.at[spots[0]].set(least).at[spots[1]].set(high)


def level_of(stream_key, extent, cuts, low, high):
    factor_of, own = 1.0, jax.random.fold_in(stream_key, 6)
    for dim, blocks in cuts:
        heights = jnp.exp(jax.random.uniform(jax.random.fold_in(own, dim), (blocks,), jnp.float32, low / len(cuts), high / len(cuts)))
        factor_of = factor_of * jnp.repeat(heights, extent[dim] // blocks).reshape([-1 if axis == dim else 1 for axis in range(len(extent))])
    return factor_of


def rank_bounds(number_of, slope):
    portions = [(1 << 20) // math.isqrt(standing ** slope) + 1 for standing in range(1, number_of + 1)]
    deviation = 1 + sum(portions) // (1 << 30)
    return np.cumsum(np.array([max(1, weight // deviation) for weight in portions]))


def ranked_ids(rng, dims, amount, slope):
    grid = rank_bounds(amount, slope)
    lot = jax.random.randint(jax.random.fold_in(rng, 1), dims, 0, int(grid[amount - 1]))
    grade = jnp.searchsorted(jnp.asarray(grid, jnp.int32), lot, side="right")
    return jax.random.permutation(jax.random.fold_in(rng, 2), amount)[grade].astype(jnp.int32)


def normal_values(key, extent, deviation, limit, split=(), held_as=jnp.bfloat16):
    factor_of = level_of(key, extent, split, -0.22, 0.18) if split else 1.0
    array = jax.random.normal(key, extent, jnp.float32) * deviation * factor_of
    return jnp.minimum(jnp.maximum(array, -limit), limit).astype(held_as)


def setup_inputs(seed: int = 0) -> dict:
    key_of = jax.random.split(jax.random.key(seed), 6)
    volume = normal_values(key_of[0], (NZ, 2 * Y, X), 1.0, 6.0, ((0, 4),), jnp.float32)
    observed = normal_values(key_of[1], (NPART, 2 * Y, U), 1.0, 6.0, ((0, 32),))
    ctf_table = jnp.clip(jax.random.uniform(key_of[2], (NCTF, Y, U), jnp.float32, -1.0, 1.0), -1.0, 1.0)
    ctf_class = with_ends(jax.random.randint(key_of[3], (NPART,), 0, NCTF), jax.random.fold_in(key_of[3], 1), 0, NCTF - 1).astype(jnp.int32)
    bin_ids = with_ends(ranked_ids(key_of[4], (NPART,), NB, 2), jax.random.fold_in(key_of[4], 3), 0, NB - 1).astype(jnp.int32)
    return dict(volume=volume, observed=observed, ctf_table=ctf_table, ctf_class=ctf_class, bin_ids=bin_ids)


def kernel(offset):
    inside = jnp.abs(offset) < 1.0
    falloff = 1.0 - offset * offset
    return (jnp.where(inside, falloff * falloff, 0.0), jnp.where(inside, -4.0 * offset * falloff, 0.0))

def project(field, bin_index):
    total_bins = NB_DEV * N_DOM
    tilt_angle = -0.5 * math.pi + math.pi * (bin_index.astype(jnp.float32) + 0.5) / total_bins
    sine_value = jnp.sin(tilt_angle)
    cosine = jnp.cos(tilt_angle)
    radius = jnp.arange(U).astype(jnp.float32)
    centre = 0.5 * NZ + radius * sine_value
    lower_plane = jnp.clip(jnp.floor(centre).astype(jnp.int32), 0, NZ - 2)
    planes = lower_plane[:, None] + jnp.arange(2, dtype=jnp.int32)[None, :]
    z_value, z_slope = kernel(planes.astype(jnp.float32) - centre[:, None])
    z_slope = z_slope * (-radius * cosine / U)[:, None]
    x_value, x_slope = kernel(jnp.arange(X).astype(jnp.float32)[None, :] - (radius * cosine)[:, None])
    x_slope = x_slope * (radius * sine_value / U)[:, None]
    picked = field[planes]
    x_sums = jnp.einsum('upcx,ux->upc', picked, x_value, precision=lax.Precision.HIGHEST)
    x_slopes = jnp.einsum('upcx,ux->upc', picked, x_slope, precision=lax.Precision.HIGHEST)
    leading = jnp.einsum('upc,up->cu', x_sums, z_value, precision=lax.Precision.HIGHEST)
    second = jnp.einsum('upc,up->cu', x_sums, z_slope, precision=lax.Precision.HIGHEST) + jnp.einsum('upc,up->cu', x_slopes, z_value, precision=lax.Precision.HIGHEST)
    return (leading, second)

def reference(volume, observed, ctf_table, ctf_class, bin_ids):
    total_bins = NB_DEV * N_DOM
    stacked_rows = 2 * Y
    bin_range = jnp.arange(total_bins, dtype=jnp.int32)
    slices = lax.map(lambda bin_index: jnp.concatenate(project(volume, bin_index), 0), bin_range)
    slices = slices.astype(jnp.bfloat16).astype(jnp.float32)
    chosen = slices[bin_ids]
    contrast = ctf_table[ctf_class]
    contrast = jnp.concatenate([contrast, contrast], 1)
    measured = observed.astype(jnp.float32)
    predicted = contrast * chosen[:, :stacked_rows]
    tangent = contrast * chosen[:, stacked_rows:]
    curvature = lax.optimization_barrier(jnp.sum(tangent * tangent, axis=(1, 2))) + 1e-05
    shift = jnp.zeros((measured.shape[0],), jnp.float32)
    for iteration in range(ITERS):
        residual_map = measured - predicted - shift[:, None, None] * tangent
        shift = shift + 0.5 * lax.optimization_barrier(jnp.sum(residual_map * tangent, axis=(1, 2))) / curvature
    pose_score = shift * jnp.sqrt(curvature)
    weighted = contrast * measured
    contributions = jnp.concatenate([weighted, shift[:, None, None] * weighted], 1)
    bin_sums = jax.ops.segment_sum(contributions, bin_ids, num_segments=total_bins)

    def accumulate(running, bin_index):
        summed = bin_sums[bin_index]
        pullback = jax.vjp(lambda field: project(field, bin_index), volume)[1]
        gradient = pullback((summed[:stacked_rows], summed[stacked_rows:]))[0]
        return (running + gradient, None)
    backprojection, unused = lax.scan(accumulate, jnp.zeros(volume.shape, jnp.float32), bin_range)
    return (pose_score, backprojection)
```

```python
import functools
import math

import jax
import jax.numpy as jnp
import numpy as np
from jax import lax
from jax.experimental import pallas as pl
from jax.experimental.pallas import tpu as pltpu
from jax.sharding import PartitionSpec as P

NZ = 768
NB_DEV = 8
NCTF = 32
ITERS = 3
EPS = 1e-05
TILE = 128
GROUP = 4
CHUNK = 512
VMEM = 56 * 2**20
f32 = jnp.float32
bf16 = jnp.bfloat16
NT = (((1,), (1,)), ((), ()))
TN = (((0,), (0,)), ((), ()))


def round_up(n, m):
    return -(-n // m) * m


def make_plan(devices, bins, samples, columns):
    planes = NZ // devices
    ut_count, xt_count = samples // TILE, columns // TILE
    theta = -0.5 * math.pi + math.pi * (np.arange(bins) + 0.5) / bins
    u = np.arange(samples)
    rows = []
    for device in range(devices):
        z0 = device * planes
        lists = [[] for _ in range(xt_count)]
        for b in range(bins):
            s, c = math.sin(theta[b]), math.cos(theta[b])
            centre = 0.5 * NZ + u * s
            near = (centre > z0 - 1.01) & (centre < z0 + planes + 0.01)
            for ut in range(ut_count):
                hit = u[ut * TILE : (ut + 1) * TILE][near[ut * TILE : (ut + 1) * TILE]]
                if hit.size == 0:
                    continue
                first = max(0, int((hit.min() * c - 1.01) // TILE))
                last = min(xt_count - 1, int((hit.max() * c + 1.01) // TILE))
                for xt in range(first, last + 1):
                    lists[xt].append(b * 4 + ut)
        idle = (bins - 1 if 2 * z0 < NZ else 0) * 4 + ut_count - 1
        tiles, codes = [], []
        for xt, entries in enumerate(lists):
            entries = entries + [idle] * (-len(entries) % GROUP)
            tiles += [xt] * (len(entries) // GROUP)
            codes += entries
        rows.append((tiles, codes))
    groups = max(len(tiles) for tiles, _ in rows)
    table = np.zeros((devices, 1 + groups * (1 + GROUP)), np.int32)
    for device, (tiles, codes) in enumerate(rows):
        table[device, 0] = len(tiles)
        table[device, 1 : 1 + len(tiles)] = tiles
        table[device, 1 + groups : 1 + groups + len(codes)] = codes
    return table, groups


def lanes_of(shape, axis):
    return lax.broadcasted_iota(jnp.int32, shape, axis).astype(f32)


def block_of(table, trig, groups, j, k):
    code = table[1 + groups + j * GROUP + k]
    b = lax.shift_right_logical(code, 2)
    ut = lax.bitwise_and(code, 3)
    return b, ut, trig[0, b], trig[1, b], (ut * TILE).astype(f32)


def bump(t):
    falloff = jnp.maximum(1.0 - t * t, 0.0)
    return falloff * falloff, -4.0 * t * falloff


def z_weights(z0, rows, u, s, c, samples):
    centre = 0.5 * NZ + u * s
    kz, kzd = bump((z0 + lanes_of((rows, TILE), 0)) - centre)
    return centre, kz, kzd * (-u * c * (1.0 / samples))


def extract_kernel(groups, planes, samples, table, trig, where, vhi, vlo, out):
    depth = vhi.shape[1] // 4
    ut_count = samples // TILE
    z0 = where[0].astype(f32)
    out[...] = jnp.zeros_like(out)

    def step(j, carry):
        xt = table[1 + j]
        hi_rows, lo_rows = vhi[xt], vlo[xt]
        xx = lanes_of((TILE, TILE), 0) + (xt * TILE).astype(f32)
        for k in range(GROUP):
            b, ut, s, c, base = block_of(table, trig, groups, j, k)
            u = lanes_of((1, TILE), 1) + base
            centre, kz, kzd = z_weights(z0, depth, u, s, c, samples)
            lower = jnp.floor(centre)
            own = jnp.where((lower >= z0) & (lower < z0 + planes), 1.0, 0.0)
            kz, kzd = kz * own, kzd * own
            kx, kxd = bump(xx - u * c)
            weights = jnp.concatenate([kx, kxd * (u * s * (1.0 / samples))], 1)
            whi = weights.astype(bf16)
            wlo = (weights - whi.astype(f32)).astype(bf16)
            sampled = (
                jnp.dot(hi_rows, whi, preferred_element_type=f32)
                + jnp.dot(lo_rows, whi, preferred_element_type=f32)
                + jnp.dot(hi_rows, wlo, preferred_element_type=f32)
            )
            leading, second = [], []
            for r in range(4):
                direct = sampled[r * depth : (r + 1) * depth, :TILE]
                tilted = sampled[r * depth : (r + 1) * depth, TILE:]
                leading.append(jnp.sum(direct * kz, axis=0, keepdims=True))
                second.append(jnp.sum(direct * kzd + tilted * kz, axis=0, keepdims=True))
            at = b * ut_count + ut
            out[at] = out[at] + jnp.concatenate(leading + second, 0)
        return carry

    lax.fori_loop(0, table[0], step, 0)


def particle_kernel(width, packed, ctf_hi, ctf_lo, slope, pairs, weighted, parts, bins_row, plain):
    count = packed.shape[0]
    bins = slope.shape[0]
    ids = packed[:, width:]
    classes = ids[:, 0:1].astype(f32)
    onehot_class = jnp.where(lanes_of((count, NCTF), 1) == classes, 1.0, 0.0)
    onehot_bin = jnp.where(lanes_of((count, bins), 1) == ids[:, 1:2].astype(f32), 1.0, 0.0)
    half = onehot_class.astype(bf16)
    contrast = jnp.dot(half, ctf_hi[...], preferred_element_type=f32) + jnp.dot(
        half, ctf_lo[...], preferred_element_type=f32
    )
    contrast = jnp.concatenate([contrast, contrast], 1)
    w = contrast * packed[:, :width].astype(f32)
    whi = w.astype(bf16)
    wlo = (w - whi.astype(f32)).astype(bf16)
    weighted[...] = whi
    slopes = slope[...]
    along = lax.dot_general(whi, slopes, NT, preferred_element_type=f32) + lax.dot_general(
        wlo, slopes, NT, preferred_element_type=f32
    )
    tables = jnp.dot(
        onehot_class, pairs[...], precision=lax.Precision.HIGHEST, preferred_element_type=f32
    )
    square = tables[:, :bins] * onehot_bin
    pull = (along - tables[:, bins:]) * onehot_bin
    ones = jnp.ones((8, bins), f32)
    rows = [
        lax.dot_general(
            ones, m, NT, precision=lax.Precision.HIGHEST, preferred_element_type=f32
        )[0:1]
        for m in (square, pull)
    ]
    parts[...] = jnp.concatenate(rows, 0)
    pick = jnp.where(lanes_of((8, TILE), 1) == 1.0, 1.0, 0.0).astype(bf16)
    bins_row[...] = lax.dot_general(pick, ids, NT, preferred_element_type=f32)[0:1]
    sums = lax.dot_general(onehot_bin.astype(bf16), whi, TN, preferred_element_type=f32)

    @pl.when(pl.program_id(0) == 0)
    def _():
        plain[...] = sums

    @pl.when(pl.program_id(0) > 0)
    def _():
        plain[...] = plain[...] + sums


def spread_kernel(
    groups, planes, samples, table, trig, where, parts, bins_row, weighted, plain, pose, out, sums, total
):
    bins, width = plain.shape
    tiles = width // TILE
    ut_count = samples // TILE
    depth = total.shape[1] // 4
    count = parts.shape[1]
    chunk = min(CHUNK, count)
    z0 = where[0].astype(f32)

    square, pull = parts[0:1, :], parts[1:2, :]
    curvature = square + EPS
    shift = jnp.zeros_like(square)
    for _ in range(ITERS):
        shift = shift + 0.5 * (pull - shift * square) / curvature
    pose[...] = shift * jnp.sqrt(curvature)

    slope_sum = jnp.zeros((bins, width), f32)
    for i in range(count // chunk):
        span = slice(i * chunk, (i + 1) * chunk)
        belongs = lanes_of((bins, chunk), 0) == bins_row[:, span]
        scaled = jnp.where(belongs, shift[:, span], 0.0)
        hi = scaled.astype(bf16)
        lo = (scaled - hi.astype(f32)).astype(bf16)
        rows = weighted[span, :]
        slope_sum = (
            slope_sum
            + jnp.dot(hi, rows, preferred_element_type=f32)
            + jnp.dot(lo, rows, preferred_element_type=f32)
        )
    for q in range(tiles):
        sums[q] = plain[:, q * TILE : (q + 1) * TILE]
        sums[tiles + q] = slope_sum[:, q * TILE : (q + 1) * TILE]
    total[...] = jnp.zeros_like(total)

    def step(j, carry):
        xt = table[1 + j]
        xx = lanes_of((TILE, TILE), 1) + (xt * TILE).astype(f32)
        left, right = [], []
        for k in range(GROUP):
            b, ut, s, c, base = block_of(table, trig, groups, j, k)
            u = lanes_of((1, TILE), 1) + base
            _, kz, kzd = z_weights(z0, depth, u, s, c, samples)
            first, second = [], []
            for r in range(4):
                direct = sums[r * ut_count + ut, pl.ds(b, 1), :]
                tilted = sums[tiles + r * ut_count + ut, pl.ds(b, 1), :]
                first.append(kz * direct + kzd * tilted)
                second.append(kz * tilted)
            left += [jnp.concatenate(first, 0).astype(bf16), jnp.concatenate(second, 0).astype(bf16)]
            uu = lanes_of((TILE, TILE), 0) + base
            kx, kxd = bump(xx - uu * c)
            right += [kx.astype(bf16), (kxd * (uu * (s * (1.0 / samples)))).astype(bf16)]
        total[xt] = total[xt] + jnp.dot(
            jnp.concatenate(left, 1), jnp.concatenate(right, 0), preferred_element_type=f32
        )
        return carry

    lax.fori_loop(0, table[0], step, 0)
    for xt in range(total.shape[0]):
        for r in range(4):
            out[:, r, xt * TILE : (xt + 1) * TILE] = total[xt, r * depth : r * depth + planes, :]


def local(volume, observed, ctf_table, ctf_class, bin_ids):
    slab, rows, columns = volume.shape
    mine, _, samples = observed.shape
    n_gz, n_dom = lax.axis_size("gz"), lax.axis_size("dom")
    devices = n_gz * n_dom
    bins = NB_DEV * n_dom
    planes = NZ // devices
    count = mine * devices
    width = rows * samples
    xt_count, ut_count = columns // TILE, samples // TILE
    gz, dom = lax.axis_index("gz"), lax.axis_index("dom")
    device = gz * n_dom + dom

    ids = jnp.stack([ctf_class, bin_ids], 1).astype(bf16)
    ids = jnp.pad(ids, ((0, 0), (0, TILE - 2)))
    packed = jnp.concatenate([observed.reshape(mine, width), ids], 1)
    packed = lax.all_gather(packed, ("gz", "dom"), axis=0, tiled=True)

    table, groups = make_plan(devices, bins, samples, columns)
    table = lax.dynamic_index_in_dim(jnp.asarray(table), device, 0, keepdims=False)
    where = (device * planes)[None].astype(jnp.int32)
    theta = -0.5 * math.pi + math.pi * (jnp.arange(bins, dtype=f32) + 0.5) / bins
    trig = jnp.stack([jnp.sin(theta), jnp.cos(theta)])

    above = lax.ppermute(volume[:1], "gz", [(i, i - 1) for i in range(1, n_gz)])
    own = lax.dynamic_slice_in_dim(volume, dom * planes, planes, 0)
    inner = lax.dynamic_slice_in_dim(volume, jnp.minimum((dom + 1) * planes, slab - 1), 1, 0)
    halo = jnp.where(dom == n_dom - 1, above, inner)
    depth_in = round_up(planes + 1, 8)
    field = jnp.concatenate([own, halo, jnp.zeros((depth_in - planes - 1, rows, columns), f32)], 0)
    field = field.reshape(depth_in, rows, xt_count, TILE).transpose(2, 1, 0, 3)
    field = field.reshape(xt_count, rows * depth_in, TILE)
    field_hi = lax.reduce_precision(field, 8, 7)
    field_lo = (field - field_hi).astype(bf16)
    field_hi = field_hi.astype(bf16)

    smem = pl.BlockSpec(memory_space=pltpu.SMEM)
    vmem = pl.BlockSpec(memory_space=pltpu.VMEM)
    params = pltpu.CompilerParams(vmem_limit_bytes=VMEM)
    slices = pl.pallas_call(
        functools.partial(extract_kernel, groups, planes, samples),
        out_shape=jax.ShapeDtypeStruct((bins * ut_count, 2 * rows, TILE), f32),
        in_specs=[smem, smem, smem, vmem, vmem],
        out_specs=vmem,
        compiler_params=params,
        name="extract",
    )(table, trig, where, field_hi, field_lo)

    slices = lax.reduce_precision(slices, 8, 7)
    slices = slices.reshape(bins, ut_count, 2 * rows, TILE).transpose(0, 2, 1, 3)
    slices = slices.reshape(bins, 2, 2, rows // 2, samples)
    direct, slope = slices[:, 0], slices[:, 1]
    squares = jnp.stack([jnp.sum(slope * slope, 1), jnp.sum(direct * slope, 1)])
    pairs = lax.dot_general(
        (ctf_table * ctf_table).reshape(NCTF, -1),
        squares.reshape(2 * bins, -1),
        NT,
        precision=lax.Precision.HIGHEST,
        preferred_element_type=f32,
    )
    slope = slope.reshape(bins, width).astype(bf16)
    flat_ctf = ctf_table.reshape(NCTF, -1)
    ctf_hi = lax.reduce_precision(flat_ctf, 8, 7)
    ctf_lo = (flat_ctf - ctf_hi).astype(bf16)
    ctf_hi = ctf_hi.astype(bf16)

    chunk = min(CHUNK, count)
    whole = lambda shape: pl.BlockSpec(shape, lambda i: (0,) * len(shape))
    weighted, parts, bins_row, plain = pl.pallas_call(
        functools.partial(particle_kernel, width),
        grid=(count // chunk,),
        out_shape=[
            jax.ShapeDtypeStruct((count, width), bf16),
            jax.ShapeDtypeStruct((2, count), f32),
            jax.ShapeDtypeStruct((1, count), f32),
            jax.ShapeDtypeStruct((bins, width), f32),
        ],
        in_specs=[
            pl.BlockSpec((chunk, width + TILE), lambda i: (i, 0)),
            whole(ctf_hi.shape),
            whole(ctf_lo.shape),
            whole(slope.shape),
            whole(pairs.shape),
        ],
        out_specs=[
            pl.BlockSpec((chunk, width), lambda i: (i, 0)),
            pl.BlockSpec((2, chunk), lambda i: (0, i)),
            pl.BlockSpec((1, chunk), lambda i: (0, i)),
            whole((bins, width)),
        ],
        compiler_params=params,
        name="particles",
    )(packed, ctf_hi, ctf_lo, slope, pairs)

    parts = lax.psum(parts, ("gz", "dom"))

    depth = round_up(planes, 8)
    pose, spread = pl.pallas_call(
        functools.partial(spread_kernel, groups, planes, samples),
        out_shape=[
            jax.ShapeDtypeStruct((1, count), f32),
            jax.ShapeDtypeStruct((planes, rows, columns), f32),
        ],
        in_specs=[smem, smem, smem, vmem, vmem, vmem, vmem],
        out_specs=[vmem, vmem],
        scratch_shapes=[
            pltpu.VMEM((2 * width // TILE, bins, TILE), f32),
            pltpu.VMEM((xt_count, rows * depth, TILE), f32),
        ],
        compiler_params=params,
        name="spread",
    )(table, trig, where, parts, bins_row, weighted, plain)
    pose = lax.dynamic_slice_in_dim(pose.reshape(count), device * mine, mine, 0)
    return pose, spread


def solution(mesh):
    return jax.shard_map(
        local,
        mesh=mesh,
        in_specs=(
            P("gz", None, None),
            P(("gz", "dom"), None, None),
            P(),
            P(("gz", "dom")),
            P(("gz", "dom")),
        ),
        out_specs=(P(("gz", "dom")), P(("gz", "dom"), None, None)),
        check_vma=False,
    )
```

```python
import functools
import math

import jax
import jax.numpy as jnp
import numpy as np
from jax import lax
from jax.experimental import pallas as pl
from jax.experimental.pallas import tpu as pltpu
from jax.sharding import PartitionSpec as P

NZ = 768
NB_DEV = 8
NCTF = 32
ITERS = 3
EPS = 1e-05
TILE = 128
GROUP = 4
CHUNK = 512
VMEM = 56 * 2**20
f32 = jnp.float32
bf16 = jnp.bfloat16
NT = (((1,), (1,)), ((), ()))
TN = (((0,), (0,)), ((), ()))


def round_up(n, m):
    return -(-n // m) * m


def make_plan(devices, bins, samples, columns):
    planes = NZ // devices
    ut_count, xt_count = samples // TILE, columns // TILE
    theta = -0.5 * math.pi + math.pi * (np.arange(bins) + 0.5) / bins
    u = np.arange(samples)
    rows = []
    for device in range(devices):
        z0 = device * planes
        lists = [[] for _ in range(xt_count)]
        for b in range(bins):
            s, c = math.sin(theta[b]), math.cos(theta[b])
            centre = 0.5 * NZ + u * s
            near = (centre > z0 - 1.01) & (centre < z0 + planes + 0.01)
            for ut in range(ut_count):
                hit = u[ut * TILE : (ut + 1) * TILE][near[ut * TILE : (ut + 1) * TILE]]
                if hit.size == 0:
                    continue
                first = max(0, int((hit.min() * c - 1.01) // TILE))
                last = min(xt_count - 1, int((hit.max() * c + 1.01) // TILE))
                for xt in range(first, last + 1):
                    lists[xt].append(b * 4 + ut)
        idle = (bins - 1 if 2 * z0 < NZ else 0) * 4 + ut_count - 1
        tiles, codes = [], []
        for xt, entries in enumerate(lists):
            entries = entries + [idle] * (-len(entries) % GROUP)
            tiles += [xt] * (len(entries) // GROUP)
            codes += entries
        rows.append((tiles, codes))
    groups = max(len(tiles) for tiles, _ in rows)
    table = np.zeros((devices, 1 + groups * (1 + GROUP)), np.int32)
    for device, (tiles, codes) in enumerate(rows):
        table[device, 0] = len(tiles)
        table[device, 1 : 1 + len(tiles)] = tiles
        table[device, 1 + groups : 1 + groups + len(codes)] = codes
    return table, groups


def lanes_of(shape, axis):
    return lax.broadcasted_iota(jnp.int32, shape, axis).astype(f32)


def block_of(table, trig, groups, j, k):
    code = table[1 + groups + j * GROUP + k]
    b = lax.shift_right_logical(code, 2)
    ut = lax.bitwise_and(code, 3)
    return b, ut, trig[0, b], trig[1, b], (ut * TILE).astype(f32)


def bump(t):
    falloff = jnp.maximum(1.0 - t * t, 0.0)
    return falloff * falloff, -4.0 * t * falloff


def z_weights(z0, rows, u, s, c, samples):
    centre = 0.5 * NZ + u * s
    kz, kzd = bump((z0 + lanes_of((rows, TILE), 0)) - centre)
    return centre, kz, kzd * (-u * c * (1.0 / samples))


def extract_kernel(groups, planes, samples, table, trig, where, vhi, vlo, out):
    depth = vhi.shape[1] // 4
    ut_count = samples // TILE
    z0 = where[0].astype(f32)
    out[...] = jnp.zeros_like(out)

    def step(j, carry):
        xt = table[1 + j]
        hi_rows, lo_rows = vhi[xt], vlo[xt]
        xx = lanes_of((TILE, TILE), 0) + (xt * TILE).astype(f32)
        for k in range(GROUP):
            b, ut, s, c, base = block_of(table, trig, groups, j, k)
            u = lanes_of((1, TILE), 1) + base
            centre, kz, kzd = z_weights(z0, depth, u, s, c, samples)
            lower = jnp.floor(centre)
            own = jnp.where((lower >= z0) & (lower < z0 + planes), 1.0, 0.0)
            kz, kzd = kz * own, kzd * own
            kx, kxd = bump(xx - u * c)
            weights = jnp.concatenate([kx, kxd * (u * s * (1.0 / samples))], 1)
            whi = weights.astype(bf16)
            wlo = (weights - whi.astype(f32)).astype(bf16)
            sampled = (
                jnp.dot(hi_rows, whi, preferred_element_type=f32)
                + jnp.dot(lo_rows, whi, preferred_element_type=f32)
                + jnp.dot(hi_rows, wlo, preferred_element_type=f32)
            )
            leading, second = [], []
            for r in range(4):
                direct = sampled[r * depth : (r + 1) * depth, :TILE]
                tilted = sampled[r * depth : (r + 1) * depth, TILE:]
                leading.append(jnp.sum(direct * kz, axis=0, keepdims=True))
                second.append(jnp.sum(direct * kzd + tilted * kz, axis=0, keepdims=True))
            at = b * ut_count + ut
            out[at] = out[at] + jnp.concatenate(leading + second, 0)
        return carry

    lax.fori_loop(0, table[0], step, 0)


def particle_kernel(width, mine, n_gz, n_dom, place, *refs):
    blocks = refs[: 2 * n_gz]
    ctf_hi, ctf_lo, slope, pairs, weighted, parts, bins_row, plain, packed, sems = refs[2 * n_gz :]
    n_z = n_dom // 2
    gz, z, core = place[0], place[1], place[2]
    copies = []
    for c in range(2):
        for j in range(n_gz):
            for k in range(n_z):
                owner = ((gz ^ j) * n_z + (z ^ k)) * 2 + (core ^ c)
                start = pl.multiple_of(owner * mine, mine)
                copies.append(
                    pltpu.make_async_copy(
                        blocks[c * n_gz + j].at[pl.ds(k * mine, mine), :],
                        packed.at[pl.ds(start, mine), :],
                        sems.at[len(copies)],
                    )
                )
    for copy in copies:
        copy.start()
    for copy in copies:
        copy.wait()

    total = packed.shape[0]
    count = min(CHUNK, total)
    bins = slope.shape[0]
    plain[...] = jnp.zeros_like(plain)

    def step(i, carry):
        span = pl.ds(pl.multiple_of(i * count, count), count)
        ids = packed[span, width:]
        classes = ids[:, 0:1].astype(f32)
        onehot_class = jnp.where(lanes_of((count, NCTF), 1) == classes, 1.0, 0.0)
        onehot_bin = jnp.where(lanes_of((count, bins), 1) == ids[:, 1:2].astype(f32), 1.0, 0.0)
        half = onehot_class.astype(bf16)
        contrast = jnp.dot(half, ctf_hi[...], preferred_element_type=f32) + jnp.dot(
            half, ctf_lo[...], preferred_element_type=f32
        )
        contrast = jnp.concatenate([contrast, contrast], 1)
        w = contrast * packed[span, :width].astype(f32)
        whi = w.astype(bf16)
        wlo = (w - whi.astype(f32)).astype(bf16)
        weighted[span, :] = whi
        slopes = slope[...]
        along = lax.dot_general(whi, slopes, NT, preferred_element_type=f32) + lax.dot_general(
            wlo, slopes, NT, preferred_element_type=f32
        )
        tables = jnp.dot(
            onehot_class, pairs[...], precision=lax.Precision.HIGHEST, preferred_element_type=f32
        )
        square = tables[:, :bins] * onehot_bin
        pull = (along - tables[:, bins:]) * onehot_bin
        ones = jnp.ones((8, bins), f32)
        for n, m in enumerate((square, pull)):
            row = lax.dot_general(
                ones, m, NT, precision=lax.Precision.HIGHEST, preferred_element_type=f32
            )[0:1]
            for q in range(count // TILE):
                at = n * (total // TILE) + i * (count // TILE) + q
                parts[pl.ds(at, 1), :] = row[:, q * TILE : (q + 1) * TILE]
        pick = jnp.where(lanes_of((8, TILE), 1) == 1.0, 1.0, 0.0).astype(bf16)
        bins_row[:, span] = lax.dot_general(pick, ids, NT, preferred_element_type=f32)[0:1]
        plain[...] = plain[...] + lax.dot_general(
            onehot_bin.astype(bf16), whi, TN, preferred_element_type=f32
        )
        return carry

    lax.fori_loop(0, total // count, step, 0)


def spread_kernel(
    groups, planes, samples, table, trig, where, parts, bins_row, weighted, plain, pose, out, sums, total
):
    bins, width = plain.shape
    tiles = width // TILE
    ut_count = samples // TILE
    depth = total.shape[1] // 4
    count = bins_row.shape[1]
    chunk = min(CHUNK, count)
    z0 = where[0].astype(f32)

    rows = 2 * count // TILE
    scalars = jnp.sum(parts[...].reshape(parts.shape[0] // rows, rows, TILE), axis=0)
    square = jnp.concatenate([scalars[q : q + 1] for q in range(rows // 2)], 1)
    pull = jnp.concatenate([scalars[q : q + 1] for q in range(rows // 2, rows)], 1)
    curvature = square + EPS
    shift = jnp.zeros_like(square)
    for _ in range(ITERS):
        shift = shift + 0.5 * (pull - shift * square) / curvature
    pose[...] = shift * jnp.sqrt(curvature)

    slope_sum = jnp.zeros((bins, width), f32)
    for i in range(count // chunk):
        span = slice(i * chunk, (i + 1) * chunk)
        belongs = lanes_of((bins, chunk), 0) == bins_row[:, span]
        scaled = jnp.where(belongs, shift[:, span], 0.0)
        hi = scaled.astype(bf16)
        lo = (scaled - hi.astype(f32)).astype(bf16)
        rows = weighted[span, :]
        slope_sum = (
            slope_sum
            + jnp.dot(hi, rows, preferred_element_type=f32)
            + jnp.dot(lo, rows, preferred_element_type=f32)
        )
    for q in range(tiles):
        sums[q] = plain[:, q * TILE : (q + 1) * TILE]
        sums[tiles + q] = slope_sum[:, q * TILE : (q + 1) * TILE]
    total[...] = jnp.zeros_like(total)

    def step(j, carry):
        xt = table[1 + j]
        xx = lanes_of((TILE, TILE), 1) + (xt * TILE).astype(f32)
        left, right = [], []
        for k in range(GROUP):
            b, ut, s, c, base = block_of(table, trig, groups, j, k)
            u = lanes_of((1, TILE), 1) + base
            _, kz, kzd = z_weights(z0, depth, u, s, c, samples)
            first, second = [], []
            for r in range(4):
                direct = sums[r * ut_count + ut, pl.ds(b, 1), :]
                tilted = sums[tiles + r * ut_count + ut, pl.ds(b, 1), :]
                first.append(kz * direct + kzd * tilted)
                second.append(kz * tilted)
            left += [jnp.concatenate(first, 0), jnp.concatenate(second, 0)]
            uu = lanes_of((TILE, TILE), 0) + base
            kx, kxd = bump(xx - uu * c)
            right += [kx.astype(bf16), (kxd * (uu * (s * (1.0 / samples)))).astype(bf16)]
        left = jnp.concatenate(left, 1)
        hi = left.astype(bf16)
        lo = (left - hi.astype(f32)).astype(bf16)
        both = jnp.dot(
            jnp.concatenate([hi, lo], 0), jnp.concatenate(right, 0), preferred_element_type=f32
        )
        total[xt] = total[xt] + both[: 4 * depth] + both[4 * depth :]
        return carry

    lax.fori_loop(0, table[0], step, 0)
    for xt in range(total.shape[0]):
        for r in range(4):
            out[:, r, xt * TILE : (xt + 1) * TILE] = total[xt, r * depth : r * depth + planes, :]


def swap(x, axis, size, distance):
    return lax.ppermute(x, axis, [(i, i ^ distance) for i in range(size)])


def local(volume, observed, ctf_table, ctf_class, bin_ids):
    slab, rows, columns = volume.shape
    mine, _, samples = observed.shape
    n_gz, n_dom = lax.axis_size("gz"), lax.axis_size("dom")
    devices = n_gz * n_dom
    bins = NB_DEV * n_dom
    planes = NZ // devices
    count = mine * devices
    width = rows * samples
    xt_count, ut_count = columns // TILE, samples // TILE
    gz, dom = lax.axis_index("gz"), lax.axis_index("dom")
    device = gz * n_dom + dom

    ids = jnp.stack([ctf_class, bin_ids], 1).astype(bf16)
    ids = jnp.pad(ids, ((0, 0), (0, TILE - 2)))
    packed = jnp.concatenate([observed.reshape(mine, width), ids], 1)
    n_z = n_dom // 2
    column = jnp.concatenate(
        [packed] + [swap(packed, "dom", n_dom, 2 * k) for k in range(1, n_z)], 0
    )
    planes_of = [column] + [swap(column, "gz", n_gz, j) for j in range(1, n_gz)]
    gathered = planes_of + [swap(part, "dom", n_dom, 1) for part in planes_of]
    place = jnp.stack([gz, dom // 2, dom % 2]).astype(jnp.int32)

    table, groups = make_plan(devices, bins, samples, columns)
    table = lax.dynamic_index_in_dim(jnp.asarray(table), device, 0, keepdims=False)
    where = (device * planes)[None].astype(jnp.int32)
    theta = -0.5 * math.pi + math.pi * (jnp.arange(bins, dtype=f32) + 0.5) / bins
    trig = jnp.stack([jnp.sin(theta), jnp.cos(theta)])

    above = lax.ppermute(volume[:1], "gz", [(i, i - 1) for i in range(1, n_gz)])
    own = lax.dynamic_slice_in_dim(volume, dom * planes, planes, 0)
    inner = lax.dynamic_slice_in_dim(volume, jnp.minimum((dom + 1) * planes, slab - 1), 1, 0)
    halo = jnp.where(dom == n_dom - 1, above, inner)
    depth_in = round_up(planes + 1, 8)
    field = jnp.concatenate([own, halo, jnp.zeros((depth_in - planes - 1, rows, columns), f32)], 0)
    field = field.reshape(depth_in, rows, xt_count, TILE).transpose(2, 1, 0, 3)
    field = field.reshape(xt_count, rows * depth_in, TILE)
    field_hi = lax.reduce_precision(field, 8, 7)
    field_lo = (field - field_hi).astype(bf16)
    field_hi = field_hi.astype(bf16)

    smem = pl.BlockSpec(memory_space=pltpu.SMEM)
    vmem = pl.BlockSpec(memory_space=pltpu.VMEM)
    params = pltpu.CompilerParams(vmem_limit_bytes=VMEM)
    slices = pl.pallas_call(
        functools.partial(extract_kernel, groups, planes, samples),
        out_shape=jax.ShapeDtypeStruct((bins * ut_count, 2 * rows, TILE), f32),
        in_specs=[smem, smem, smem, vmem, vmem],
        out_specs=vmem,
        compiler_params=params,
        name="extract",
    )(table, trig, where, field_hi, field_lo)

    slices = lax.reduce_precision(slices, 8, 7)
    slices = slices.reshape(bins, ut_count, 2 * rows, TILE).transpose(0, 2, 1, 3)
    slices = slices.reshape(bins, 2, 2, rows // 2, samples)
    direct, slope = slices[:, 0], slices[:, 1]
    squares = jnp.stack([jnp.sum(slope * slope, 1), jnp.sum(direct * slope, 1)])
    pairs = lax.dot_general(
        (ctf_table * ctf_table).reshape(NCTF, -1),
        squares.reshape(2 * bins, -1),
        NT,
        precision=lax.Precision.HIGHEST,
        preferred_element_type=f32,
    )
    slope = slope.reshape(bins, width).astype(bf16)
    flat_ctf = ctf_table.reshape(NCTF, -1)
    ctf_hi = lax.reduce_precision(flat_ctf, 8, 7)
    ctf_lo = (flat_ctf - ctf_hi).astype(bf16)
    ctf_hi = ctf_hi.astype(bf16)

    hbm = pl.BlockSpec(memory_space=pl.ANY)
    weighted, parts, bins_row, plain = pl.pallas_call(
        functools.partial(particle_kernel, width, mine, n_gz, n_dom),
        out_shape=[
            jax.ShapeDtypeStruct((count, width), bf16),
            jax.ShapeDtypeStruct((2 * count // TILE, TILE), f32),
            jax.ShapeDtypeStruct((1, count), f32),
            jax.ShapeDtypeStruct((bins, width), f32),
        ],
        in_specs=[smem] + [hbm] * len(gathered) + [vmem] * 4,
        out_specs=[vmem] * 4,
        scratch_shapes=[
            pltpu.VMEM((count, width + TILE), bf16),
            pltpu.SemaphoreType.DMA((devices,)),
        ],
        compiler_params=params,
        name="particles",
    )(place, *gathered, ctf_hi, ctf_lo, slope, pairs)

    parts = lax.all_gather(parts, ("gz", "dom"), axis=0, tiled=True)

    depth = round_up(planes, 8)
    pose, spread = pl.pallas_call(
        functools.partial(spread_kernel, groups, planes, samples),
        out_shape=[
            jax.ShapeDtypeStruct((1, count), f32),
            jax.ShapeDtypeStruct((planes, rows, columns), f32),
        ],
        in_specs=[smem, smem, smem, vmem, vmem, vmem, vmem],
        out_specs=[vmem, vmem],
        scratch_shapes=[
            pltpu.VMEM((2 * width // TILE, bins, TILE), f32),
            pltpu.VMEM((xt_count, rows * depth, TILE), f32),
        ],
        compiler_params=params,
        name="spread",
    )(table, trig, where, parts, bins_row, weighted, plain)
    pose = lax.dynamic_slice_in_dim(pose.reshape(count), device * mine, mine, 0)
    return pose, spread


def solution(mesh):
    return jax.shard_map(
        local,
        mesh=mesh,
        in_specs=(
            P("gz", None, None),
            P(("gz", "dom"), None, None),
            P(),
            P(("gz", "dom")),
            P(("gz", "dom")),
        ),
        out_specs=(P(("gz", "dom")), P(("gz", "dom"), None, None)),
        check_vma=False,
    )
```

```python
import functools
import math

import jax
import jax.numpy as jnp
import numpy as np
from jax import lax
from jax.experimental import pallas as pl
from jax.experimental.pallas import tpu as pltpu
from jax.sharding import PartitionSpec as P

NZ = 768
NB_DEV = 8
NCTF = 32
ITERS = 3
EPS = 1e-05
TILE = 128
GROUP = 4
CHUNK = 512
VMEM = 56 * 2**20
f32 = jnp.float32
bf16 = jnp.bfloat16
NT = (((1,), (1,)), ((), ()))


def round_up(n, m):
    return -(-n // m) * m


def make_plan(devices, bins, samples, columns):
    planes = NZ // devices
    ut_count, xt_count = samples // TILE, columns // TILE
    theta = -0.5 * math.pi + math.pi * (np.arange(bins) + 0.5) / bins
    u = np.arange(samples)
    rows = []
    for device in range(devices):
        z0 = device * planes
        lists = [[] for _ in range(xt_count)]
        for b in range(bins):
            s, c = math.sin(theta[b]), math.cos(theta[b])
            centre = 0.5 * NZ + u * s
            near = (centre > z0 - 1.01) & (centre < z0 + planes + 0.01)
            for ut in range(ut_count):
                hit = u[ut * TILE : (ut + 1) * TILE][near[ut * TILE : (ut + 1) * TILE]]
                if hit.size == 0:
                    continue
                first = max(0, int((hit.min() * c - 1.01) // TILE))
                last = min(xt_count - 1, int((hit.max() * c + 1.01) // TILE))
                for xt in range(first, last + 1):
                    lists[xt].append(b * 4 + ut)
        idle = (bins - 1 if 2 * z0 < NZ else 0) * 4 + ut_count - 1
        tiles, codes = [], []
        for xt, entries in enumerate(lists):
            entries = entries + [idle] * (-len(entries) % GROUP)
            tiles += [xt] * (len(entries) // GROUP)
            codes += entries
        rows.append((tiles, codes))
    groups = max(len(tiles) for tiles, _ in rows)
    table = np.zeros((devices, 1 + groups * (1 + GROUP)), np.int32)
    for device, (tiles, codes) in enumerate(rows):
        table[device, 0] = len(tiles)
        table[device, 1 : 1 + len(tiles)] = tiles
        table[device, 1 + groups : 1 + groups + len(codes)] = codes
    return table, groups


def lanes_of(shape, axis):
    return lax.broadcasted_iota(jnp.int32, shape, axis).astype(f32)


def block_of(table, trig, groups, j, k):
    code = table[1 + groups + j * GROUP + k]
    b = lax.shift_right_logical(code, 2)
    ut = lax.bitwise_and(code, 3)
    return b, ut, trig[0, b], trig[1, b], (ut * TILE).astype(f32)


def bump(t):
    falloff = jnp.maximum(1.0 - t * t, 0.0)
    return falloff * falloff, -4.0 * t * falloff


def z_weights(z0, rows, u, s, c, samples):
    centre = 0.5 * NZ + u * s
    kz, kzd = bump((z0 + lanes_of((rows, TILE), 0)) - centre)
    return centre, kz, kzd * (-u * c * (1.0 / samples))


def extract_kernel(groups, planes, samples, table, trig, where, vhi, vlo, after, out):
    depth = vhi.shape[1] // 4
    ut_count = samples // TILE
    z0 = where[0].astype(f32)
    out[...] = jnp.zeros_like(out)

    def step(j, carry):
        xt = table[1 + j]
        hi_rows, lo_rows = vhi[xt], vlo[xt]
        xx = lanes_of((TILE, TILE), 0) + (xt * TILE).astype(f32)
        for k in range(GROUP):
            b, ut, s, c, base = block_of(table, trig, groups, j, k)
            u = lanes_of((1, TILE), 1) + base
            centre, kz, kzd = z_weights(z0, depth, u, s, c, samples)
            lower = jnp.floor(centre)
            own = jnp.where((lower >= z0) & (lower < z0 + planes), 1.0, 0.0)
            kz, kzd = kz * own, kzd * own
            kx, kxd = bump(xx - u * c)
            weights = jnp.concatenate([kx, kxd * (u * s * (1.0 / samples))], 1)
            whi = weights.astype(bf16)
            wlo = (weights - whi.astype(f32)).astype(bf16)
            sampled = (
                jnp.dot(hi_rows, whi, preferred_element_type=f32)
                + jnp.dot(lo_rows, whi, preferred_element_type=f32)
                + jnp.dot(hi_rows, wlo, preferred_element_type=f32)
            )
            leading, second = [], []
            for r in range(4):
                direct = sampled[r * depth : (r + 1) * depth, :TILE]
                tilted = sampled[r * depth : (r + 1) * depth, TILE:]
                leading.append(jnp.sum(direct * kz, axis=0, keepdims=True))
                second.append(jnp.sum(direct * kzd + tilted * kz, axis=0, keepdims=True))
            at = b * ut_count + ut
            out[at] = out[at] + jnp.concatenate(leading + second, 0)
        return carry

    lax.fori_loop(0, table[0], step, 0)


def particle_kernel(width, mine, n_gz, n_dom, place, *refs):
    blocks = refs[: 2 * n_gz]
    ctf_hi, ctf_lo, slope, pairs, weighted, parts, bins_row, packed, sems = refs[2 * n_gz :]
    n_z = n_dom // 2
    gz, z, core = place[0], place[1], place[2]
    copies = []
    for c in range(2):
        for j in range(n_gz):
            for k in range(n_z):
                owner = ((gz ^ j) * n_z + (z ^ k)) * 2 + (core ^ c)
                start = pl.multiple_of(owner * mine, mine)
                copies.append(
                    pltpu.make_async_copy(
                        blocks[c * n_gz + j].at[pl.ds(k * mine, mine), :],
                        packed.at[pl.ds(start, mine), :],
                        sems.at[len(copies)],
                    )
                )
    for copy in copies:
        copy.start()
    for copy in copies:
        copy.wait()

    total = packed.shape[0]
    count = min(CHUNK, total)
    bins = slope.shape[0]

    def step(i, carry):
        span = pl.ds(pl.multiple_of(i * count, count), count)
        ids = packed[span, width:]
        classes = ids[:, 0:1].astype(f32)
        onehot_class = jnp.where(lanes_of((count, NCTF), 1) == classes, 1.0, 0.0)
        onehot_bin = jnp.where(lanes_of((count, bins), 1) == ids[:, 1:2].astype(f32), 1.0, 0.0)
        half = onehot_class.astype(bf16)
        contrast = jnp.dot(half, ctf_hi[...], preferred_element_type=f32) + jnp.dot(
            half, ctf_lo[...], preferred_element_type=f32
        )
        contrast = jnp.concatenate([contrast, contrast], 1)
        w = contrast * packed[span, :width].astype(f32)
        whi = w.astype(bf16)
        wlo = (w - whi.astype(f32)).astype(bf16)
        weighted[span, :] = whi
        slopes = slope[...]
        along = lax.dot_general(whi, slopes, NT, preferred_element_type=f32) + lax.dot_general(
            wlo, slopes, NT, preferred_element_type=f32
        )
        tables = jnp.dot(
            onehot_class, pairs[...], precision=lax.Precision.HIGHEST, preferred_element_type=f32
        )
        square = tables[:, :bins] * onehot_bin
        pull = (along - tables[:, bins:]) * onehot_bin
        ones = jnp.ones((8, bins), f32)
        for n, m in enumerate((square, pull)):
            row = lax.dot_general(
                ones, m, NT, precision=lax.Precision.HIGHEST, preferred_element_type=f32
            )[0:1]
            for q in range(count // TILE):
                at = n * (total // TILE) + i * (count // TILE) + q
                parts[pl.ds(at, 1), :] = row[:, q * TILE : (q + 1) * TILE]
        pick = jnp.where(lanes_of((8, TILE), 1) == 1.0, 1.0, 0.0).astype(bf16)
        bins_row[:, span] = lax.dot_general(pick, ids, NT, preferred_element_type=f32)[0:1]
        return carry

    lax.fori_loop(0, total // count, step, 0)


def plain_kernel(bins_row, weighted, plain):
    count = weighted.shape[0]
    chunk = min(CHUNK, count)
    sums = jnp.zeros(plain.shape, f32)
    for i in range(count // chunk):
        span = slice(i * chunk, (i + 1) * chunk)
        belongs = lanes_of((plain.shape[0], chunk), 0) == bins_row[:, span]
        onehot = jnp.where(belongs, 1.0, 0.0).astype(bf16)
        sums = sums + jnp.dot(onehot, weighted[span, :], preferred_element_type=f32)
    plain[...] = sums


def spread_kernel(
    groups, planes, samples, mine, n_gz, table, trig, where, bins_row, weighted, plain, *refs
):
    parts = refs[:n_gz]
    pose, out, sums, total, poses = refs[n_gz:]
    bins, width = plain.shape
    tiles = width // TILE
    ut_count = samples // TILE
    depth = total.shape[1] // 4
    count = bins_row.shape[1]
    chunk = min(CHUNK, count)
    z0 = where[0].astype(f32)

    rows = count // TILE
    scalars = sum([part[...] for part in parts[1:]], parts[0][...])
    square, pull = scalars[:rows], scalars[rows:]
    curvature = square + EPS
    shift = jnp.zeros_like(square)
    for _ in range(ITERS):
        shift = shift + 0.5 * (pull - shift * square) / curvature
    poses[...] = shift * jnp.sqrt(curvature)
    first = (where[0] // planes) * mine
    row = poses[pl.ds(first // TILE, 1), :]
    pose[...] = pltpu.roll(row, TILE - lax.rem(first, TILE), 1)[:, :mine]
    shift = jnp.concatenate([shift[q : q + 1] for q in range(rows)], 1)

    slope_sum = jnp.zeros((bins, width), f32)
    for i in range(count // chunk):
        span = slice(i * chunk, (i + 1) * chunk)
        belongs = lanes_of((bins, chunk), 0) == bins_row[:, span]
        scaled = jnp.where(belongs, shift[:, span], 0.0)
        hi = scaled.astype(bf16)
        lo = (scaled - hi.astype(f32)).astype(bf16)
        rows = weighted[span, :]
        slope_sum = (
            slope_sum
            + jnp.dot(hi, rows, preferred_element_type=f32)
            + jnp.dot(lo, rows, preferred_element_type=f32)
        )
    for q in range(tiles):
        sums[q] = plain[:, q * TILE : (q + 1) * TILE]
        sums[tiles + q] = slope_sum[:, q * TILE : (q + 1) * TILE]
    total[...] = jnp.zeros_like(total)

    def step(j, carry):
        xt = table[1 + j]
        xx = lanes_of((TILE, TILE), 1) + (xt * TILE).astype(f32)
        left, right = [], []
        for k in range(GROUP):
            b, ut, s, c, base = block_of(table, trig, groups, j, k)
            u = lanes_of((1, TILE), 1) + base
            _, kz, kzd = z_weights(z0, depth, u, s, c, samples)
            first, second = [], []
            for r in range(4):
                direct = sums[r * ut_count + ut, pl.ds(b, 1), :]
                tilted = sums[tiles + r * ut_count + ut, pl.ds(b, 1), :]
                first.append(kz * direct + kzd * tilted)
                second.append(kz * tilted)
            left += [jnp.concatenate(first, 0), jnp.concatenate(second, 0)]
            uu = lanes_of((TILE, TILE), 0) + base
            kx, kxd = bump(xx - uu * c)
            right += [kx.astype(bf16), (kxd * (uu * (s * (1.0 / samples)))).astype(bf16)]
        left = jnp.concatenate(left, 1)
        hi = left.astype(bf16)
        lo = (left - hi.astype(f32)).astype(bf16)
        both = jnp.dot(
            jnp.concatenate([hi, lo], 0), jnp.concatenate(right, 0), preferred_element_type=f32
        )
        total[xt] = total[xt] + both[: 4 * depth] + both[4 * depth :]
        return carry

    lax.fori_loop(0, table[0], step, 0)
    for xt in range(total.shape[0]):
        for r in range(4):
            out[:, r, xt * TILE : (xt + 1) * TILE] = total[xt, r * depth : r * depth + planes, :]


def swap(x, axis, size, distance):
    return lax.ppermute(x, axis, [(i, i ^ distance) for i in range(size)])


def local(volume, observed, ctf_table, ctf_class, bin_ids):
    slab, rows, columns = volume.shape
    mine, _, samples = observed.shape
    n_gz, n_dom = lax.axis_size("gz"), lax.axis_size("dom")
    devices = n_gz * n_dom
    bins = NB_DEV * n_dom
    planes = NZ // devices
    count = mine * devices
    width = rows * samples
    xt_count, ut_count = columns // TILE, samples // TILE
    gz, dom = lax.axis_index("gz"), lax.axis_index("dom")
    device = gz * n_dom + dom

    ids = jnp.stack([ctf_class, bin_ids], 1).astype(bf16)
    ids = jnp.pad(ids, ((0, 0), (0, TILE - 2)))
    packed = jnp.concatenate([observed.reshape(mine, width), ids], 1)
    n_z = n_dom // 2
    column = jnp.concatenate(
        [packed] + [swap(packed, "dom", n_dom, 2 * k) for k in range(1, n_z)], 0
    )
    planes_of = [column] + [swap(column, "gz", n_gz, j) for j in range(1, n_gz)]
    gathered = planes_of + [swap(part, "dom", n_dom, 1) for part in planes_of]
    place = jnp.stack([gz, dom // 2, dom % 2]).astype(jnp.int32)

    table, groups = make_plan(devices, bins, samples, columns)
    table = lax.dynamic_index_in_dim(jnp.asarray(table), device, 0, keepdims=False)
    where = (device * planes)[None].astype(jnp.int32)
    theta = -0.5 * math.pi + math.pi * (jnp.arange(bins, dtype=f32) + 0.5) / bins
    trig = jnp.stack([jnp.sin(theta), jnp.cos(theta)])

    above = lax.ppermute(volume[:1], "gz", [(i, i - 1) for i in range(1, n_gz)])
    own = lax.dynamic_slice_in_dim(volume, dom * planes, planes, 0)
    inner = lax.dynamic_slice_in_dim(volume, jnp.minimum((dom + 1) * planes, slab - 1), 1, 0)
    halo = jnp.where(dom == n_dom - 1, above, inner)
    depth_in = round_up(planes + 1, 8)
    field = jnp.concatenate([own, halo, jnp.zeros((depth_in - planes - 1, rows, columns), f32)], 0)
    field = field.reshape(depth_in, rows, xt_count, TILE).transpose(2, 1, 0, 3)
    field = field.reshape(xt_count, rows * depth_in, TILE)
    field_hi = lax.reduce_precision(field, 8, 7)
    field_lo = (field - field_hi).astype(bf16)
    field_hi = field_hi.astype(bf16)

    smem = pl.BlockSpec(memory_space=pltpu.SMEM)
    vmem = pl.BlockSpec(memory_space=pltpu.VMEM)
    hbm = pl.BlockSpec(memory_space=pl.ANY)
    params = pltpu.CompilerParams(vmem_limit_bytes=VMEM)
    slices = pl.pallas_call(
        functools.partial(extract_kernel, groups, planes, samples),
        out_shape=jax.ShapeDtypeStruct((bins * ut_count, 2 * rows, TILE), f32),
        in_specs=[smem, smem, smem, vmem, vmem, hbm],
        out_specs=vmem,
        compiler_params=params,
        cost_estimate=pl.CostEstimate(flops=6 * 10**9, bytes_accessed=2**20, transcendentals=0),
        name="extract",
    )(table, trig, where, field_hi, field_lo, column)

    slices = lax.reduce_precision(slices, 8, 7)
    slices = slices.reshape(bins, ut_count, 2 * rows, TILE).transpose(0, 2, 1, 3)
    slices = slices.reshape(bins, 2, 2, rows // 2, samples)
    direct, slope = slices[:, 0], slices[:, 1]
    squares = jnp.stack([jnp.sum(slope * slope, 1), jnp.sum(direct * slope, 1)])
    pairs = lax.dot_general(
        (ctf_table * ctf_table).reshape(NCTF, -1),
        squares.reshape(2 * bins, -1),
        NT,
        precision=lax.Precision.HIGHEST,
        preferred_element_type=f32,
    )
    slope = slope.reshape(bins, width).astype(bf16)
    flat_ctf = ctf_table.reshape(NCTF, -1)
    ctf_hi = lax.reduce_precision(flat_ctf, 8, 7)
    ctf_lo = (flat_ctf - ctf_hi).astype(bf16)
    ctf_hi = ctf_hi.astype(bf16)

    weighted, parts, bins_row = pl.pallas_call(
        functools.partial(particle_kernel, width, mine, n_gz, n_dom),
        out_shape=[
            jax.ShapeDtypeStruct((count, width), bf16),
            jax.ShapeDtypeStruct((2 * count // TILE, TILE), f32),
            jax.ShapeDtypeStruct((1, count), f32),
        ],
        in_specs=[smem] + [hbm] * len(gathered) + [vmem] * 4,
        out_specs=[vmem] * 3,
        scratch_shapes=[
            pltpu.VMEM((count, width + TILE), bf16),
            pltpu.SemaphoreType.DMA((devices,)),
        ],
        compiler_params=params,
        name="particles",
    )(place, *gathered, ctf_hi, ctf_lo, slope, pairs)

    plain = pl.pallas_call(
        plain_kernel,
        out_shape=jax.ShapeDtypeStruct((bins, width), f32),
        in_specs=[vmem, vmem],
        out_specs=vmem,
        compiler_params=params,
        cost_estimate=pl.CostEstimate(flops=2 * 10**9, bytes_accessed=2**21, transcendentals=0),
        name="plain_sums",
    )(bins_row, weighted)

    parts = sum([swap(parts, "dom", n_dom, k) for k in range(1, n_dom)], parts)
    parts = [parts] + [swap(parts, "gz", n_gz, j) for j in range(1, n_gz)]

    depth = round_up(planes, 8)
    pose, spread = pl.pallas_call(
        functools.partial(spread_kernel, groups, planes, samples, mine, n_gz),
        out_shape=[
            jax.ShapeDtypeStruct((1, mine), f32),
            jax.ShapeDtypeStruct((planes, rows, columns), f32),
        ],
        in_specs=[smem, smem, smem] + [vmem] * (3 + n_gz),
        out_specs=[vmem, vmem],
        scratch_shapes=[
            pltpu.VMEM((2 * width // TILE, bins, TILE), f32),
            pltpu.VMEM((xt_count, rows * depth, TILE), f32),
            pltpu.VMEM((count // TILE, TILE), f32),
        ],
        compiler_params=params,
        name="spread",
    )(table, trig, where, bins_row, weighted, plain, *parts)
    pose = pose.reshape(mine)
    return pose, spread


def solution(mesh):
    return jax.shard_map(
        local,
        mesh=mesh,
        in_specs=(
            P("gz", None, None),
            P(("gz", "dom"), None, None),
            P(),
            P(("gz", "dom")),
            P(("gz", "dom")),
        ),
        out_specs=(P(("gz", "dom")), P(("gz", "dom"), None, None)),
        check_vma=False,
    )
```

```python
import functools
import math

import jax
import jax.numpy as jnp
import numpy as np
from jax import lax
from jax.experimental import pallas as pl
from jax.experimental.pallas import tpu as pltpu
from jax.sharding import PartitionSpec as P

NZ = 768
NB_DEV = 8
NCTF = 32
ITERS = 3
EPS = 1e-05
TILE = 128
GROUP = 4
CHUNK = 512
VMEM = 56 * 2**20
f32 = jnp.float32
bf16 = jnp.bfloat16
NT = (((1,), (1,)), ((), ()))


def round_up(n, m):
    return -(-n // m) * m


def make_plan(devices, bins, samples, columns):
    planes = NZ // devices
    middle = NZ // 2
    ut_count, xt_count = samples // TILE, columns // TILE
    theta = -0.5 * math.pi + math.pi * (np.arange(bins) + 0.5) / bins
    trig = np.concatenate([np.sin(theta), np.cos(theta)]).astype(np.float32)
    u = np.arange(samples)
    slack = 1e-3
    reach = 0
    plans = []
    for spread in (False, True):
        rows = []
        for device in range(devices):
            z0 = device * planes
            z1 = z0 + planes
            lists = [[] for _ in range(xt_count)]
            edge = []
            for b in range(bins):
                s, c = math.sin(theta[b]), math.cos(theta[b])
                centre = middle + u * s
                near = (centre > z0 - slack - (1 if spread else 0)) & (centre < z1 + slack)
                if spread:
                    near[0] = z0 - 1 < middle < z1
                else:
                    near[0] = z0 <= middle < z1 if s > 0 else z0 < middle <= z1
                if not near.any():
                    continue
                if spread and s < 0 and z0 == middle:
                    edge.append(b * 4)
                    reach = max(reach, int(u[near].max()) + 1)
                    continue
                for ut in range(ut_count):
                    hit = u[ut * TILE : (ut + 1) * TILE][near[ut * TILE : (ut + 1) * TILE]]
                    if hit.size == 0:
                        continue
                    first = max(0, int((hit.min() * c - 1.01) // TILE))
                    last = min(xt_count - 1, int((hit.max() * c + 1.01) // TILE))
                    for xt in range(first, last + 1):
                        lists[xt].append(b * 4 + ut)
            idle = (bins - 1 if z0 < middle else 0) * 4 + ut_count - 1
            tiles, codes = [], []
            for xt, entries in enumerate(lists):
                entries = entries + [idle] * (-len(entries) % GROUP)
                tiles += [xt] * (len(entries) // GROUP)
                codes += entries
            rows.append((tiles, codes, edge))
        groups = max(len(tiles) for tiles, _, _ in rows)
        start = 1 + groups * (1 + GROUP)
        table = np.zeros((devices, start + 1 + max(len(edge) for _, _, edge in rows)), np.int32)
        for device, (tiles, codes, edge) in enumerate(rows):
            table[device, 0] = len(tiles)
            table[device, 1 : 1 + len(tiles)] = tiles
            table[device, 1 + groups : 1 + groups + len(codes)] = codes
            table[device, start] = len(edge) // GROUP
            table[device, start + 1 : start + 1 + len(edge)] = edge
        plans.append((table, groups))
    edge_samples = round_up(reach, 16)
    assert edge_samples <= TILE and (bins // 2) % GROUP == 0
    return plans[0], plans[1], edge_samples, trig


def lanes_of(shape, axis):
    return lax.broadcasted_iota(jnp.int32, shape, axis).astype(f32)


def block_of(table, trig, at, bins):
    code = table[at]
    b = lax.shift_right_logical(code, 2)
    ut = lax.bitwise_and(code, 3)
    return b, ut, trig[b], trig[bins + b], (ut * TILE).astype(f32)


def split3(x):
    hi = x.astype(bf16)
    rest = x - hi.astype(f32)
    mid = rest.astype(bf16)
    return [hi, mid, (rest - mid.astype(f32)).astype(bf16)]


def bump(t):
    falloff = jnp.maximum(1.0 - t * t, 0.0)
    return falloff * falloff, -4.0 * t * falloff


def z_weights(z0, rows, u, s, c, samples):
    centre = 0.5 * NZ + u * s
    kz, kzd = bump((z0 + lanes_of((rows, TILE), 0)) - centre)
    return centre, kz, kzd * (-u * c * (1.0 / samples))


def extract_kernel(
    groups, length, samples, bins, planes, n_dom,
    table, trig, volume, above, ctf, slope, pairs, field, vhi, vlo, out, sem,
):
    depth = field.shape[0]
    xt_count = vhi.shape[0]
    ut_count = samples // TILE
    dom = lax.axis_index("dom")
    device = lax.axis_index("gz") * n_dom + dom
    row = device * length
    first = device * planes
    z0, z1 = first.astype(f32), (first + planes).astype(f32)

    own = pltpu.make_async_copy(
        volume.at[pl.ds(dom * planes, planes)], field.at[pl.ds(0, planes)], sem.at[0]
    )
    own.start()

    @pl.when(dom < n_dom - 1)
    def _():
        copy = pltpu.make_async_copy(
            volume.at[pl.ds((dom + 1) * planes, 1)], field.at[pl.ds(planes, 1)], sem.at[1]
        )
        copy.start()
        copy.wait()

    @pl.when(dom == n_dom - 1)
    def _():
        copy = pltpu.make_async_copy(above, field.at[pl.ds(planes, 1)], sem.at[1])
        copy.start()
        copy.wait()

    for z in range(planes + 1, depth):
        field[z] = jnp.zeros(field.shape[1:], f32)
    out[...] = jnp.zeros_like(out)
    own.wait()
    for xt in range(xt_count):
        stacked = jnp.concatenate(
            [field[:, r, xt * TILE : (xt + 1) * TILE] for r in range(4)], 0
        )
        hi = stacked.astype(bf16)
        vhi[xt] = hi
        vlo[xt] = (stacked - hi.astype(f32)).astype(bf16)

    def step(j, carry):
        xt = table[row + 1 + j]
        hi_rows, lo_rows = vhi[xt], vlo[xt]
        xx = lanes_of((TILE, TILE), 0) + (xt * TILE).astype(f32)
        for k in range(GROUP):
            at = row + 1 + groups + j * GROUP + k
            b, ut, s, c, base = block_of(table, trig, at, bins)
            u = lanes_of((1, TILE), 1) + base
            centre, kz, kzd = z_weights(z0, depth, u, s, c, samples)
            below = s < 0.0
            place = centre * jnp.where(below, -1.0, 1.0)
            least, most = jnp.where(below, -z1, z0), jnp.where(below, -z0, z1)
            own = jnp.where((place >= least) & (place < most), 1.0, 0.0)
            kz, kzd = kz * own, kzd * own
            kx, kxd = bump(xx - u * c)
            weights = jnp.concatenate([kx, kxd * (u * s * (1.0 / samples))], 1)
            whi = weights.astype(bf16)
            wlo = (weights - whi.astype(f32)).astype(bf16)
            sampled = (
                jnp.dot(hi_rows, whi, preferred_element_type=f32)
                + jnp.dot(lo_rows, whi, preferred_element_type=f32)
                + jnp.dot(hi_rows, wlo, preferred_element_type=f32)
            )
            leading, second = [], []
            for r in range(4):
                direct = sampled[r * depth : (r + 1) * depth, :TILE]
                tilted = sampled[r * depth : (r + 1) * depth, TILE:]
                leading.append(jnp.sum(direct * kz, axis=0, keepdims=True))
                second.append(jnp.sum(direct * kzd + tilted * kz, axis=0, keepdims=True))
            span = pl.ds(pl.multiple_of((b * ut_count + ut) * 8, 8), 8)
            out[span, :] = out[span, :] + jnp.concatenate(leading + second, 0)
        return carry

    lax.fori_loop(0, table[row], step, 0)

    slope[...] = jnp.zeros_like(slope)
    square, mixed = [], []
    for y in range(2):
        for ut in range(ut_count):
            square_sum, mixed_sum = 0.0, 0.0
            for r in (y, 2 + y):
                direct = out[pl.ds(ut * 8 + r, bins, stride=ut_count * 8), :].astype(bf16).astype(f32)
                tilted = out[pl.ds(ut * 8 + 4 + r, bins, stride=ut_count * 8), :].astype(bf16)
                at = (r * ut_count + ut) * TILE
                slope[bins:, at : at + TILE] = tilted
                tilted = tilted.astype(f32)
                square_sum = square_sum + tilted * tilted
                mixed_sum = mixed_sum - direct * tilted
            square.append(square_sum)
            mixed.append(mixed_sum)
    moments = jnp.concatenate([jnp.concatenate(square, 1), jnp.concatenate(mixed, 1)], 0)
    flat = jnp.concatenate([ctf[:, 0, :], ctf[:, 1, :]], 1)
    product = lax.dot_general(
        flat * flat, moments, NT, precision=lax.Precision.HIGHEST, preferred_element_type=f32
    )
    pairs[...] = jnp.concatenate(split3(product), 1)


def particle_kernel(width, mine, n_gz, n_dom, *refs):
    blocks = refs[: 2 * n_gz]
    ctf, slope, pairs, weighted, parts, bins_row, packed, sems = refs[2 * n_gz :]
    n_z = n_dom // 2
    gz, dom = lax.axis_index("gz"), lax.axis_index("dom")
    z, core = lax.shift_right_logical(dom, 1), lax.bitwise_and(dom, 1)
    copies = []
    for c in range(2):
        for j in range(n_gz):
            for k in range(n_z):
                owner = ((gz ^ j) * n_z + (z ^ k)) * 2 + (core ^ c)
                start = pl.multiple_of(owner * mine, mine)
                copies.append(
                    pltpu.make_async_copy(
                        blocks[c * n_gz + j].at[pl.ds(k * mine, mine), :],
                        packed.at[pl.ds(start, mine), :],
                        sems.at[len(copies)],
                    )
                )
    for copy in copies:
        copy.start()
    for copy in copies:
        copy.wait()

    total = packed.shape[0]
    count = min(CHUNK, total)
    both = slope.shape[0]
    bins = both // 2
    flat = jnp.concatenate([ctf[:, 0, :], ctf[:, 1, :]], 1)
    ctf_hi = flat.astype(bf16)
    ctf_lo = (flat - ctf_hi.astype(f32)).astype(bf16)
    upper = jnp.where(lanes_of((8, both), 1) >= bins, 1.0, 0.0)
    select = jnp.where(lanes_of((8, both), 0) == upper, 1.0, 0.0).astype(bf16)
    select = jnp.concatenate([select] * 3, 1)

    def step(i, carry):
        span = pl.ds(pl.multiple_of(i * count, count), count)
        ids = packed[span, width:]
        classes = ids[:, 0:1].astype(f32)
        onehot_class = jnp.where(lanes_of((count, NCTF), 1) == classes, 1.0, 0.0).astype(bf16)
        bin_of = ids[:, 1:2].astype(f32)
        lane = lanes_of((count, both), 1)
        chosen = (lane == bin_of) | (lane == bin_of + bins)
        contrast = jnp.dot(onehot_class, ctf_hi, preferred_element_type=f32) + jnp.dot(
            onehot_class, ctf_lo, preferred_element_type=f32
        )
        contrast = jnp.concatenate([contrast, contrast], 1)
        w = contrast * packed[span, :width].astype(f32)
        whi = w.astype(bf16)
        wlo = (w - whi.astype(f32)).astype(bf16)
        weighted[span, :] = whi
        slopes = slope[...]
        along = lax.dot_general(whi, slopes, NT, preferred_element_type=f32) + lax.dot_general(
            wlo, slopes, NT, preferred_element_type=f32
        )
        tables = jnp.dot(onehot_class, pairs[...], preferred_element_type=f32)
        tables = tables[:, :both] + tables[:, both : 2 * both] + tables[:, 2 * both :]
        terms = jnp.concatenate(split3(jnp.where(chosen, along + tables, 0.0)), 1)
        rows = lax.dot_general(select, terms, NT, preferred_element_type=f32)
        for n in range(2):
            row = rows[n : n + 1]
            for q in range(count // TILE):
                at = n * (total // TILE) + i * (count // TILE) + q
                parts[pl.ds(at, 1), :] = row[:, q * TILE : (q + 1) * TILE]
        pick = jnp.where(lanes_of((8, TILE), 1) == 1.0, 1.0, 0.0).astype(bf16)
        bins_row[:, span] = lax.dot_general(pick, ids, NT, preferred_element_type=f32)[0:1]
        return carry

    lax.fori_loop(0, total // count, step, 0)


def plain_kernel(bins_row, weighted, plain):
    count = weighted.shape[0]
    chunk = min(CHUNK, count)
    sums = jnp.zeros(plain.shape, f32)
    for i in range(count // chunk):
        span = slice(i * chunk, (i + 1) * chunk)
        belongs = lanes_of((plain.shape[0], chunk), 0) == bins_row[:, span]
        onehot = jnp.where(belongs, 1.0, 0.0).astype(bf16)
        sums = sums + jnp.dot(onehot, weighted[span, :], preferred_element_type=f32)
    plain[...] = sums


def spread_kernel(
    groups, length, planes, samples, edge_samples, mine, n_gz, n_dom,
    table, trig, bins_row, weighted, plain, *refs
):
    parts = refs[:n_gz]
    pose, out, sums, total, poses = refs[n_gz:]
    bins, width = plain.shape
    tiles = width // TILE
    ut_count = samples // TILE
    depth = total.shape[1] // 4
    count = bins_row.shape[1]
    chunk = min(CHUNK, count)
    device = lax.axis_index("gz") * n_dom + lax.axis_index("dom")
    row = device * length
    z0 = (device * planes).astype(f32)

    rows = count // TILE
    scalars = sum([part[...] for part in parts[1:]], parts[0][...])
    square, pull = scalars[:rows], scalars[rows:]
    curvature = square + EPS
    shift = jnp.zeros_like(square)
    for _ in range(ITERS):
        shift = shift + 0.5 * (pull - shift * square) / curvature
    poses[...] = shift * jnp.sqrt(curvature)
    first = device * mine
    line = poses[pl.ds(lax.div(first, TILE), 1), :]
    pose[...] = pltpu.roll(line, TILE - lax.rem(first, TILE), 1)[:, :mine]
    shift = jnp.concatenate([shift[q : q + 1] for q in range(rows)], 1)

    slope_sum = jnp.zeros((bins, width), f32)
    for i in range(count // chunk):
        span = slice(i * chunk, (i + 1) * chunk)
        belongs = lanes_of((bins, chunk), 0) == bins_row[:, span]
        scaled = jnp.where(belongs, shift[:, span], 0.0)
        hi = scaled.astype(bf16)
        lo = (scaled - hi.astype(f32)).astype(bf16)
        rows = weighted[span, :]
        slope_sum = (
            slope_sum
            + jnp.dot(hi, rows, preferred_element_type=f32)
            + jnp.dot(lo, rows, preferred_element_type=f32)
        )
    for q in range(tiles):
        sums[q] = plain[:, q * TILE : (q + 1) * TILE]
        sums[tiles + q] = slope_sum[:, q * TILE : (q + 1) * TILE]
    total[...] = jnp.zeros_like(total)

    def step(j, carry):
        xt = table[row + 1 + j]
        xx = lanes_of((TILE, TILE), 1) + (xt * TILE).astype(f32)
        left, right = [], []
        for k in range(GROUP):
            at = row + 1 + groups + j * GROUP + k
            b, ut, s, c, base = block_of(table, trig, at, bins)
            u = lanes_of((1, TILE), 1) + base
            _, kz, kzd = z_weights(z0, depth, u, s, c, samples)
            first, second = [], []
            for r in range(4):
                direct = sums[r * ut_count + ut, pl.ds(b, 1), :]
                tilted = sums[tiles + r * ut_count + ut, pl.ds(b, 1), :]
                first.append(kz * direct + kzd * tilted)
                second.append(kz * tilted)
            left += [jnp.concatenate(first, 0), jnp.concatenate(second, 0)]
            uu = lanes_of((TILE, TILE), 0) + base
            kx, kxd = bump(xx - uu * c)
            right += [kx.astype(bf16), (kxd * (uu * (s * (1.0 / samples)))).astype(bf16)]
        left = jnp.concatenate(left, 1)
        hi = left.astype(bf16)
        lo = (left - hi.astype(f32)).astype(bf16)
        both = jnp.dot(
            jnp.concatenate([hi, lo], 0), jnp.concatenate(right, 0), preferred_element_type=f32
        )
        total[xt] = total[xt] + both[: 4 * depth] + both[4 * depth :]
        return carry

    lax.fori_loop(0, table[row], step, 0)
    tail = row + 1 + groups * (1 + GROUP)

    def edge(j, carry):
        left, right = [], []
        rest = jnp.zeros((TILE - edge_samples, TILE), f32)
        for k in range(GROUP):
            b, _, s, c, _ = block_of(table, trig, tail + 1 + j * GROUP + k, bins)
            u = lanes_of((1, TILE), 1)
            _, kz, kzd = z_weights(z0, 1, u, s, c, samples)
            direct = jnp.concatenate(
                [sums[r * ut_count, pl.ds(b, 1), :] for r in range(4)], 0
            )
            tilted = jnp.concatenate(
                [sums[tiles + r * ut_count, pl.ds(b, 1), :] for r in range(4)], 0
            )
            left += [kz * direct + kzd * tilted, kz * tilted]
            uu = lanes_of((edge_samples, TILE), 0)
            kx, kxd = bump(lanes_of((edge_samples, TILE), 1) - uu * c)
            for part in (kx, kxd * (uu * (s * (1.0 / samples)))):
                right.append(jnp.concatenate([part, rest], 0).astype(bf16))
        left = jnp.concatenate(left, 1)
        hi = left.astype(bf16).astype(f32)
        split = jnp.concatenate([hi, left - hi], 0).astype(bf16)
        both = jnp.dot(split, jnp.concatenate(right, 0), preferred_element_type=f32)
        return carry + both[:4] + both[4:]

    extra = lax.fori_loop(0, table[tail], edge, jnp.zeros((4, TILE), f32))
    for xt in range(total.shape[0]):
        for r in range(4):
            out[:, r, xt * TILE : (xt + 1) * TILE] = total[xt, r * depth : r * depth + planes, :]
    out[0, :, :TILE] = out[0, :, :TILE] + extra


def swap(x, axis, size, distance):
    return lax.ppermute(x, axis, [(i, i ^ distance) for i in range(size)])


def local(volume, observed, ctf_table, ctf_class, bin_ids):
    slab, rows, columns = volume.shape
    mine, _, samples = observed.shape
    n_gz, n_dom = lax.axis_size("gz"), lax.axis_size("dom")
    devices = n_gz * n_dom
    bins = NB_DEV * n_dom
    planes = NZ // devices
    count = mine * devices
    width = rows * samples
    xt_count, ut_count = columns // TILE, samples // TILE
    ids = jnp.stack([ctf_class, bin_ids], 1).astype(bf16)
    ids = jnp.pad(ids, ((0, 0), (0, TILE - 2)))
    packed = jnp.concatenate([observed.reshape(mine, width), ids], 1)
    n_z = n_dom // 2
    above = lax.ppermute(volume[:1], "gz", [(i, i - 1) for i in range(1, n_gz)])
    column = jnp.concatenate(
        [packed] + [swap(packed, "dom", n_dom, 2 * k) for k in range(1, n_z)], 0
    )
    column, above = lax.optimization_barrier((column, above))
    planes_of = [column] + [swap(column, "gz", n_gz, j) for j in range(1, n_gz)]

    extract_plan, spread_plan, edge_samples, trig = make_plan(devices, bins, samples, columns)
    trig = jnp.asarray(trig)
    depth_in = round_up(planes + 1, 8)

    smem = pl.BlockSpec(memory_space=pltpu.SMEM)
    vmem = pl.BlockSpec(memory_space=pltpu.VMEM)
    hbm = pl.BlockSpec(memory_space=pl.ANY)
    params = pltpu.CompilerParams(vmem_limit_bytes=VMEM)
    table, groups = extract_plan
    slope, pairs = pl.pallas_call(
        functools.partial(
            extract_kernel, groups, table.shape[1], samples, bins, planes, n_dom
        ),
        out_shape=[
            jax.ShapeDtypeStruct((2 * bins, width), bf16),
            jax.ShapeDtypeStruct((NCTF, 6 * bins), bf16),
        ],
        in_specs=[smem, smem, hbm, hbm, vmem],
        out_specs=[vmem, vmem],
        scratch_shapes=[
            pltpu.VMEM((depth_in, rows, columns), f32),
            pltpu.VMEM((xt_count, rows * depth_in, TILE), bf16),
            pltpu.VMEM((xt_count, rows * depth_in, TILE), bf16),
            pltpu.VMEM((bins * ut_count * 2 * rows, TILE), f32),
            pltpu.SemaphoreType.DMA((2,)),
        ],
        compiler_params=params,
        cost_estimate=pl.CostEstimate(flops=6 * 10**9, bytes_accessed=2**20, transcendentals=0),
        name="extract",
    )(jnp.asarray(table.reshape(-1)), trig, volume, above, ctf_table)

    planes_of, slope = lax.optimization_barrier((planes_of, slope))
    gathered = planes_of + [swap(part, "dom", n_dom, 1) for part in planes_of]
    weighted, parts, bins_row = pl.pallas_call(
        functools.partial(particle_kernel, width, mine, n_gz, n_dom),
        out_shape=[
            jax.ShapeDtypeStruct((count, width), bf16),
            jax.ShapeDtypeStruct((2 * count // TILE, TILE), f32),
            jax.ShapeDtypeStruct((1, count), f32),
        ],
        in_specs=[hbm] * len(gathered) + [vmem] * 3,
        out_specs=[vmem] * 3,
        scratch_shapes=[
            pltpu.VMEM((count, width + TILE), bf16),
            pltpu.SemaphoreType.DMA((devices,)),
        ],
        compiler_params=params,
        name="particles",
    )(*gathered, ctf_table, slope, pairs)

    plain = pl.pallas_call(
        plain_kernel,
        out_shape=jax.ShapeDtypeStruct((bins, width), f32),
        in_specs=[vmem, vmem],
        out_specs=vmem,
        compiler_params=params,
        cost_estimate=pl.CostEstimate(flops=2 * 10**9, bytes_accessed=2**21, transcendentals=0),
        name="plain_sums",
    )(bins_row, weighted)

    parts = sum([swap(parts, "dom", n_dom, k) for k in range(1, n_dom)], parts)
    parts = [parts] + [swap(parts, "gz", n_gz, j) for j in range(1, n_gz)]

    depth = round_up(planes, 8)
    table, groups = spread_plan
    pose, spread = pl.pallas_call(
        functools.partial(
            spread_kernel, groups, table.shape[1], planes, samples, edge_samples, mine, n_gz, n_dom
        ),
        out_shape=[
            jax.ShapeDtypeStruct((1, mine), f32),
            jax.ShapeDtypeStruct((planes, rows, columns), f32),
        ],
        in_specs=[smem, smem] + [vmem] * (3 + n_gz),
        out_specs=[vmem, vmem],
        scratch_shapes=[
            pltpu.VMEM((2 * width // TILE, bins, TILE), f32),
            pltpu.VMEM((xt_count, rows * depth, TILE), f32),
            pltpu.VMEM((count // TILE, TILE), f32),
        ],
        compiler_params=params,
        name="spread",
    )(jnp.asarray(table.reshape(-1)), trig, bins_row, weighted, plain, *parts)
    pose = pose.reshape(mine)
    return pose, spread


def solution(mesh):
    return jax.shard_map(
        local,
        mesh=mesh,
        in_specs=(
            P("gz", None, None),
            P(("gz", "dom"), None, None),
            P(),
            P(("gz", "dom")),
            P(("gz", "dom")),
        ),
        out_specs=(P(("gz", "dom")), P(("gz", "dom"), None, None)),
        check_vma=False,
    )
```

```python
import functools
import math

import jax
import jax.numpy as jnp
import numpy as np
from jax import lax
from jax.experimental import pallas as pl
from jax.experimental.pallas import tpu as pltpu
from jax.sharding import PartitionSpec as P

NZ = 768
NB_DEV = 8
NCTF = 32
ITERS = 3
EPS = 1e-05
TILE = 128
GROUP = 4
EDGE_GROUP = 8
CHUNK = 512
f32 = jnp.float32
bf16 = jnp.bfloat16
NT = (((1,), (1,)), ((), ()))


def round_up(n, m):
    return -(-n // m) * m


def make_plan(devices, bins, samples, columns):
    planes = NZ // devices
    middle = NZ // 2
    ut_count, xt_count = samples // TILE, columns // TILE
    theta = -0.5 * math.pi + math.pi * (np.arange(bins) + 0.5) / bins
    trig = np.concatenate([np.sin(theta), np.cos(theta)]).astype(np.float32)
    u = np.arange(samples)
    slack = 1e-3
    reach = 0
    plans = []
    for spread in (False, True):
        rows = []
        for device in range(devices):
            z0 = device * planes
            z1 = z0 + planes
            lists = [[] for _ in range(xt_count)]
            edge = []
            for b in range(bins):
                s, c = math.sin(theta[b]), math.cos(theta[b])
                centre = middle + u * s
                near = (centre > z0 - slack - (1 if spread else 0)) & (centre < z1 + slack)
                if spread:
                    near[0] = z0 - 1 < middle < z1
                else:
                    near[0] = z0 <= middle < z1 if s > 0 else z0 < middle <= z1
                if not near.any():
                    continue
                if spread and s < 0 and z0 == middle:
                    edge.append(b * 4)
                    reach = max(reach, int(u[near].max()) + 1)
                    continue
                for ut in range(ut_count):
                    hit = u[ut * TILE : (ut + 1) * TILE][near[ut * TILE : (ut + 1) * TILE]]
                    if hit.size == 0:
                        continue
                    first = max(0, int((hit.min() * c - 1.01) // TILE))
                    last = min(xt_count - 1, int((hit.max() * c + 1.01) // TILE))
                    for xt in range(first, last + 1):
                        lists[xt].append(b * 4 + ut)
            idle = (bins - 1 if z0 < middle else 0) * 4 + ut_count - 1
            tiles, codes = [], []
            for xt, entries in enumerate(lists):
                entries = entries + [idle] * (-len(entries) % GROUP)
                tiles += [xt] * (len(entries) // GROUP)
                codes += entries
            rows.append((tiles, codes, edge))
        groups = max(len(tiles) for tiles, _, _ in rows)
        start = 1 + groups * (1 + GROUP)
        table = np.zeros((devices, start + 1 + max(len(edge) for _, _, edge in rows)), np.int32)
        for device, (tiles, codes, edge) in enumerate(rows):
            table[device, 0] = len(tiles)
            table[device, 1 : 1 + len(tiles)] = tiles
            table[device, 1 + groups : 1 + groups + len(codes)] = codes
            table[device, start] = len(edge) // EDGE_GROUP
            table[device, start + 1 : start + 1 + len(edge)] = edge
        plans.append((table, groups))
    edge_samples = round_up(reach, 16)
    assert edge_samples <= TILE and (bins // 2) % EDGE_GROUP == 0
    return plans[0], plans[1], edge_samples, trig


def lanes_of(shape, axis):
    return lax.broadcasted_iota(jnp.int32, shape, axis).astype(f32)


def block_of(table, trig, at, bins):
    code = table[at]
    b = lax.shift_right_logical(code, 2)
    ut = lax.bitwise_and(code, 3)
    return b, ut, trig[b], trig[bins + b], (ut * TILE).astype(f32)


def split3(x):
    hi = x.astype(bf16)
    rest = x - hi.astype(f32)
    mid = rest.astype(bf16)
    return [hi, mid, (rest - mid.astype(f32)).astype(bf16)]


def bump(t):
    falloff = jnp.maximum(1.0 - t * t, 0.0)
    return falloff * falloff, t * falloff


def row_weights(z0, rows, u, s, c, samples):
    centre = 0.5 * NZ + u * s
    kz, kzd = bump((z0 + lanes_of((rows, TILE), 0)) - centre)
    return centre, kz, kzd, u * (c * (4.0 / samples)), u * (s * (-4.0 / samples))


def reorder(x, device, mine):
    lane = lax.broadcasted_iota(jnp.int32, x.shape, 1)
    rows = x.shape[0]
    size = mine
    bit = 0
    while size < rows // 2 * TILE:
        if size < TILE:
            moved = jnp.where(
                lax.bitwise_and(lane, size) != 0,
                pltpu.roll(x, size, 1),
                pltpu.roll(x, TILE - size, 1),
            )
        else:
            step = size // TILE
            moved = jnp.concatenate([x[r ^ step : (r ^ step) + 1] for r in range(rows)], 0)
        flag = lax.bitwise_and(lax.shift_right_logical(device, bit), 1)
        x = jnp.where(flag == 1, moved, x)
        size, bit = 2 * size, bit + 1
    return x


def position(n_gz, n_dom):
    dom = lax.axis_index("dom")
    n_z = n_dom // 2
    core, z = lax.bitwise_and(dom, 1), lax.shift_right_logical(dom, 1)
    return (core * n_gz + lax.axis_index("gz")) * n_z + z


def extract_kernel(
    groups, length, samples, bins, planes, n_dom,
    table, trig, volume, above, ctf, slope, pairs, field, vhi, vlo, out, sem,
):
    depth = field.shape[0]
    xt_count = vhi.shape[0]
    ut_count = samples // TILE
    dom = lax.axis_index("dom")
    device = lax.axis_index("gz") * n_dom + dom
    row = device * length
    first = device * planes
    z0, z1 = first.astype(f32), (first + planes).astype(f32)

    own = pltpu.make_async_copy(
        volume.at[pl.ds(dom * planes, planes)], field.at[pl.ds(0, planes)], sem.at[0]
    )
    own.start()

    field[planes] = above[0]
    for z in range(planes + 1, depth):
        field[z] = jnp.zeros(field.shape[1:], f32)
    out[...] = jnp.zeros_like(out)
    own.wait()
    for xt in range(xt_count):
        stacked = jnp.concatenate(
            [field[:, r, xt * TILE : (xt + 1) * TILE] for r in range(4)], 0
        )
        hi = stacked.astype(bf16)
        vhi[xt] = hi
        vlo[xt] = (stacked - hi.astype(f32)).astype(bf16)

    def step(j, carry):
        xt = table[row + 1 + j]
        hi_rows, lo_rows = vhi[xt], vlo[xt]
        xx = lanes_of((TILE, TILE), 0) + (xt * TILE).astype(f32)
        for k in range(GROUP):
            at = row + 1 + groups + j * GROUP + k
            b, ut, s, c, base = block_of(table, trig, at, bins)
            u = lanes_of((1, TILE), 1) + base
            centre, kz, kzd, z_factor, x_factor = row_weights(z0, depth, u, s, c, samples)
            below = s < 0.0
            place = centre * jnp.where(below, -1.0, 1.0)
            least, most = jnp.where(below, -z1, z0), jnp.where(below, -z0, z1)
            own = jnp.where((place >= least) & (place < most), 1.0, 0.0)
            z_factor, x_factor = z_factor * own, x_factor * own
            weights = jnp.concatenate(bump(xx - u * c), 1)
            whi = weights.astype(bf16)
            wlo = (weights - whi.astype(f32)).astype(bf16)
            sampled = (
                jnp.dot(hi_rows, whi, preferred_element_type=f32)
                + jnp.dot(lo_rows, whi, preferred_element_type=f32)
                + jnp.dot(hi_rows, wlo, preferred_element_type=f32)
            )
            leading, second = [], []
            for r in range(4):
                direct = sampled[r * depth : (r + 1) * depth, :TILE]
                tilted = sampled[r * depth : (r + 1) * depth, TILE:]
                leading.append(own * jnp.sum(direct * kz, axis=0, keepdims=True))
                second.append(
                    z_factor * jnp.sum(direct * kzd, axis=0, keepdims=True)
                    + x_factor * jnp.sum(tilted * kz, axis=0, keepdims=True)
                )
            span = pl.ds(pl.multiple_of((b * ut_count + ut) * 8, 8), 8)
            out[span, :] = out[span, :] + jnp.concatenate(leading + second, 0)
        return carry

    lax.fori_loop(0, table[row], step, 0)

    slope[...] = jnp.zeros_like(slope)
    square, mixed = [], []
    for y in range(2):
        for ut in range(ut_count):
            square_sum, mixed_sum = 0.0, 0.0
            for r in (y, 2 + y):
                direct = out[pl.ds(ut * 8 + r, bins, stride=ut_count * 8), :].astype(bf16).astype(f32)
                tilted = out[pl.ds(ut * 8 + 4 + r, bins, stride=ut_count * 8), :].astype(bf16)
                at = (r * ut_count + ut) * TILE
                slope[bins:, at : at + TILE] = tilted
                tilted = tilted.astype(f32)
                square_sum = square_sum + tilted * tilted
                mixed_sum = mixed_sum - direct * tilted
            square.append(square_sum)
            mixed.append(mixed_sum)
    moments = jnp.concatenate([jnp.concatenate(square, 1), jnp.concatenate(mixed, 1)], 0)
    flat = jnp.concatenate([ctf[:, 0, :], ctf[:, 1, :]], 1)
    product = lax.dot_general(
        flat * flat, moments, NT, precision=lax.Precision.HIGHEST, preferred_element_type=f32
    )
    pairs[...] = jnp.concatenate(split3(product), 1)


def particle_kernel(width, mine, n_gz, n_dom, *refs):
    blocks = refs[: 2 * n_gz]
    ctf, slope, pairs, weighted, parts, bins_row = refs[2 * n_gz :]
    size = blocks[0].shape[0]
    joined = max(1, CHUNK // size)
    both = slope.shape[0]
    bins = both // 2
    flat = jnp.concatenate([ctf[:, 0, :], ctf[:, 1, :]], 1)
    ctf_hi = flat.astype(bf16)
    ctf_lo = (flat - ctf_hi.astype(f32)).astype(bf16)
    upper = jnp.where(lanes_of((8, both), 1) >= bins, 1.0, 0.0)
    select = jnp.where(lanes_of((8, both), 0) == upper, 1.0, 0.0).astype(bf16)
    select = jnp.concatenate([select] * 3, 1)
    slopes = slope[...]
    scalars = [[], []]

    for i in range(0, 2 * n_gz, joined):
        packed = jnp.concatenate([ref[...] for ref in blocks[i : i + joined]], 0)
        count = packed.shape[0]
        span = slice(i * size, i * size + count)
        ids = packed[:, width:]
        classes = ids[:, 0:1].astype(f32)
        onehot_class = jnp.where(lanes_of((count, NCTF), 1) == classes, 1.0, 0.0).astype(bf16)
        bin_of = ids[:, 1:2].astype(f32)
        lane = lanes_of((count, both), 1)
        chosen = (lane == bin_of) | (lane == bin_of + bins)
        contrast = jnp.dot(onehot_class, ctf_hi, preferred_element_type=f32) + jnp.dot(
            onehot_class, ctf_lo, preferred_element_type=f32
        )
        contrast = jnp.concatenate([contrast, contrast], 1)
        w = contrast * packed[:, :width].astype(f32)
        whi = w.astype(bf16)
        wlo = (w - whi.astype(f32)).astype(bf16)
        weighted[span, :] = whi
        along = lax.dot_general(whi, slopes, NT, preferred_element_type=f32) + lax.dot_general(
            wlo, slopes, NT, preferred_element_type=f32
        )
        tables = jnp.dot(onehot_class, pairs[...], preferred_element_type=f32)
        tables = tables[:, :both] + tables[:, both : 2 * both] + tables[:, 2 * both :]
        terms = jnp.concatenate(split3(jnp.where(chosen, along + tables, 0.0)), 1)
        rows = lax.dot_general(select, terms, NT, preferred_element_type=f32)
        for n in range(2):
            for q in range(count // TILE):
                scalars[n].append(rows[n : n + 1, q * TILE : (q + 1) * TILE])
        pick = jnp.where(lanes_of((8, TILE), 1) == 1.0, 1.0, 0.0).astype(bf16)
        bins_row[:, span] = lax.dot_general(pick, ids, NT, preferred_element_type=f32)[0:1]

    scalars = jnp.concatenate(scalars[0] + scalars[1], 0)
    scalars = reorder(scalars, position(n_gz, n_dom), mine)
    rows = scalars.shape[0]
    for n in range(parts.shape[0] // rows):
        parts[n * rows : (n + 1) * rows, :] = scalars


def spread_kernel(
    groups, length, planes, samples, edge_samples, mine, n_gz, n_dom,
    table, trig, parts, bins_row, weighted, pose, out, sums, total, poses,
):
    tiles, bins = sums.shape[0] // 2, sums.shape[1]
    ut_count = samples // TILE
    depth = total.shape[1] // 4
    count = bins_row.shape[1]
    chunk = min(CHUNK, count)
    device = lax.axis_index("gz") * n_dom + lax.axis_index("dom")
    row = device * length
    z0 = (device * planes).astype(f32)

    rows = count // TILE
    scalars = jnp.sum(parts[...].reshape(parts.shape[0] // (2 * rows), 2 * rows, TILE), axis=0)
    square, pull = scalars[:rows], scalars[rows:]
    curvature = square + EPS
    shift = jnp.zeros_like(square)
    for _ in range(ITERS):
        shift = shift + 0.5 * (pull - shift * square) / curvature
    here = position(n_gz, n_dom)
    poses[...] = shift * jnp.sqrt(curvature)
    first = here * mine
    line = poses[pl.ds(lax.div(first, TILE), 1), :]
    pose[...] = pltpu.roll(line, TILE - lax.rem(first, TILE), 1)[:, :mine]
    shift = reorder(jnp.concatenate([shift, shift], 0), here, mine)
    shift = jnp.concatenate([shift[q : q + 1] for q in range(rows)], 1)

    bin_sums = jnp.zeros((3 * bins, tiles * TILE), f32)
    for i in range(count // chunk):
        span = slice(i * chunk, (i + 1) * chunk)
        belongs = lanes_of((bins, chunk), 0) == bins_row[:, span]
        scaled = jnp.where(belongs, shift[:, span], 0.0)
        hi = scaled.astype(bf16)
        lo = (scaled - hi.astype(f32)).astype(bf16)
        onehot = jnp.where(belongs, 1.0, 0.0).astype(bf16)
        bin_sums = bin_sums + jnp.dot(
            jnp.concatenate([onehot, hi, lo], 0), weighted[span, :], preferred_element_type=f32
        )
    plain = bin_sums[:bins]
    slope_sum = bin_sums[bins : 2 * bins] + bin_sums[2 * bins :]
    for q in range(tiles):
        sums[q] = plain[:, q * TILE : (q + 1) * TILE]
        sums[tiles + q] = slope_sum[:, q * TILE : (q + 1) * TILE]
    total[...] = jnp.zeros_like(total)

    def step(j, carry):
        xt = table[row + 1 + j]
        xx = lanes_of((1, TILE), 1) + (xt * TILE).astype(f32)
        uu = lanes_of((TILE, TILE), 0)
        left, right = [], []
        for k in range(GROUP):
            at = row + 1 + groups + j * GROUP + k
            b, ut, s, c, base = block_of(table, trig, at, bins)
            u = lanes_of((1, TILE), 1) + base
            _, kz, kzd, z_factor, x_factor = row_weights(z0, depth, u, s, c, samples)
            first, second = [], []
            for r in range(4):
                direct = sums[r * ut_count + ut, pl.ds(b, 1), :]
                tilted = sums[tiles + r * ut_count + ut, pl.ds(b, 1), :]
                first.append(kz * direct + kzd * (tilted * z_factor))
                second.append(kz * (tilted * x_factor))
            left += [jnp.concatenate(first, 0), jnp.concatenate(second, 0)]
            right += [k.astype(bf16) for k in bump((xx - base * c) - uu * c)]
        left = jnp.concatenate(left, 1)
        hi = left.astype(bf16)
        lo = (left - hi.astype(f32)).astype(bf16)
        both = jnp.dot(
            jnp.concatenate([hi, lo], 0), jnp.concatenate(right, 0), preferred_element_type=f32
        )
        total[xt] = total[xt] + both[: 4 * depth] + both[4 * depth :]
        return carry

    lax.fori_loop(0, table[row], step, 0)
    tail = row + 1 + groups * (1 + GROUP)

    def edge(j, carry):
        left, right = [], []
        rest = jnp.zeros((TILE - edge_samples, TILE), f32)
        for k in range(EDGE_GROUP):
            b, _, s, c, _ = block_of(table, trig, tail + 1 + j * EDGE_GROUP + k, bins)
            u = lanes_of((1, TILE), 1)
            _, kz, kzd, z_factor, x_factor = row_weights(z0, 1, u, s, c, samples)
            direct = jnp.concatenate(
                [sums[r * ut_count, pl.ds(b, 1), :] for r in range(4)], 0
            )
            tilted = jnp.concatenate(
                [sums[tiles + r * ut_count, pl.ds(b, 1), :] for r in range(4)], 0
            )
            left += [kz * direct + (kzd * z_factor) * tilted, (kz * x_factor) * tilted]
            uu = lanes_of((edge_samples, TILE), 0)
            for part in bump(lanes_of((1, TILE), 1) - uu * c):
                right.append(jnp.concatenate([part, rest], 0).astype(bf16))
        left = jnp.concatenate(left, 1)
        hi = left.astype(bf16).astype(f32)
        split = jnp.concatenate([hi, left - hi], 0).astype(bf16)
        both = jnp.dot(split, jnp.concatenate(right, 0), preferred_element_type=f32)
        return carry + both[:4] + both[4:]

    extra = lax.fori_loop(0, table[tail], edge, jnp.zeros((4, TILE), f32))
    for xt in range(total.shape[0]):
        for r in range(4):
            out[:, r, xt * TILE : (xt + 1) * TILE] = total[xt, r * depth : r * depth + planes, :]
    out[0, :, :TILE] = out[0, :, :TILE] + extra


def swap(x, axis, size, distance):
    return lax.ppermute(x, axis, [(i, i ^ distance) for i in range(size)])


def local(volume, observed, ctf_table, ctf_class, bin_ids):
    slab, rows, columns = volume.shape
    mine, _, samples = observed.shape
    n_gz, n_dom = lax.axis_size("gz"), lax.axis_size("dom")
    devices = n_gz * n_dom
    bins = NB_DEV * n_dom
    planes = NZ // devices
    count = mine * devices
    width = rows * samples
    xt_count, ut_count = columns // TILE, samples // TILE
    ids = jnp.stack([ctf_class, bin_ids], 1).astype(bf16)
    ids = jnp.pad(ids, ((0, 0), (0, TILE - 2)))
    packed = jnp.concatenate([observed.reshape(mine, width), ids], 1)
    n_z = n_dom // 2
    above = lax.ppermute(volume[:1], "gz", [(i, i - 1) for i in range(1, n_gz)])
    column = jnp.concatenate(
        [packed] + [swap(packed, "dom", n_dom, 2 * k) for k in range(1, n_z)], 0
    )
    inner = lax.dynamic_slice_in_dim(
        volume, jnp.minimum((lax.axis_index("dom") + 1) * planes, slab - 1), 1, 0
    )
    above = jnp.where(lax.axis_index("dom") == n_dom - 1, above, inner)
    column, above = lax.optimization_barrier((column, above))
    planes_of = [column] + [swap(column, "gz", n_gz, j) for j in range(1, n_gz)]

    extract_plan, spread_plan, edge_samples, trig = make_plan(devices, bins, samples, columns)
    trig = jnp.asarray(trig)
    depth_in = round_up(planes + 1, 8)

    smem = pl.BlockSpec(memory_space=pltpu.SMEM)
    vmem = pl.BlockSpec(memory_space=pltpu.VMEM)
    hbm = pl.BlockSpec(memory_space=pl.ANY)
    params = pltpu.CompilerParams(vmem_limit_bytes=min(56, 19 + 37 * count // 4096) * 2**20)
    table, groups = extract_plan
    slope, pairs = pl.pallas_call(
        functools.partial(
            extract_kernel, groups, table.shape[1], samples, bins, planes, n_dom
        ),
        out_shape=[
            jax.ShapeDtypeStruct((2 * bins, width), bf16),
            jax.ShapeDtypeStruct((NCTF, 6 * bins), bf16),
        ],
        in_specs=[smem, smem, hbm, vmem, vmem],
        out_specs=[vmem, vmem],
        scratch_shapes=[
            pltpu.VMEM((depth_in, rows, columns), f32),
            pltpu.VMEM((xt_count, rows * depth_in, TILE), bf16),
            pltpu.VMEM((xt_count, rows * depth_in, TILE), bf16),
            pltpu.VMEM((bins * ut_count * 2 * rows, TILE), f32),
            pltpu.SemaphoreType.DMA((1,)),
        ],
        compiler_params=params,
        cost_estimate=pl.CostEstimate(flops=6 * 10**9, bytes_accessed=2**20, transcendentals=0),
        name="extract",
    )(jnp.asarray(table.reshape(-1)), trig, volume, above, ctf_table)

    planes_of, slope = lax.optimization_barrier((planes_of, slope))
    gathered = planes_of + [swap(part, "dom", n_dom, 1) for part in planes_of]
    weighted, parts, bins_row = pl.pallas_call(
        functools.partial(particle_kernel, width, mine, n_gz, n_dom),
        out_shape=[
            jax.ShapeDtypeStruct((count, width), bf16),
            jax.ShapeDtypeStruct((devices * 2 * count // TILE, TILE), f32),
            jax.ShapeDtypeStruct((1, count), f32),
        ],
        in_specs=[vmem] * (len(gathered) + 3),
        out_specs=[vmem] * 3,
        compiler_params=params,
        name="particles",
    )(*gathered, ctf_table, slope, pairs)

    parts = lax.all_to_all(parts, ("gz", "dom"), 0, 0, tiled=True)

    depth = round_up(planes, 8)
    table, groups = spread_plan
    pose, spread = pl.pallas_call(
        functools.partial(
            spread_kernel, groups, table.shape[1], planes, samples, edge_samples, mine, n_gz, n_dom
        ),
        out_shape=[
            jax.ShapeDtypeStruct((1, mine), f32),
            jax.ShapeDtypeStruct((planes, rows, columns), f32),
        ],
        in_specs=[smem, smem, vmem, vmem, vmem],
        out_specs=[vmem, vmem],
        scratch_shapes=[
            pltpu.VMEM((2 * width // TILE, bins, TILE), f32),
            pltpu.VMEM((xt_count, rows * depth, TILE), f32),
            pltpu.VMEM((count // TILE, TILE), f32),
        ],
        compiler_params=params,
        name="spread",
    )(jnp.asarray(table.reshape(-1)), trig, parts, bins_row, weighted)
    pose = pose.reshape(mine)
    return pose, spread


def solution(mesh):
    return jax.shard_map(
        local,
        mesh=mesh,
        in_specs=(
            P("gz", None, None),
            P(("gz", "dom"), None, None),
            P(),
            P(("gz", "dom")),
            P(("gz", "dom")),
        ),
        out_specs=(P(("gz", "dom")), P(("gz", "dom"), None, None)),
        check_vma=False,
    )
```

```python
import functools
import math

import jax
import jax.numpy as jnp
import numpy as np
from jax import lax
from jax.experimental import pallas as pl
from jax.experimental.pallas import tpu as pltpu
from jax.sharding import PartitionSpec as P

NZ = 768
NB_DEV = 8
NCTF = 32
ITERS = 3
EPS = 1e-05
TILE = 128
GROUP = 4
EDGE_GROUP = 8
CHUNK = 512
f32 = jnp.float32
bf16 = jnp.bfloat16
NT = (((1,), (1,)), ((), ()))


def round_up(n, m):
    return -(-n // m) * m


def make_plan(devices, bins, samples, columns):
    planes = NZ // devices
    middle = NZ // 2
    ut_count, xt_count = samples // TILE, columns // TILE
    theta = -0.5 * math.pi + math.pi * (np.arange(bins) + 0.5) / bins
    trig = np.concatenate([np.sin(theta), np.cos(theta)]).astype(np.float32)
    u = np.arange(samples)
    slack = 1e-3
    reach = 0
    plans = []
    for spread in (False, True):
        rows = []
        for device in range(devices):
            z0 = device * planes
            z1 = z0 + planes
            lists = [[] for _ in range(xt_count)]
            edge = []
            for b in range(bins):
                s, c = math.sin(theta[b]), math.cos(theta[b])
                centre = middle + u * s
                near = (centre > z0 - slack - (1 if spread else 0)) & (centre < z1 + slack)
                if spread:
                    near[0] = z0 - 1 < middle < z1
                else:
                    near[0] = z0 <= middle < z1 if s > 0 else z0 < middle <= z1
                if not near.any():
                    continue
                if spread and s < 0 and z0 == middle:
                    edge.append(b * 4)
                    reach = max(reach, int(u[near].max()) + 1)
                    continue
                for ut in range(ut_count):
                    hit = u[ut * TILE : (ut + 1) * TILE][near[ut * TILE : (ut + 1) * TILE]]
                    if hit.size == 0:
                        continue
                    first = max(0, int((hit.min() * c - 1.01) // TILE))
                    last = min(xt_count - 1, int((hit.max() * c + 1.01) // TILE))
                    for xt in range(first, last + 1):
                        lists[xt].append(b * 4 + ut)
            idle = (bins - 1 if z0 < middle else 0) * 4 + ut_count - 1
            tiles, codes = [], []
            for xt, entries in enumerate(lists):
                entries = entries + [idle] * (-len(entries) % GROUP)
                tiles += [xt] * (len(entries) // GROUP)
                codes += entries
            rows.append((tiles, codes, edge))
        groups = max(len(tiles) for tiles, _, _ in rows)
        start = 1 + groups * (1 + GROUP)
        table = np.zeros((devices, start + 1 + max(len(edge) for _, _, edge in rows)), np.int32)
        for device, (tiles, codes, edge) in enumerate(rows):
            table[device, 0] = len(tiles)
            table[device, 1 : 1 + len(tiles)] = tiles
            table[device, 1 + groups : 1 + groups + len(codes)] = codes
            table[device, start] = len(edge) // EDGE_GROUP
            table[device, start + 1 : start + 1 + len(edge)] = edge
        plans.append((table, groups))
    edge_samples = round_up(reach, 16)
    assert edge_samples <= TILE and (bins // 2) % EDGE_GROUP == 0
    return plans[0], plans[1], edge_samples, trig


def lanes_of(shape, axis):
    return lax.broadcasted_iota(jnp.int32, shape, axis).astype(f32)


def block_of(table, trig, at, bins):
    code = table[at]
    b = lax.shift_right_logical(code, 2)
    ut = lax.bitwise_and(code, 3)
    return b, ut, trig[b], trig[bins + b], (ut * TILE).astype(f32)


def split3(x):
    hi = x.astype(bf16)
    rest = x - hi.astype(f32)
    mid = rest.astype(bf16)
    return [hi, mid, (rest - mid.astype(f32)).astype(bf16)]


def bump(t):
    falloff = jnp.maximum(1.0 - t * t, 0.0)
    return falloff * falloff, t * falloff


def row_weights(z0, rows, u, s, c, samples):
    centre = 0.5 * NZ + u * s
    kz, kzd = bump((z0 + lanes_of((rows, TILE), 0)) - centre)
    return centre, kz, kzd, u * (c * (4.0 / samples)), u * (s * (-4.0 / samples))


def reorder(x, device, mine):
    lane = lax.broadcasted_iota(jnp.int32, x.shape, 1)
    rows = x.shape[0]
    size = mine
    bit = 0
    while size < rows // 2 * TILE:
        if size < TILE:
            moved = jnp.where(
                lax.bitwise_and(lane, size) != 0,
                pltpu.roll(x, size, 1),
                pltpu.roll(x, TILE - size, 1),
            )
        else:
            step = size // TILE
            moved = jnp.concatenate([x[r ^ step : (r ^ step) + 1] for r in range(rows)], 0)
        flag = lax.bitwise_and(lax.shift_right_logical(device, bit), 1)
        x = jnp.where(flag == 1, moved, x)
        size, bit = 2 * size, bit + 1
    return x


def position(n_gz, n_dom):
    dom = lax.axis_index("dom")
    n_z = n_dom // 2
    core, z = lax.bitwise_and(dom, 1), lax.shift_right_logical(dom, 1)
    return (core * n_gz + lax.axis_index("gz")) * n_z + z


def fetch(pairs, sems):
    copies = [pltpu.make_async_copy(a, b, sems.at[n]) for n, (a, b) in enumerate(pairs)]
    for copy in copies:
        copy.start()
    return copies


def pack_kernel(
    observed_hbm, classes_hbm, bins_hbm, volume, packed, plane, observed, classes, bin_ids, sems
):
    copies = fetch(
        [
            (observed_hbm, observed),
            (classes_hbm, classes),
            (bins_hbm, bin_ids),
            (volume.at[pl.ds(0, 1)], plane),
        ],
        sems,
    )
    for copy in copies:
        copy.wait()
    count, rows, samples = observed.shape
    values = observed[...].astype(f32)
    for r in range(rows):
        packed[:, r * samples : (r + 1) * samples] = values[:, r, :].astype(bf16)
    diagonal = lanes_of((count, count), 0) == lanes_of((count, count), 1)
    lane = lanes_of((count, TILE), 1)
    tail = jnp.zeros((count, TILE), f32)
    for n, ids in enumerate((classes, bin_ids)):
        column = jnp.where(diagonal, ids[...].astype(f32), 0.0)
        tail = jnp.where(lane == n, jnp.sum(column, axis=1, keepdims=True), tail)
    packed[:, rows * samples :] = tail.astype(bf16)


def extract_kernel(
    groups, length, samples, bins, planes, n_dom,
    table_hbm, trig_hbm, volume, above, ctf_hbm, slope, pairs, flat,
    table, trig, ctf, field, vhi, vlo, out, sems,
):
    depth = field.shape[0]
    xt_count = vhi.shape[0]
    ut_count = samples // TILE
    dom = lax.axis_index("dom")
    device = lax.axis_index("gz") * n_dom + dom
    row = device * length
    first = device * planes
    z0, z1 = first.astype(f32), (first + planes).astype(f32)

    copies = fetch(
        [
            (volume.at[pl.ds(dom * planes, planes)], field.at[pl.ds(0, planes)]),
            (table_hbm, table),
            (trig_hbm, trig),
            (ctf_hbm, ctf),
        ],
        sems,
    )
    field[planes] = above[0]
    for z in range(planes + 1, depth):
        field[z] = jnp.zeros(field.shape[1:], f32)
    out[...] = jnp.zeros_like(out)
    for copy in copies:
        copy.wait()
    for xt in range(xt_count):
        stacked = jnp.concatenate(
            [field[:, r, xt * TILE : (xt + 1) * TILE] for r in range(4)], 0
        )
        hi = stacked.astype(bf16)
        vhi[xt] = hi
        vlo[xt] = (stacked - hi.astype(f32)).astype(bf16)

    def step(j, carry):
        xt = table[row + 1 + j]
        hi_rows, lo_rows = vhi[xt], vlo[xt]
        xx = lanes_of((TILE, TILE), 0) + (xt * TILE).astype(f32)
        for k in range(GROUP):
            at = row + 1 + groups + j * GROUP + k
            b, ut, s, c, base = block_of(table, trig, at, bins)
            u = lanes_of((1, TILE), 1) + base
            centre, kz, kzd, z_factor, x_factor = row_weights(z0, depth, u, s, c, samples)
            below = s < 0.0
            place = centre * jnp.where(below, -1.0, 1.0)
            least, most = jnp.where(below, -z1, z0), jnp.where(below, -z0, z1)
            own = jnp.where((place >= least) & (place < most), 1.0, 0.0)
            z_factor, x_factor = z_factor * own, x_factor * own
            weights = jnp.concatenate(bump(xx - u * c), 1)
            whi = weights.astype(bf16)
            wlo = (weights - whi.astype(f32)).astype(bf16)
            sampled = (
                jnp.dot(hi_rows, whi, preferred_element_type=f32)
                + jnp.dot(lo_rows, whi, preferred_element_type=f32)
                + jnp.dot(hi_rows, wlo, preferred_element_type=f32)
            )
            leading, second = [], []
            for r in range(4):
                direct = sampled[r * depth : (r + 1) * depth, :TILE]
                tilted = sampled[r * depth : (r + 1) * depth, TILE:]
                leading.append(own * jnp.sum(direct * kz, axis=0, keepdims=True))
                second.append(
                    z_factor * jnp.sum(direct * kzd, axis=0, keepdims=True)
                    + x_factor * jnp.sum(tilted * kz, axis=0, keepdims=True)
                )
            span = pl.ds(pl.multiple_of((b * ut_count + ut) * 8, 8), 8)
            out[span, :] = out[span, :] + jnp.concatenate(leading + second, 0)
        return carry

    lax.fori_loop(0, table[row], step, 0)

    slope[...] = jnp.zeros_like(slope)
    square, mixed = [], []
    for y in range(2):
        for ut in range(ut_count):
            square_sum, mixed_sum = 0.0, 0.0
            for r in (y, 2 + y):
                direct = out[pl.ds(ut * 8 + r, bins, stride=ut_count * 8), :].astype(bf16).astype(f32)
                tilted = out[pl.ds(ut * 8 + 4 + r, bins, stride=ut_count * 8), :].astype(bf16)
                at = (r * ut_count + ut) * TILE
                slope[bins:, at : at + TILE] = tilted
                tilted = tilted.astype(f32)
                square_sum = square_sum + tilted * tilted
                mixed_sum = mixed_sum - direct * tilted
            square.append(square_sum)
            mixed.append(mixed_sum)
    moments = jnp.concatenate([jnp.concatenate(square, 1), jnp.concatenate(mixed, 1)], 0)
    contrast = jnp.concatenate([ctf[:, 0, :], ctf[:, 1, :]], 1)
    flat[...] = contrast
    product = lax.dot_general(
        contrast * contrast, moments, NT, precision=lax.Precision.HIGHEST, preferred_element_type=f32
    )
    pairs[...] = jnp.concatenate(split3(product), 1)


def particle_kernel(width, mine, n_gz, n_dom, *refs):
    blocks = refs[: 2 * n_gz]
    ctf, slope, pairs, weighted, parts, bins_row = refs[2 * n_gz :]
    size = blocks[0].shape[0]
    joined = max(1, CHUNK // size)
    both = slope.shape[0]
    bins = both // 2
    flat = ctf[...]
    ctf_hi = flat.astype(bf16)
    ctf_lo = (flat - ctf_hi.astype(f32)).astype(bf16)
    upper = jnp.where(lanes_of((8, both), 1) >= bins, 1.0, 0.0)
    select = jnp.where(lanes_of((8, both), 0) == upper, 1.0, 0.0).astype(bf16)
    select = jnp.concatenate([select] * 3, 1)
    slopes = slope[...]
    scalars = [[], []]

    for i in range(0, 2 * n_gz, joined):
        packed = jnp.concatenate([ref[...] for ref in blocks[i : i + joined]], 0)
        count = packed.shape[0]
        span = slice(i * size, i * size + count)
        ids = packed[:, width:]
        classes = ids[:, 0:1].astype(f32)
        onehot_class = jnp.where(lanes_of((count, NCTF), 1) == classes, 1.0, 0.0).astype(bf16)
        bin_of = ids[:, 1:2].astype(f32)
        lane = lanes_of((count, both), 1)
        chosen = (lane == bin_of) | (lane == bin_of + bins)
        contrast = jnp.dot(onehot_class, ctf_hi, preferred_element_type=f32) + jnp.dot(
            onehot_class, ctf_lo, preferred_element_type=f32
        )
        contrast = jnp.concatenate([contrast, contrast], 1)
        w = contrast * packed[:, :width].astype(f32)
        whi = w.astype(bf16)
        wlo = (w - whi.astype(f32)).astype(bf16)
        weighted[span, :] = whi
        along = lax.dot_general(whi, slopes, NT, preferred_element_type=f32) + lax.dot_general(
            wlo, slopes, NT, preferred_element_type=f32
        )
        tables = jnp.dot(onehot_class, pairs[...], preferred_element_type=f32)
        tables = tables[:, :both] + tables[:, both : 2 * both] + tables[:, 2 * both :]
        terms = jnp.concatenate(split3(jnp.where(chosen, along + tables, 0.0)), 1)
        rows = lax.dot_general(select, terms, NT, preferred_element_type=f32)
        for n in range(2):
            for q in range(count // TILE):
                scalars[n].append(rows[n : n + 1, q * TILE : (q + 1) * TILE])
        pick = jnp.where(lanes_of((8, TILE), 1) == 1.0, 1.0, 0.0).astype(bf16)
        bins_row[:, span] = lax.dot_general(pick, ids, NT, preferred_element_type=f32)[0:1]

    scalars = jnp.concatenate(scalars[0] + scalars[1], 0)
    scalars = reorder(scalars, position(n_gz, n_dom), mine)
    rows = scalars.shape[0]
    for n in range(parts.shape[0] // rows):
        parts[n * rows : (n + 1) * rows, :] = scalars


def spread_kernel(
    groups, length, planes, samples, edge_samples, mine, n_gz, n_dom,
    table, trig, parts, bins_row, weighted, pose, out, sums, total, poses,
):
    tiles, bins = sums.shape[0] // 2, sums.shape[1]
    ut_count = samples // TILE
    depth = total.shape[1] // 4
    count = bins_row.shape[1]
    chunk = min(CHUNK, count)
    device = lax.axis_index("gz") * n_dom + lax.axis_index("dom")
    row = device * length
    z0 = (device * planes).astype(f32)

    rows = count // TILE
    scalars = jnp.sum(parts[...].reshape(parts.shape[0] // (2 * rows), 2 * rows, TILE), axis=0)
    square, pull = scalars[:rows], scalars[rows:]
    curvature = square + EPS
    shift = jnp.zeros_like(square)
    for _ in range(ITERS):
        shift = shift + 0.5 * (pull - shift * square) / curvature
    here = position(n_gz, n_dom)
    poses[...] = shift * jnp.sqrt(curvature)
    first = here * mine
    line = poses[pl.ds(lax.div(first, TILE), 1), :]
    pose[...] = pltpu.roll(line, TILE - lax.rem(first, TILE), 1)[:, :mine]
    shift = reorder(jnp.concatenate([shift, shift], 0), here, mine)
    shift = jnp.concatenate([shift[q : q + 1] for q in range(rows)], 1)

    bin_sums = jnp.zeros((3 * bins, tiles * TILE), f32)
    for i in range(count // chunk):
        span = slice(i * chunk, (i + 1) * chunk)
        belongs = lanes_of((bins, chunk), 0) == bins_row[:, span]
        scaled = jnp.where(belongs, shift[:, span], 0.0)
        hi = scaled.astype(bf16)
        lo = (scaled - hi.astype(f32)).astype(bf16)
        onehot = jnp.where(belongs, 1.0, 0.0).astype(bf16)
        bin_sums = bin_sums + jnp.dot(
            jnp.concatenate([onehot, hi, lo], 0), weighted[span, :], preferred_element_type=f32
        )
    plain = bin_sums[:bins]
    slope_sum = bin_sums[bins : 2 * bins] + bin_sums[2 * bins :]
    for q in range(tiles):
        sums[q] = plain[:, q * TILE : (q + 1) * TILE]
        sums[tiles + q] = slope_sum[:, q * TILE : (q + 1) * TILE]
    total[...] = jnp.zeros_like(total)

    def step(j, carry):
        xt = table[row + 1 + j]
        xx = lanes_of((1, TILE), 1) + (xt * TILE).astype(f32)
        uu = lanes_of((TILE, TILE), 0)
        left, right = [], []
        for k in range(GROUP):
            at = row + 1 + groups + j * GROUP + k
            b, ut, s, c, base = block_of(table, trig, at, bins)
            u = lanes_of((1, TILE), 1) + base
            _, kz, kzd, z_factor, x_factor = row_weights(z0, depth, u, s, c, samples)
            first, second = [], []
            for r in range(4):
                direct = sums[r * ut_count + ut, pl.ds(b, 1), :]
                tilted = sums[tiles + r * ut_count + ut, pl.ds(b, 1), :]
                first.append(kz * direct + kzd * (tilted * z_factor))
                second.append(kz * (tilted * x_factor))
            left += [jnp.concatenate(first, 0), jnp.concatenate(second, 0)]
            right += [k.astype(bf16) for k in bump((xx - base * c) - uu * c)]
        left = jnp.concatenate(left, 1)
        hi = left.astype(bf16)
        lo = (left - hi.astype(f32)).astype(bf16)
        both = jnp.dot(
            jnp.concatenate([hi, lo], 0), jnp.concatenate(right, 0), preferred_element_type=f32
        )
        total[xt] = total[xt] + both[: 4 * depth] + both[4 * depth :]
        return carry

    lax.fori_loop(0, table[row], step, 0)
    tail = row + 1 + groups * (1 + GROUP)

    def edge(j, carry):
        left, right = [], []
        rest = jnp.zeros((TILE - edge_samples, TILE), f32)
        for k in range(EDGE_GROUP):
            b, _, s, c, _ = block_of(table, trig, tail + 1 + j * EDGE_GROUP + k, bins)
            u = lanes_of((1, TILE), 1)
            _, kz, kzd, z_factor, x_factor = row_weights(z0, 1, u, s, c, samples)
            direct = jnp.concatenate(
                [sums[r * ut_count, pl.ds(b, 1), :] for r in range(4)], 0
            )
            tilted = jnp.concatenate(
                [sums[tiles + r * ut_count, pl.ds(b, 1), :] for r in range(4)], 0
            )
            left += [kz * direct + (kzd * z_factor) * tilted, (kz * x_factor) * tilted]
            uu = lanes_of((edge_samples, TILE), 0)
            for part in bump(lanes_of((1, TILE), 1) - uu * c):
                right.append(jnp.concatenate([part, rest], 0).astype(bf16))
        left = jnp.concatenate(left, 1)
        hi = left.astype(bf16).astype(f32)
        split = jnp.concatenate([hi, left - hi], 0).astype(bf16)
        both = jnp.dot(split, jnp.concatenate(right, 0), preferred_element_type=f32)
        return carry + both[:4] + both[4:]

    extra = lax.fori_loop(0, table[tail], edge, jnp.zeros((4, TILE), f32))
    for xt in range(total.shape[0]):
        for r in range(4):
            out[:, r, xt * TILE : (xt + 1) * TILE] = total[xt, r * depth : r * depth + planes, :]
    out[0, :, :TILE] = out[0, :, :TILE] + extra


def swap(x, axis, size, distance):
    return lax.ppermute(x, axis, [(i, i ^ distance) for i in range(size)])


def local(volume, observed, ctf_table, ctf_class, bin_ids):
    slab, rows, columns = volume.shape
    mine, _, samples = observed.shape
    n_gz, n_dom = lax.axis_size("gz"), lax.axis_size("dom")
    devices = n_gz * n_dom
    bins = NB_DEV * n_dom
    planes = NZ // devices
    count = mine * devices
    width = rows * samples
    xt_count, ut_count = columns // TILE, samples // TILE
    smem = pl.BlockSpec(memory_space=pltpu.SMEM)
    vmem = pl.BlockSpec(memory_space=pltpu.VMEM)
    hbm = pl.BlockSpec(memory_space=pltpu.HBM)
    wide = pltpu.CompilerParams(vmem_limit_bytes=60 * 2**20)
    params = pltpu.CompilerParams(vmem_limit_bytes=min(56, 19 + 37 * count // 4096) * 2**20)
    packed, plane = pl.pallas_call(
        pack_kernel,
        out_shape=[
            jax.ShapeDtypeStruct((mine, width + TILE), bf16),
            jax.ShapeDtypeStruct((1, rows, columns), f32),
        ],
        in_specs=[hbm] * 4,
        out_specs=[vmem, vmem],
        scratch_shapes=[
            pltpu.VMEM(observed.shape, bf16),
            pltpu.VMEM((1, mine), jnp.int32),
            pltpu.VMEM((1, mine), jnp.int32),
            pltpu.SemaphoreType.DMA((4,)),
        ],
        compiler_params=wide,
        name="pack",
    )(observed, ctf_class.reshape(1, mine), bin_ids.reshape(1, mine), volume)

    n_z = n_dom // 2
    above = lax.ppermute(plane, "gz", [(i, i - 1) for i in range(1, n_gz)])
    column = jnp.concatenate(
        [packed] + [swap(packed, "dom", n_dom, 2 * k) for k in range(1, n_z)], 0
    )
    inner = lax.dynamic_slice_in_dim(
        volume, jnp.minimum((lax.axis_index("dom") + 1) * planes, slab - 1), 1, 0
    )
    above = jnp.where(lax.axis_index("dom") == n_dom - 1, above, inner)
    column, above = lax.optimization_barrier((column, above))
    planes_of = [column] + [swap(column, "gz", n_gz, j) for j in range(1, n_gz)]

    extract_plan, spread_plan, edge_samples, trig = make_plan(devices, bins, samples, columns)
    trig = jnp.asarray(trig)
    depth_in = round_up(planes + 1, 8)

    table, groups = extract_plan
    slope, pairs, flat_ctf = pl.pallas_call(
        functools.partial(
            extract_kernel, groups, table.shape[1], samples, bins, planes, n_dom
        ),
        out_shape=[
            jax.ShapeDtypeStruct((2 * bins, width), bf16),
            jax.ShapeDtypeStruct((NCTF, 6 * bins), bf16),
            jax.ShapeDtypeStruct((NCTF, width // 2), f32),
        ],
        in_specs=[hbm, hbm, hbm, vmem, hbm],
        out_specs=[vmem, vmem, vmem],
        scratch_shapes=[
            pltpu.SMEM((table.size,), jnp.int32),
            pltpu.SMEM(trig.shape, f32),
            pltpu.VMEM(ctf_table.shape, f32),
            pltpu.VMEM((depth_in, rows, columns), f32),
            pltpu.VMEM((xt_count, rows * depth_in, TILE), bf16),
            pltpu.VMEM((xt_count, rows * depth_in, TILE), bf16),
            pltpu.VMEM((bins * ut_count * 2 * rows, TILE), f32),
            pltpu.SemaphoreType.DMA((4,)),
        ],
        compiler_params=params,
        cost_estimate=pl.CostEstimate(flops=6 * 10**9, bytes_accessed=2**20, transcendentals=0),
        name="extract",
    )(jnp.asarray(table.reshape(-1)), trig, volume, above, ctf_table)

    planes_of, slope = lax.optimization_barrier((planes_of, slope))
    gathered = planes_of + [swap(part, "dom", n_dom, 1) for part in planes_of]
    weighted, parts, bins_row = pl.pallas_call(
        functools.partial(particle_kernel, width, mine, n_gz, n_dom),
        out_shape=[
            jax.ShapeDtypeStruct((count, width), bf16),
            jax.ShapeDtypeStruct((devices * 2 * count // TILE, TILE), f32),
            jax.ShapeDtypeStruct((1, count), f32),
        ],
        in_specs=[vmem] * (len(gathered) + 3),
        out_specs=[vmem] * 3,
        compiler_params=params,
        name="particles",
    )(*gathered, flat_ctf, slope, pairs)

    parts = lax.all_to_all(parts, ("gz", "dom"), 0, 0, tiled=True)

    depth = round_up(planes, 8)
    table, groups = spread_plan
    pose, spread = pl.pallas_call(
        functools.partial(
            spread_kernel, groups, table.shape[1], planes, samples, edge_samples, mine, n_gz, n_dom
        ),
        out_shape=[
            jax.ShapeDtypeStruct((1, mine), f32),
            jax.ShapeDtypeStruct((planes, rows, columns), f32),
        ],
        in_specs=[smem, smem, vmem, vmem, vmem],
        out_specs=[vmem, vmem],
        scratch_shapes=[
            pltpu.VMEM((2 * width // TILE, bins, TILE), f32),
            pltpu.VMEM((xt_count, rows * depth, TILE), f32),
            pltpu.VMEM((count // TILE, TILE), f32),
        ],
        compiler_params=params,
        name="spread",
    )(jnp.asarray(table.reshape(-1)), trig, parts, bins_row, weighted)
    pose = pose.reshape(mine)
    return pose, spread


def solution(mesh):
    return jax.shard_map(
        local,
        mesh=mesh,
        in_specs=(
            P("gz", None, None),
            P(("gz", "dom"), None, None),
            P(),
            P(("gz", "dom")),
            P(("gz", "dom")),
        ),
        out_specs=(P(("gz", "dom")), P(("gz", "dom"), None, None)),
        check_vma=False,
    )
```

```python
import functools
import math

import jax
import jax.numpy as jnp
import numpy as np
from jax import lax
from jax.experimental import pallas as pl
from jax.experimental.pallas import tpu as pltpu
from jax.sharding import PartitionSpec as P

NZ = 768
NB_DEV = 8
NCTF = 32
ITERS = 3
EPS = 1e-05
TILE = 128
GROUP = 4
EDGE_GROUP = 8
CHUNK = 512
f32 = jnp.float32
bf16 = jnp.bfloat16
NT = (((1,), (1,)), ((), ()))


def round_up(n, m):
    return -(-n // m) * m


def make_plan(devices, bins, samples, columns):
    planes = NZ // devices
    middle = NZ // 2
    ut_count, xt_count = samples // TILE, columns // TILE
    theta = -0.5 * math.pi + math.pi * (np.arange(bins) + 0.5) / bins
    trig = np.concatenate([np.sin(theta), np.cos(theta)]).astype(np.float32)
    u = np.arange(samples)
    slack = 1e-3
    reach = 0
    plans = []
    for spread in (False, True):
        rows = []
        for device in range(devices):
            z0 = device * planes
            z1 = z0 + planes
            lists = [[] for _ in range(xt_count)]
            edge = []
            for b in range(bins):
                s, c = math.sin(theta[b]), math.cos(theta[b])
                centre = middle + u * s
                near = (centre > z0 - slack - (1 if spread else 0)) & (centre < z1 + slack)
                if spread:
                    near[0] = z0 - 1 < middle < z1
                else:
                    near[0] = z0 <= middle < z1 if s > 0 else z0 < middle <= z1
                if not near.any():
                    continue
                if spread and s < 0 and z0 == middle:
                    edge.append(b * 4)
                    reach = max(reach, int(u[near].max()) + 1)
                    continue
                for ut in range(ut_count):
                    hit = u[ut * TILE : (ut + 1) * TILE][near[ut * TILE : (ut + 1) * TILE]]
                    if hit.size == 0:
                        continue
                    first = max(0, int((hit.min() * c - 1.01) // TILE))
                    last = min(xt_count - 1, int((hit.max() * c + 1.01) // TILE))
                    for xt in range(first, last + 1):
                        lists[xt].append(b * 4 + ut)
            idle = (bins - 1 if z0 < middle else 0) * 4 + ut_count - 1
            tiles, codes = [], []
            for xt, entries in enumerate(lists):
                entries = entries + [idle] * (-len(entries) % GROUP)
                tiles += [xt] * (len(entries) // GROUP)
                codes += entries
            rows.append((tiles, codes, edge))
        groups = max(len(tiles) for tiles, _, _ in rows)
        start = 1 + groups * (1 + GROUP)
        table = np.zeros((devices, start + 1 + max(len(edge) for _, _, edge in rows)), np.int32)
        for device, (tiles, codes, edge) in enumerate(rows):
            table[device, 0] = len(tiles)
            table[device, 1 : 1 + len(tiles)] = tiles
            table[device, 1 + groups : 1 + groups + len(codes)] = codes
            table[device, start] = len(edge) // EDGE_GROUP
            table[device, start + 1 : start + 1 + len(edge)] = edge
        plans.append((table, groups))
    edge_samples = round_up(reach, 16)
    assert edge_samples <= TILE and (bins // 2) % EDGE_GROUP == 0
    return plans[0], plans[1], edge_samples, trig


def lanes_of(shape, axis):
    return lax.broadcasted_iota(jnp.int32, shape, axis).astype(f32)


def block_of(table, trig, at, bins):
    code = table[at]
    b = lax.shift_right_logical(code, 2)
    ut = lax.bitwise_and(code, 3)
    return b, ut, trig[b], trig[bins + b], (ut * TILE).astype(f32)


def split3(x):
    hi = x.astype(bf16)
    rest = x - hi.astype(f32)
    mid = rest.astype(bf16)
    return [hi, mid, (rest - mid.astype(f32)).astype(bf16)]


def bump(t):
    falloff = jnp.maximum(1.0 - t * t, 0.0)
    return falloff * falloff, t * falloff


def row_weights(z0, rows, u, s, c, samples):
    centre = 0.5 * NZ + u * s
    kz, kzd = bump((z0 + lanes_of((rows, TILE), 0)) - centre)
    return centre, kz, kzd, u * (c * (4.0 / samples)), u * (s * (-4.0 / samples))


def reorder(x, device, mine):
    lane = lax.broadcasted_iota(jnp.int32, x.shape, 1)
    rows = x.shape[0]
    size = mine
    bit = 0
    while size < rows // 2 * TILE:
        if size < TILE:
            moved = jnp.where(
                lax.bitwise_and(lane, size) != 0,
                pltpu.roll(x, size, 1),
                pltpu.roll(x, TILE - size, 1),
            )
        else:
            step = size // TILE
            moved = jnp.concatenate([x[r ^ step : (r ^ step) + 1] for r in range(rows)], 0)
        flag = lax.bitwise_and(lax.shift_right_logical(device, bit), 1)
        x = jnp.where(flag == 1, moved, x)
        size, bit = 2 * size, bit + 1
    return x


def position(n_gz, n_dom):
    dom = lax.axis_index("dom")
    n_z = n_dom // 2
    core, z = lax.bitwise_and(dom, 1), lax.shift_right_logical(dom, 1)
    return (core * n_gz + lax.axis_index("gz")) * n_z + z


def fetch(pairs, sems):
    copies = [pltpu.make_async_copy(a, b, sems.at[n]) for n, (a, b) in enumerate(pairs)]
    for copy in copies:
        copy.start()
    return copies


def pack_kernel(
    observed_hbm, classes_hbm, bins_hbm, volume, packed, plane, observed, classes, bin_ids, sems
):
    copies = fetch(
        [
            (observed_hbm, observed),
            (classes_hbm, classes),
            (bins_hbm, bin_ids),
            (volume.at[pl.ds(0, 1)], plane),
        ],
        sems,
    )
    for copy in copies[:3]:
        copy.wait()
    count, rows, samples = observed.shape
    values = observed[...].astype(f32)
    for r in range(rows):
        packed[:, r * samples : (r + 1) * samples] = values[:, r, :].astype(bf16)
    diagonal = lanes_of((count, count), 0) == lanes_of((count, count), 1)
    lane = lanes_of((count, TILE), 1)
    tail = jnp.zeros((count, TILE), f32)
    for n, ids in enumerate((classes, bin_ids)):
        column = jnp.where(diagonal, ids[...].astype(f32), 0.0)
        tail = jnp.where(lane == n, jnp.sum(column, axis=1, keepdims=True), tail)
    packed[:, rows * samples :] = tail.astype(bf16)
    copies[3].wait()


def extract_kernel(
    groups, length, samples, bins, planes, n_dom,
    table_hbm, trig_hbm, volume, above, ctf_hbm, slope, pairs, flat,
    table, trig, ctf, field, vhi, vlo, out, sems,
):
    depth = field.shape[0]
    xt_count = vhi.shape[0]
    ut_count = samples // TILE
    dom = lax.axis_index("dom")
    device = lax.axis_index("gz") * n_dom + dom
    row = device * length
    first = device * planes
    z0, z1 = first.astype(f32), (first + planes).astype(f32)

    copies = fetch(
        [
            (volume.at[pl.ds(dom * planes, planes)], field.at[pl.ds(0, planes)]),
            (table_hbm, table),
            (trig_hbm, trig),
            (ctf_hbm, ctf),
        ],
        sems,
    )
    field[planes] = above[0]
    for z in range(planes + 1, depth):
        field[z] = jnp.zeros(field.shape[1:], f32)
    out[...] = jnp.zeros_like(out)
    for copy in copies:
        copy.wait()
    for xt in range(xt_count):
        stacked = jnp.concatenate(
            [field[:, r, xt * TILE : (xt + 1) * TILE] for r in range(4)], 0
        )
        hi = stacked.astype(bf16)
        vhi[xt] = hi
        vlo[xt] = (stacked - hi.astype(f32)).astype(bf16)

    def step(j, carry):
        xt = table[row + 1 + j]
        hi_rows, lo_rows = vhi[xt], vlo[xt]
        xx = lanes_of((TILE, TILE), 0) + (xt * TILE).astype(f32)
        for k in range(GROUP):
            at = row + 1 + groups + j * GROUP + k
            b, ut, s, c, base = block_of(table, trig, at, bins)
            u = lanes_of((1, TILE), 1) + base
            centre, kz, kzd, z_factor, x_factor = row_weights(z0, depth, u, s, c, samples)
            below = s < 0.0
            place = centre * jnp.where(below, -1.0, 1.0)
            least, most = jnp.where(below, -z1, z0), jnp.where(below, -z0, z1)
            own = jnp.where((place >= least) & (place < most), 1.0, 0.0)
            z_factor, x_factor = z_factor * own, x_factor * own
            weights = jnp.concatenate(bump(xx - u * c), 1)
            whi = weights.astype(bf16)
            wlo = (weights - whi.astype(f32)).astype(bf16)
            sampled = (
                jnp.dot(hi_rows, whi, preferred_element_type=f32)
                + jnp.dot(lo_rows, whi, preferred_element_type=f32)
                + jnp.dot(hi_rows, wlo, preferred_element_type=f32)
            )
            leading, second = [], []
            for r in range(4):
                direct = sampled[r * depth : (r + 1) * depth, :TILE]
                tilted = sampled[r * depth : (r + 1) * depth, TILE:]
                leading.append(own * jnp.sum(direct * kz, axis=0, keepdims=True))
                second.append(
                    z_factor * jnp.sum(direct * kzd, axis=0, keepdims=True)
                    + x_factor * jnp.sum(tilted * kz, axis=0, keepdims=True)
                )
            span = pl.ds(pl.multiple_of((b * ut_count + ut) * 8, 8), 8)
            out[span, :] = out[span, :] + jnp.concatenate(leading + second, 0)
        return carry

    lax.fori_loop(0, table[row], step, 0)

    slope[...] = jnp.zeros_like(slope)
    square, mixed = [], []
    for y in range(2):
        for ut in range(ut_count):
            square_sum, mixed_sum = 0.0, 0.0
            for r in (y, 2 + y):
                direct = out[pl.ds(ut * 8 + r, bins, stride=ut_count * 8), :].astype(bf16).astype(f32)
                tilted = out[pl.ds(ut * 8 + 4 + r, bins, stride=ut_count * 8), :].astype(bf16)
                at = (r * ut_count + ut) * TILE
                slope[bins:, at : at + TILE] = tilted
                tilted = tilted.astype(f32)
                square_sum = square_sum + tilted * tilted
                mixed_sum = mixed_sum - direct * tilted
            square.append(square_sum)
            mixed.append(mixed_sum)
    moments = jnp.concatenate([jnp.concatenate(square, 1), jnp.concatenate(mixed, 1)], 0)
    contrast = jnp.concatenate([ctf[:, 0, :], ctf[:, 1, :]], 1)
    flat[...] = contrast
    product = lax.dot_general(
        contrast * contrast, moments, NT, precision=lax.Precision.HIGHEST, preferred_element_type=f32
    )
    pairs[...] = jnp.concatenate(split3(product), 1)


def particle_kernel(width, mine, n_gz, n_dom, *refs):
    blocks = refs[: 2 * n_gz]
    ctf, slope, pairs, weighted, parts, bins_row = refs[2 * n_gz :]
    size = blocks[0].shape[0]
    joined = max(1, CHUNK // size)
    both = slope.shape[0]
    bins = both // 2
    flat = ctf[...]
    ctf_hi = flat.astype(bf16)
    ctf_lo = (flat - ctf_hi.astype(f32)).astype(bf16)
    upper = jnp.where(lanes_of((8, both), 1) >= bins, 1.0, 0.0)
    select = jnp.where(lanes_of((8, both), 0) == upper, 1.0, 0.0).astype(bf16)
    select = jnp.concatenate([select] * 3, 1)
    slopes = slope[...]
    scalars = [[], []]

    for i in range(0, 2 * n_gz, joined):
        packed = jnp.concatenate([ref[...] for ref in blocks[i : i + joined]], 0)
        count = packed.shape[0]
        span = slice(i * size, i * size + count)
        ids = packed[:, width:]
        classes = ids[:, 0:1].astype(f32)
        onehot_class = jnp.where(lanes_of((count, NCTF), 1) == classes, 1.0, 0.0).astype(bf16)
        bin_of = ids[:, 1:2].astype(f32)
        lane = lanes_of((count, both), 1)
        chosen = (lane == bin_of) | (lane == bin_of + bins)
        contrast = jnp.dot(onehot_class, ctf_hi, preferred_element_type=f32) + jnp.dot(
            onehot_class, ctf_lo, preferred_element_type=f32
        )
        contrast = jnp.concatenate([contrast, contrast], 1)
        w = contrast * packed[:, :width].astype(f32)
        whi = w.astype(bf16)
        wlo = (w - whi.astype(f32)).astype(bf16)
        weighted[span, :] = whi
        along = lax.dot_general(whi, slopes, NT, preferred_element_type=f32) + lax.dot_general(
            wlo, slopes, NT, preferred_element_type=f32
        )
        tables = jnp.dot(onehot_class, pairs[...], preferred_element_type=f32)
        tables = tables[:, :both] + tables[:, both : 2 * both] + tables[:, 2 * both :]
        terms = jnp.concatenate(split3(jnp.where(chosen, along + tables, 0.0)), 1)
        rows = lax.dot_general(select, terms, NT, preferred_element_type=f32)
        for n in range(2):
            for q in range(count // TILE):
                scalars[n].append(rows[n : n + 1, q * TILE : (q + 1) * TILE])
        pick = jnp.where(lanes_of((8, TILE), 1) == 1.0, 1.0, 0.0).astype(bf16)
        bins_row[:, span] = lax.dot_general(pick, ids, NT, preferred_element_type=f32)[0:1]

    scalars = jnp.concatenate(scalars[0] + scalars[1], 0)
    scalars = reorder(scalars, position(n_gz, n_dom), mine)
    rows = scalars.shape[0]
    for n in range(parts.shape[0] // rows):
        parts[n * rows : (n + 1) * rows, :] = scalars


def weight_kernel(groups, length, bins, planes, n_dom, edge_samples, table, trig, right, edges):
    device = lax.axis_index("gz") * n_dom + lax.axis_index("dom")
    row = device * length
    uu = lanes_of((TILE, TILE), 0)

    def step(j, carry):
        xx = lanes_of((1, TILE), 1) + (table[row + 1 + j] * TILE).astype(f32)
        for k in range(GROUP):
            at = row + 1 + groups + j * GROUP + k
            _, _, _, c, base = block_of(table, trig, at, bins)
            for n, part in enumerate(bump((xx - base * c) - uu * c)):
                right[j, (2 * k + n) * TILE : (2 * k + n + 1) * TILE, :] = part.astype(bf16)
        return carry

    lax.fori_loop(0, table[row], step, 0)
    tail = row + 1 + groups * (1 + GROUP)

    def edge(j, carry):
        for k in range(EDGE_GROUP):
            at = j * EDGE_GROUP + k
            _, _, _, c, _ = block_of(table, trig, tail + 1 + at, bins)
            uu = lanes_of((edge_samples, TILE), 0)
            for n, part in enumerate(bump(lanes_of((1, TILE), 1) - uu * c)):
                edges[at, n * edge_samples : (n + 1) * edge_samples, :] = part.astype(bf16)
        return carry

    lax.fori_loop(0, table[tail], edge, 0)


def spread_kernel(
    groups, length, planes, samples, edge_samples, mine, n_gz, n_dom,
    table, trig, right, edges, parts, bins_row, weighted, pose, out, sums, total, poses,
):
    tiles, bins = sums.shape[0] // 2, sums.shape[1]
    ut_count = samples // TILE
    depth = total.shape[1] // 4
    count = bins_row.shape[1]
    chunk = min(CHUNK, count)
    device = lax.axis_index("gz") * n_dom + lax.axis_index("dom")
    row = device * length
    z0 = (device * planes).astype(f32)

    rows = count // TILE
    scalars = jnp.sum(parts[...].reshape(parts.shape[0] // (2 * rows), 2 * rows, TILE), axis=0)
    square, pull = scalars[:rows], scalars[rows:]
    curvature = square + EPS
    shift = jnp.zeros_like(square)
    for _ in range(ITERS):
        shift = shift + 0.5 * (pull - shift * square) / curvature
    here = position(n_gz, n_dom)
    poses[...] = shift * jnp.sqrt(curvature)
    first = here * mine
    line = poses[pl.ds(lax.div(first, TILE), 1), :]
    pose[...] = pltpu.roll(line, TILE - lax.rem(first, TILE), 1)[:, :mine]
    shift = reorder(jnp.concatenate([shift, shift], 0), here, mine)
    shift = jnp.concatenate([shift[q : q + 1] for q in range(rows)], 1)

    bin_sums = jnp.zeros((3 * bins, tiles * TILE), f32)
    for i in range(count // chunk):
        span = slice(i * chunk, (i + 1) * chunk)
        belongs = lanes_of((bins, chunk), 0) == bins_row[:, span]
        scaled = jnp.where(belongs, shift[:, span], 0.0)
        hi = scaled.astype(bf16)
        lo = (scaled - hi.astype(f32)).astype(bf16)
        onehot = jnp.where(belongs, 1.0, 0.0).astype(bf16)
        bin_sums = bin_sums + jnp.dot(
            jnp.concatenate([onehot, hi, lo], 0), weighted[span, :], preferred_element_type=f32
        )
    plain = bin_sums[:bins]
    slope_sum = bin_sums[bins : 2 * bins] + bin_sums[2 * bins :]
    for q in range(tiles):
        sums[q] = plain[:, q * TILE : (q + 1) * TILE]
        sums[tiles + q] = slope_sum[:, q * TILE : (q + 1) * TILE]
    total[...] = jnp.zeros_like(total)

    def step(j, carry):
        xt = table[row + 1 + j]
        left = []
        for k in range(GROUP):
            at = row + 1 + groups + j * GROUP + k
            b, ut, s, c, base = block_of(table, trig, at, bins)
            u = lanes_of((1, TILE), 1) + base
            _, kz, kzd, z_factor, x_factor = row_weights(z0, depth, u, s, c, samples)
            first, second = [], []
            for r in range(4):
                direct = sums[r * ut_count + ut, pl.ds(b, 1), :]
                tilted = sums[tiles + r * ut_count + ut, pl.ds(b, 1), :]
                first.append(kz * direct + kzd * (tilted * z_factor))
                second.append(kz * (tilted * x_factor))
            left += [jnp.concatenate(first, 0), jnp.concatenate(second, 0)]
        left = jnp.concatenate(left, 1)
        hi = left.astype(bf16)
        lo = (left - hi.astype(f32)).astype(bf16)
        both = jnp.dot(
            jnp.concatenate([hi, lo], 0), right[j], preferred_element_type=f32
        )
        total[xt] = total[xt] + both[: 4 * depth] + both[4 * depth :]
        return carry

    lax.fori_loop(0, table[row], step, 0)
    tail = row + 1 + groups * (1 + GROUP)

    def edge(j, carry):
        left, below = [], []
        rest = jnp.zeros((TILE - edge_samples, TILE), bf16)
        for k in range(EDGE_GROUP):
            b, _, s, c, _ = block_of(table, trig, tail + 1 + j * EDGE_GROUP + k, bins)
            u = lanes_of((1, TILE), 1)
            _, kz, kzd, z_factor, x_factor = row_weights(z0, 1, u, s, c, samples)
            direct = jnp.concatenate(
                [sums[r * ut_count, pl.ds(b, 1), :] for r in range(4)], 0
            )
            tilted = jnp.concatenate(
                [sums[tiles + r * ut_count, pl.ds(b, 1), :] for r in range(4)], 0
            )
            left += [kz * direct + (kzd * z_factor) * tilted, (kz * x_factor) * tilted]
            part = edges[j * EDGE_GROUP + k]
            below += [part[:edge_samples], rest, part[edge_samples:], rest]
        left = jnp.concatenate(left, 1)
        hi = left.astype(bf16).astype(f32)
        split = jnp.concatenate([hi, left - hi], 0).astype(bf16)
        both = jnp.dot(split, jnp.concatenate(below, 0), preferred_element_type=f32)
        return carry + both[:4] + both[4:]

    extra = lax.fori_loop(0, table[tail], edge, jnp.zeros((4, TILE), f32))
    for xt in range(total.shape[0]):
        for r in range(4):
            out[:, r, xt * TILE : (xt + 1) * TILE] = total[xt, r * depth : r * depth + planes, :]
    out[0, :, :TILE] = out[0, :, :TILE] + extra


def swap(x, axis, size, distance):
    return lax.ppermute(x, axis, [(i, i ^ distance) for i in range(size)])


def local(volume, observed, ctf_table, ctf_class, bin_ids):
    slab, rows, columns = volume.shape
    mine, _, samples = observed.shape
    n_gz, n_dom = lax.axis_size("gz"), lax.axis_size("dom")
    devices = n_gz * n_dom
    bins = NB_DEV * n_dom
    planes = NZ // devices
    count = mine * devices
    width = rows * samples
    xt_count, ut_count = columns // TILE, samples // TILE
    smem = pl.BlockSpec(memory_space=pltpu.SMEM)
    vmem = pl.BlockSpec(memory_space=pltpu.VMEM)
    hbm = pl.BlockSpec(memory_space=pltpu.HBM)
    wide = pltpu.CompilerParams(vmem_limit_bytes=60 * 2**20)
    params = pltpu.CompilerParams(vmem_limit_bytes=min(56, 19 + 37 * count // 4096) * 2**20)
    extract_plan, spread_plan, edge_samples, trig = make_plan(devices, bins, samples, columns)
    trig = jnp.asarray(trig)
    packed, plane = pl.pallas_call(
        pack_kernel,
        out_shape=[
            jax.ShapeDtypeStruct((mine, width + TILE), bf16),
            jax.ShapeDtypeStruct((1, rows, columns), f32),
        ],
        in_specs=[hbm] * 4,
        out_specs=[vmem, vmem],
        scratch_shapes=[
            pltpu.VMEM(observed.shape, bf16),
            pltpu.VMEM((1, mine), jnp.int32),
            pltpu.VMEM((1, mine), jnp.int32),
            pltpu.SemaphoreType.DMA((4,)),
        ],
        compiler_params=wide,
        name="pack",
    )(observed, ctf_class.reshape(1, mine), bin_ids.reshape(1, mine), volume)

    n_z = n_dom // 2
    above = lax.ppermute(plane, "gz", [(i, i - 1) for i in range(1, n_gz)])
    column = jnp.concatenate(
        [packed] + [swap(packed, "dom", n_dom, 2 * k) for k in range(1, n_z)], 0
    )
    inner = lax.dynamic_slice_in_dim(
        volume, jnp.minimum((lax.axis_index("dom") + 1) * planes, slab - 1), 1, 0
    )
    above = jnp.where(lax.axis_index("dom") == n_dom - 1, above, inner)
    spread_table, spread_groups = spread_plan
    spread_table_flat = jnp.asarray(spread_table.reshape(-1))
    right, edges = pl.pallas_call(
        functools.partial(
            weight_kernel, spread_groups, spread_table.shape[1], bins, planes, n_dom, edge_samples
        ),
        out_shape=[
            jax.ShapeDtypeStruct((spread_groups, GROUP * 2 * TILE, TILE), bf16),
            jax.ShapeDtypeStruct((bins // 2, 2 * edge_samples, TILE), bf16),
        ],
        in_specs=[smem, smem],
        out_specs=[vmem, vmem],
        compiler_params=params,
        cost_estimate=pl.CostEstimate(flops=3 * 10**9, bytes_accessed=2**21, transcendentals=0),
        name="weights",
    )(spread_table_flat, trig)
    column, above, right, edges = lax.optimization_barrier((column, above, right, edges))
    planes_of = [column] + [swap(column, "gz", n_gz, j) for j in range(1, n_gz)]

    depth_in = round_up(planes + 1, 8)

    table, groups = extract_plan
    slope, pairs, flat_ctf = pl.pallas_call(
        functools.partial(
            extract_kernel, groups, table.shape[1], samples, bins, planes, n_dom
        ),
        out_shape=[
            jax.ShapeDtypeStruct((2 * bins, width), bf16),
            jax.ShapeDtypeStruct((NCTF, 6 * bins), bf16),
            jax.ShapeDtypeStruct((NCTF, width // 2), f32),
        ],
        in_specs=[hbm, hbm, hbm, vmem, hbm],
        out_specs=[vmem, vmem, vmem],
        scratch_shapes=[
            pltpu.SMEM((table.size,), jnp.int32),
            pltpu.SMEM(trig.shape, f32),
            pltpu.VMEM(ctf_table.shape, f32),
            pltpu.VMEM((depth_in, rows, columns), f32),
            pltpu.VMEM((xt_count, rows * depth_in, TILE), bf16),
            pltpu.VMEM((xt_count, rows * depth_in, TILE), bf16),
            pltpu.VMEM((bins * ut_count * 2 * rows, TILE), f32),
            pltpu.SemaphoreType.DMA((4,)),
        ],
        compiler_params=params,
        cost_estimate=pl.CostEstimate(flops=6 * 10**9, bytes_accessed=2**20, transcendentals=0),
        name="extract",
    )(jnp.asarray(table.reshape(-1)), trig, volume, above, ctf_table)

    planes_of, slope = lax.optimization_barrier((planes_of, slope))
    gathered = planes_of + [swap(part, "dom", n_dom, 1) for part in planes_of]
    weighted, parts, bins_row = pl.pallas_call(
        functools.partial(particle_kernel, width, mine, n_gz, n_dom),
        out_shape=[
            jax.ShapeDtypeStruct((count, width), bf16),
            jax.ShapeDtypeStruct((devices * 2 * count // TILE, TILE), f32),
            jax.ShapeDtypeStruct((1, count), f32),
        ],
        in_specs=[vmem] * (len(gathered) + 3),
        out_specs=[vmem] * 3,
        compiler_params=params,
        name="particles",
    )(*gathered, flat_ctf, slope, pairs)

    parts = lax.all_to_all(parts, ("gz", "dom"), 0, 0, tiled=True)

    depth = round_up(planes, 8)
    pose, spread = pl.pallas_call(
        functools.partial(
            spread_kernel, spread_groups, spread_table.shape[1], planes, samples, edge_samples, mine, n_gz, n_dom
        ),
        out_shape=[
            jax.ShapeDtypeStruct((1, mine), f32),
            jax.ShapeDtypeStruct((planes, rows, columns), f32),
        ],
        in_specs=[smem, smem] + [vmem] * 5,
        out_specs=[vmem, vmem],
        scratch_shapes=[
            pltpu.VMEM((2 * width // TILE, bins, TILE), f32),
            pltpu.VMEM((xt_count, rows * depth, TILE), f32),
            pltpu.VMEM((count // TILE, TILE), f32),
        ],
        compiler_params=params,
        name="spread",
    )(spread_table_flat, trig, right, edges, parts, bins_row, weighted)
    pose = pose.reshape(mine)
    return pose, spread


def solution(mesh):
    return jax.shard_map(
        local,
        mesh=mesh,
        in_specs=(
            P("gz", None, None),
            P(("gz", "dom"), None, None),
            P(),
            P(("gz", "dom")),
            P(("gz", "dom")),
        ),
        out_specs=(P(("gz", "dom")), P(("gz", "dom"), None, None)),
        check_vma=False,
    )
```

```python
import functools
import math

import jax
import jax.numpy as jnp
import numpy as np
from jax import lax
from jax.experimental import pallas as pl
from jax.experimental.pallas import tpu as pltpu
from jax.sharding import PartitionSpec as P

NZ = 768
NB_DEV = 8
NCTF = 32
ITERS = 3
EPS = 1e-05
TILE = 128
GROUP = 4
SPREAD_GROUP = 8
EDGE_GROUP = 8
CHUNK = 512
f32 = jnp.float32
bf16 = jnp.bfloat16
NT = (((1,), (1,)), ((), ()))


def round_up(n, m):
    return -(-n // m) * m


def make_plan(devices, bins, samples, columns):
    planes = NZ // devices
    middle = NZ // 2
    ut_count, xt_count = samples // TILE, columns // TILE
    theta = -0.5 * math.pi + math.pi * (np.arange(bins) + 0.5) / bins
    trig = np.concatenate([np.sin(theta), np.cos(theta)]).astype(np.float32)
    u = np.arange(samples)
    slack = 1e-3
    reach = 0
    plans = []
    for spread, size in ((False, GROUP), (True, SPREAD_GROUP)):
        rows = []
        for device in range(devices):
            z0 = device * planes
            z1 = z0 + planes
            lists = [[] for _ in range(xt_count)]
            edge = []
            for b in range(bins):
                s, c = math.sin(theta[b]), math.cos(theta[b])
                centre = middle + u * s
                near = (centre > z0 - slack - (1 if spread else 0)) & (centre < z1 + slack)
                if spread:
                    near[0] = z0 - 1 < middle < z1
                else:
                    near[0] = z0 <= middle < z1 if s > 0 else z0 < middle <= z1
                if not near.any():
                    continue
                if spread and s < 0 and z0 == middle:
                    edge.append(b * 4)
                    reach = max(reach, int(u[near].max()) + 1)
                    continue
                for ut in range(ut_count):
                    hit = u[ut * TILE : (ut + 1) * TILE][near[ut * TILE : (ut + 1) * TILE]]
                    if hit.size == 0:
                        continue
                    first = max(0, int((hit.min() * c - 1.01) // TILE))
                    last = min(xt_count - 1, int((hit.max() * c + 1.01) // TILE))
                    for xt in range(first, last + 1):
                        lists[xt].append(b * 4 + ut)
            idle = (bins - 1 if z0 < middle else 0) * 4 + ut_count - 1
            tiles, codes = [], []
            for xt, entries in enumerate(lists):
                entries = entries + [idle] * (-len(entries) % size)
                tiles += [xt] * (len(entries) // size)
                codes += entries
            rows.append((tiles, codes, edge))
        groups = max(len(tiles) for tiles, _, _ in rows)
        start = 1 + groups * (1 + size)
        table = np.zeros((devices, start + 1 + max(len(edge) for _, _, edge in rows)), np.int32)
        for device, (tiles, codes, edge) in enumerate(rows):
            table[device, 0] = len(tiles)
            table[device, 1 : 1 + len(tiles)] = tiles
            table[device, 1 + groups : 1 + groups + len(codes)] = codes
            table[device, start] = len(edge) // EDGE_GROUP
            table[device, start + 1 : start + 1 + len(edge)] = edge
        plans.append((table, groups))
    edge_samples = round_up(reach, 16)
    assert edge_samples <= TILE and (bins // 2) % EDGE_GROUP == 0
    return plans[0], plans[1], edge_samples, trig


def lanes_of(shape, axis):
    return lax.broadcasted_iota(jnp.int32, shape, axis).astype(f32)


def block_of(table, trig, at, bins):
    code = table[at]
    b = lax.shift_right_logical(code, 2)
    ut = lax.bitwise_and(code, 3)
    return b, ut, trig[b], trig[bins + b], (ut * TILE).astype(f32)


def split3(x):
    hi = x.astype(bf16)
    rest = x - hi.astype(f32)
    mid = rest.astype(bf16)
    return [hi, mid, (rest - mid.astype(f32)).astype(bf16)]


def bump(t):
    falloff = jnp.maximum(1.0 - t * t, 0.0)
    return falloff * falloff, t * falloff


def row_weights(z0, rows, u, s, c, samples):
    centre = 0.5 * NZ + u * s
    kz, kzd = bump((z0 + lanes_of((rows, TILE), 0)) - centre)
    return centre, kz, kzd, u * (c * (4.0 / samples)), u * (s * (-4.0 / samples))


def reorder(x, device, mine):
    lane = lax.broadcasted_iota(jnp.int32, x.shape, 1)
    rows = x.shape[0]
    size = mine
    bit = 0
    while size < rows // 2 * TILE:
        if size < TILE:
            moved = jnp.where(
                lax.bitwise_and(lane, size) != 0,
                pltpu.roll(x, size, 1),
                pltpu.roll(x, TILE - size, 1),
            )
        else:
            step = size // TILE
            moved = jnp.concatenate([x[r ^ step : (r ^ step) + 1] for r in range(rows)], 0)
        flag = lax.bitwise_and(lax.shift_right_logical(device, bit), 1)
        x = jnp.where(flag == 1, moved, x)
        size, bit = 2 * size, bit + 1
    return x


def position(n_gz, n_dom):
    dom = lax.axis_index("dom")
    n_z = n_dom // 2
    core, z = lax.bitwise_and(dom, 1), lax.shift_right_logical(dom, 1)
    return (core * n_gz + lax.axis_index("gz")) * n_z + z


def fetch(pairs, sems):
    copies = [pltpu.make_async_copy(a, b, sems.at[n]) for n, (a, b) in enumerate(pairs)]
    for copy in copies:
        copy.start()
    return copies


def pack_kernel(
    observed_hbm, classes_hbm, bins_hbm, volume, packed, plane, observed, classes, bin_ids, sems
):
    copies = fetch(
        [
            (observed_hbm, observed),
            (classes_hbm, classes),
            (bins_hbm, bin_ids),
            (volume.at[pl.ds(0, 1)], plane),
        ],
        sems,
    )
    for copy in copies[:3]:
        copy.wait()
    count, rows, samples = observed.shape
    values = observed[...].astype(f32)
    for r in range(rows):
        packed[:, r * samples : (r + 1) * samples] = values[:, r, :].astype(bf16)
    diagonal = lanes_of((count, count), 0) == lanes_of((count, count), 1)
    lane = lanes_of((count, TILE), 1)
    tail = jnp.zeros((count, TILE), f32)
    for n, ids in enumerate((classes, bin_ids)):
        column = jnp.where(diagonal, ids[...].astype(f32), 0.0)
        tail = jnp.where(lane == n, jnp.sum(column, axis=1, keepdims=True), tail)
    packed[:, rows * samples :] = tail.astype(bf16)
    copies[3].wait()


def extract_kernel(
    groups, length, samples, bins, planes, n_dom,
    table_hbm, trig_hbm, field, ctf_hbm, slope, pairs, flat,
    table, trig, ctf, vhi, vlo, out, sems,
):
    depth = field.shape[0]
    xt_count = vhi.shape[0]
    ut_count = samples // TILE
    device = lax.axis_index("gz") * n_dom + lax.axis_index("dom")
    row = device * length
    first = device * planes
    z0, z1 = first.astype(f32), (first + planes).astype(f32)

    copies = fetch(
        [
            (table_hbm, table),
            (trig_hbm, trig),
            (ctf_hbm, ctf),
        ],
        sems,
    )
    out[...] = jnp.zeros_like(out)
    for copy in copies:
        copy.wait()
    for xt in range(xt_count):
        stacked = jnp.concatenate(
            [field[:, r, xt * TILE : (xt + 1) * TILE] for r in range(4)], 0
        )
        hi = stacked.astype(bf16)
        vhi[xt] = hi
        vlo[xt] = (stacked - hi.astype(f32)).astype(bf16)

    def step(j, carry):
        xt = table[row + 1 + j]
        hi_rows, lo_rows = vhi[xt], vlo[xt]
        xx = lanes_of((TILE, TILE), 0) + (xt * TILE).astype(f32)
        for k in range(GROUP):
            at = row + 1 + groups + j * GROUP + k
            b, ut, s, c, base = block_of(table, trig, at, bins)
            u = lanes_of((1, TILE), 1) + base
            centre, kz, kzd, z_factor, x_factor = row_weights(z0, depth, u, s, c, samples)
            below = s < 0.0
            place = centre * jnp.where(below, -1.0, 1.0)
            least, most = jnp.where(below, -z1, z0), jnp.where(below, -z0, z1)
            own = jnp.where((place >= least) & (place < most), 1.0, 0.0)
            z_factor, x_factor = z_factor * own, x_factor * own
            weights = jnp.concatenate(bump(xx - u * c), 1)
            whi = weights.astype(bf16)
            wlo = (weights - whi.astype(f32)).astype(bf16)
            sampled = (
                jnp.dot(hi_rows, whi, preferred_element_type=f32)
                + jnp.dot(lo_rows, whi, preferred_element_type=f32)
                + jnp.dot(hi_rows, wlo, preferred_element_type=f32)
            )
            leading, second = [], []
            for r in range(4):
                direct = sampled[r * depth : (r + 1) * depth, :TILE]
                tilted = sampled[r * depth : (r + 1) * depth, TILE:]
                leading.append(own * jnp.sum(direct * kz, axis=0, keepdims=True))
                second.append(
                    z_factor * jnp.sum(direct * kzd, axis=0, keepdims=True)
                    + x_factor * jnp.sum(tilted * kz, axis=0, keepdims=True)
                )
            span = pl.ds(pl.multiple_of((b * ut_count + ut) * 8, 8), 8)
            out[span, :] = out[span, :] + jnp.concatenate(leading + second, 0)
        return carry

    lax.fori_loop(0, table[row], step, 0)

    slope[...] = jnp.zeros_like(slope)
    square, mixed = [], []
    for y in range(2):
        for ut in range(ut_count):
            square_sum, mixed_sum = 0.0, 0.0
            for r in (y, 2 + y):
                direct = out[pl.ds(ut * 8 + r, bins, stride=ut_count * 8), :].astype(bf16).astype(f32)
                tilted = out[pl.ds(ut * 8 + 4 + r, bins, stride=ut_count * 8), :].astype(bf16)
                at = (r * ut_count + ut) * TILE
                slope[bins:, at : at + TILE] = tilted
                tilted = tilted.astype(f32)
                square_sum = square_sum + tilted * tilted
                mixed_sum = mixed_sum - direct * tilted
            square.append(square_sum)
            mixed.append(mixed_sum)
    moments = jnp.concatenate([jnp.concatenate(square, 1), jnp.concatenate(mixed, 1)], 0)
    contrast = jnp.concatenate([ctf[:, 0, :], ctf[:, 1, :]], 1)
    flat[...] = contrast
    product = lax.dot_general(
        contrast * contrast, moments, NT, precision=lax.Precision.HIGHEST, preferred_element_type=f32
    )
    pairs[...] = jnp.concatenate(split3(product), 1)


def particle_kernel(width, mine, n_gz, n_dom, *refs):
    blocks = refs[: 2 * n_gz]
    ctf, slope, pairs, weighted, parts, bins_row = refs[2 * n_gz :]
    size = blocks[0].shape[0]
    joined = max(1, CHUNK // size)
    both = slope.shape[0]
    bins = both // 2
    flat = ctf[...]
    ctf_hi = flat.astype(bf16)
    ctf_lo = (flat - ctf_hi.astype(f32)).astype(bf16)
    upper = jnp.where(lanes_of((8, both), 1) >= bins, 1.0, 0.0)
    select = jnp.where(lanes_of((8, both), 0) == upper, 1.0, 0.0).astype(bf16)
    select = jnp.concatenate([select] * 3, 1)
    slopes = slope[...]
    scalars = [[], []]

    for i in range(0, 2 * n_gz, joined):
        packed = jnp.concatenate([ref[...] for ref in blocks[i : i + joined]], 0)
        count = packed.shape[0]
        span = slice(i * size, i * size + count)
        ids = packed[:, width:]
        classes = ids[:, 0:1].astype(f32)
        onehot_class = jnp.where(lanes_of((count, NCTF), 1) == classes, 1.0, 0.0).astype(bf16)
        bin_of = ids[:, 1:2].astype(f32)
        lane = lanes_of((count, both), 1)
        chosen = (lane == bin_of) | (lane == bin_of + bins)
        contrast = jnp.dot(onehot_class, ctf_hi, preferred_element_type=f32) + jnp.dot(
            onehot_class, ctf_lo, preferred_element_type=f32
        )
        contrast = jnp.concatenate([contrast, contrast], 1)
        w = contrast * packed[:, :width].astype(f32)
        whi = w.astype(bf16)
        wlo = (w - whi.astype(f32)).astype(bf16)
        weighted[span, :] = whi
        along = lax.dot_general(whi, slopes, NT, preferred_element_type=f32) + lax.dot_general(
            wlo, slopes, NT, preferred_element_type=f32
        )
        tables = jnp.dot(onehot_class, pairs[...], preferred_element_type=f32)
        tables = tables[:, :both] + tables[:, both : 2 * both] + tables[:, 2 * both :]
        terms = jnp.concatenate(split3(jnp.where(chosen, along + tables, 0.0)), 1)
        rows = lax.dot_general(select, terms, NT, preferred_element_type=f32)
        for n in range(2):
            for q in range(count // TILE):
                scalars[n].append(rows[n : n + 1, q * TILE : (q + 1) * TILE])
        pick = jnp.where(lanes_of((8, TILE), 1) == 1.0, 1.0, 0.0).astype(bf16)
        bins_row[:, span] = lax.dot_general(pick, ids, NT, preferred_element_type=f32)[0:1]

    scalars = jnp.concatenate(scalars[0] + scalars[1], 0)
    scalars = reorder(scalars, position(n_gz, n_dom), mine)
    rows = scalars.shape[0]
    for n in range(parts.shape[0] // rows):
        parts[n * rows : (n + 1) * rows, :] = scalars


def weight_kernel(groups, length, bins, planes, n_dom, edge_samples, table, trig, right, edges):
    device = lax.axis_index("gz") * n_dom + lax.axis_index("dom")
    row = device * length
    uu = lanes_of((TILE, TILE), 0)

    def step(j, carry):
        xx = lanes_of((1, TILE), 1) + (table[row + 1 + j] * TILE).astype(f32)
        for k in range(SPREAD_GROUP):
            at = row + 1 + groups + j * SPREAD_GROUP + k
            _, _, _, c, base = block_of(table, trig, at, bins)
            for n, part in enumerate(bump((xx - base * c) - uu * c)):
                right[j, (2 * k + n) * TILE : (2 * k + n + 1) * TILE, :] = part.astype(bf16)
        return carry

    lax.fori_loop(0, table[row], step, 0)
    tail = row + 1 + groups * (1 + SPREAD_GROUP)

    def edge(j, carry):
        for k in range(EDGE_GROUP):
            at = j * EDGE_GROUP + k
            _, _, _, c, _ = block_of(table, trig, tail + 1 + at, bins)
            uu = lanes_of((edge_samples, TILE), 0)
            for n, part in enumerate(bump(lanes_of((1, TILE), 1) - uu * c)):
                edges[at, n * edge_samples : (n + 1) * edge_samples, :] = part.astype(bf16)
        return carry

    lax.fori_loop(0, table[tail], edge, 0)


def spread_kernel(
    groups, length, planes, samples, edge_samples, mine, n_gz, n_dom,
    table, trig, right, edges, parts, bins_row, weighted, pose, out, sums, total, poses,
):
    tiles, bins = sums.shape[0] // 2, sums.shape[1]
    ut_count = samples // TILE
    depth = total.shape[1] // 4
    count = bins_row.shape[1]
    chunk = min(CHUNK, count)
    device = lax.axis_index("gz") * n_dom + lax.axis_index("dom")
    row = device * length
    z0 = (device * planes).astype(f32)

    rows = count // TILE
    scalars = jnp.sum(parts[...].reshape(parts.shape[0] // (2 * rows), 2 * rows, TILE), axis=0)
    square, pull = scalars[:rows], scalars[rows:]
    curvature = square + EPS
    shift = jnp.zeros_like(square)
    for _ in range(ITERS):
        shift = shift + 0.5 * (pull - shift * square) / curvature
    here = position(n_gz, n_dom)
    poses[...] = shift * jnp.sqrt(curvature)
    first = here * mine
    line = poses[pl.ds(lax.div(first, TILE), 1), :]
    pose[...] = pltpu.roll(line, TILE - lax.rem(first, TILE), 1)[:, :mine]
    shift = reorder(jnp.concatenate([shift, shift], 0), here, mine)
    shift = jnp.concatenate([shift[q : q + 1] for q in range(rows)], 1)

    bin_sums = jnp.zeros((3 * bins, tiles * TILE), f32)
    for i in range(count // chunk):
        span = slice(i * chunk, (i + 1) * chunk)
        belongs = lanes_of((bins, chunk), 0) == bins_row[:, span]
        scaled = jnp.where(belongs, shift[:, span], 0.0)
        hi = scaled.astype(bf16)
        lo = (scaled - hi.astype(f32)).astype(bf16)
        onehot = jnp.where(belongs, 1.0, 0.0).astype(bf16)
        bin_sums = bin_sums + jnp.dot(
            jnp.concatenate([onehot, hi, lo], 0), weighted[span, :], preferred_element_type=f32
        )
    plain = bin_sums[:bins]
    slope_sum = bin_sums[bins : 2 * bins] + bin_sums[2 * bins :]
    for q in range(tiles):
        sums[q] = plain[:, q * TILE : (q + 1) * TILE]
        sums[tiles + q] = slope_sum[:, q * TILE : (q + 1) * TILE]
    total[...] = jnp.zeros_like(total)

    def step(j, carry):
        xt = table[row + 1 + j]
        left = []
        for k in range(SPREAD_GROUP):
            at = row + 1 + groups + j * SPREAD_GROUP + k
            b, ut, s, c, base = block_of(table, trig, at, bins)
            u = lanes_of((1, TILE), 1) + base
            _, kz, kzd, z_factor, x_factor = row_weights(z0, depth, u, s, c, samples)
            first, second = [], []
            for r in range(4):
                direct = sums[r * ut_count + ut, pl.ds(b, 1), :]
                tilted = sums[tiles + r * ut_count + ut, pl.ds(b, 1), :]
                first.append(kz * direct + kzd * (tilted * z_factor))
                second.append(kz * (tilted * x_factor))
            left += [jnp.concatenate(first, 0), jnp.concatenate(second, 0)]
        left = jnp.concatenate(left, 1)
        hi = left.astype(bf16)
        lo = (left - hi.astype(f32)).astype(bf16)
        both = jnp.dot(
            jnp.concatenate([hi, lo], 0), right[j], preferred_element_type=f32
        )
        total[xt] = total[xt] + both[: 4 * depth] + both[4 * depth :]
        return carry

    lax.fori_loop(0, table[row], step, 0)
    tail = row + 1 + groups * (1 + SPREAD_GROUP)

    def edge(j, carry):
        left, below = [], []
        rest = jnp.zeros((TILE - edge_samples, TILE), bf16)
        for k in range(EDGE_GROUP):
            b, _, s, c, _ = block_of(table, trig, tail + 1 + j * EDGE_GROUP + k, bins)
            u = lanes_of((1, TILE), 1)
            _, kz, kzd, z_factor, x_factor = row_weights(z0, 1, u, s, c, samples)
            direct = jnp.concatenate(
                [sums[r * ut_count, pl.ds(b, 1), :] for r in range(4)], 0
            )
            tilted = jnp.concatenate(
                [sums[tiles + r * ut_count, pl.ds(b, 1), :] for r in range(4)], 0
            )
            left += [kz * direct + (kzd * z_factor) * tilted, (kz * x_factor) * tilted]
            part = edges[j * EDGE_GROUP + k]
            below += [part[:edge_samples], rest, part[edge_samples:], rest]
        left = jnp.concatenate(left, 1)
        hi = left.astype(bf16).astype(f32)
        split = jnp.concatenate([hi, left - hi], 0).astype(bf16)
        both = jnp.dot(split, jnp.concatenate(below, 0), preferred_element_type=f32)
        return carry + both[:4] + both[4:]

    extra = lax.fori_loop(0, table[tail], edge, jnp.zeros((4, TILE), f32))
    for xt in range(total.shape[0]):
        for r in range(4):
            out[:, r, xt * TILE : (xt + 1) * TILE] = total[xt, r * depth : r * depth + planes, :]
    out[0, :, :TILE] = out[0, :, :TILE] + extra


def swap(x, axis, size, distance):
    return lax.ppermute(x, axis, [(i, i ^ distance) for i in range(size)])


def local(volume, observed, ctf_table, ctf_class, bin_ids):
    slab, rows, columns = volume.shape
    mine, _, samples = observed.shape
    n_gz, n_dom = lax.axis_size("gz"), lax.axis_size("dom")
    devices = n_gz * n_dom
    bins = NB_DEV * n_dom
    planes = NZ // devices
    count = mine * devices
    width = rows * samples
    xt_count, ut_count = columns // TILE, samples // TILE
    smem = pl.BlockSpec(memory_space=pltpu.SMEM)
    vmem = pl.BlockSpec(memory_space=pltpu.VMEM)
    hbm = pl.BlockSpec(memory_space=pltpu.HBM)
    wide = pltpu.CompilerParams(vmem_limit_bytes=60 * 2**20)
    params = pltpu.CompilerParams(vmem_limit_bytes=min(56, 19 + 37 * count // 4096) * 2**20)
    extract_plan, spread_plan, edge_samples, trig = make_plan(devices, bins, samples, columns)
    trig = jnp.asarray(trig)
    packed, plane = pl.pallas_call(
        pack_kernel,
        out_shape=[
            jax.ShapeDtypeStruct((mine, width + TILE), bf16),
            jax.ShapeDtypeStruct((1, rows, columns), f32),
        ],
        in_specs=[hbm] * 4,
        out_specs=[vmem, vmem],
        scratch_shapes=[
            pltpu.VMEM(observed.shape, bf16),
            pltpu.VMEM((1, mine), jnp.int32),
            pltpu.VMEM((1, mine), jnp.int32),
            pltpu.SemaphoreType.DMA((4,)),
        ],
        compiler_params=wide,
        name="pack",
    )(observed, ctf_class.reshape(1, mine), bin_ids.reshape(1, mine), volume)

    n_z = n_dom // 2
    above = lax.ppermute(plane, "gz", [(i, i - 1) for i in range(1, n_gz)])
    column = jnp.concatenate(
        [packed] + [swap(packed, "dom", n_dom, 2 * k) for k in range(1, n_z)], 0
    )
    dom = lax.axis_index("dom")
    own = lax.dynamic_slice_in_dim(volume, dom * planes, planes, 0)
    inner = lax.dynamic_slice_in_dim(volume, jnp.minimum((dom + 1) * planes, slab - 1), 1, 0)
    halo = jnp.where(dom == n_dom - 1, above, inner)
    depth_in = round_up(planes + 1, 8)
    field = jnp.concatenate([own, halo, jnp.zeros((depth_in - planes - 1, rows, columns), f32)], 0)
    spread_table, spread_groups = spread_plan
    spread_table_flat = jnp.asarray(spread_table.reshape(-1))
    right, edges = pl.pallas_call(
        functools.partial(
            weight_kernel, spread_groups, spread_table.shape[1], bins, planes, n_dom, edge_samples
        ),
        out_shape=[
            jax.ShapeDtypeStruct((spread_groups, SPREAD_GROUP * 2 * TILE, TILE), bf16),
            jax.ShapeDtypeStruct((bins // 2, 2 * edge_samples, TILE), bf16),
        ],
        in_specs=[smem, smem],
        out_specs=[vmem, vmem],
        compiler_params=params,
        cost_estimate=pl.CostEstimate(flops=3 * 10**9, bytes_accessed=2**21, transcendentals=0),
        name="weights",
    )(spread_table_flat, trig)
    column, field, right, edges = lax.optimization_barrier((column, field, right, edges))
    planes_of = [column] + [swap(column, "gz", n_gz, j) for j in range(1, n_gz)]


    table, groups = extract_plan
    slope, pairs, flat_ctf = pl.pallas_call(
        functools.partial(
            extract_kernel, groups, table.shape[1], samples, bins, planes, n_dom
        ),
        out_shape=[
            jax.ShapeDtypeStruct((2 * bins, width), bf16),
            jax.ShapeDtypeStruct((NCTF, 6 * bins), bf16),
            jax.ShapeDtypeStruct((NCTF, width // 2), f32),
        ],
        in_specs=[hbm, hbm, vmem, hbm],
        out_specs=[vmem, vmem, vmem],
        scratch_shapes=[
            pltpu.SMEM((table.size,), jnp.int32),
            pltpu.SMEM(trig.shape, f32),
            pltpu.VMEM(ctf_table.shape, f32),
            pltpu.VMEM((xt_count, rows * depth_in, TILE), bf16),
            pltpu.VMEM((xt_count, rows * depth_in, TILE), bf16),
            pltpu.VMEM((bins * ut_count * 2 * rows, TILE), f32),
            pltpu.SemaphoreType.DMA((3,)),
        ],
        compiler_params=params,
        cost_estimate=pl.CostEstimate(flops=6 * 10**9, bytes_accessed=2**20, transcendentals=0),
        name="extract",
    )(jnp.asarray(table.reshape(-1)), trig, field, ctf_table)

    planes_of, slope = lax.optimization_barrier((planes_of, slope))
    gathered = planes_of + [swap(part, "dom", n_dom, 1) for part in planes_of]
    weighted, parts, bins_row = pl.pallas_call(
        functools.partial(particle_kernel, width, mine, n_gz, n_dom),
        out_shape=[
            jax.ShapeDtypeStruct((count, width), bf16),
            jax.ShapeDtypeStruct((devices * 2 * count // TILE, TILE), f32),
            jax.ShapeDtypeStruct((1, count), f32),
        ],
        in_specs=[vmem] * (len(gathered) + 3),
        out_specs=[vmem] * 3,
        compiler_params=params,
        name="particles",
    )(*gathered, flat_ctf, slope, pairs)

    parts = lax.all_to_all(parts, ("gz", "dom"), 0, 0, tiled=True)

    depth = round_up(planes, 8)
    pose, spread = pl.pallas_call(
        functools.partial(
            spread_kernel, spread_groups, spread_table.shape[1], planes, samples, edge_samples, mine, n_gz, n_dom
        ),
        out_shape=[
            jax.ShapeDtypeStruct((1, mine), f32),
            jax.ShapeDtypeStruct((planes, rows, columns), f32),
        ],
        in_specs=[smem, smem] + [vmem] * 5,
        out_specs=[vmem, vmem],
        scratch_shapes=[
            pltpu.VMEM((2 * width // TILE, bins, TILE), f32),
            pltpu.VMEM((xt_count, rows * depth, TILE), f32),
            pltpu.VMEM((count // TILE, TILE), f32),
        ],
        compiler_params=params,
        name="spread",
    )(spread_table_flat, trig, right, edges, parts, bins_row, weighted)
    pose = pose.reshape(mine)
    return pose, spread


def solution(mesh):
    return jax.shard_map(
        local,
        mesh=mesh,
        in_specs=(
            P("gz", None, None),
            P(("gz", "dom"), None, None),
            P(),
            P(("gz", "dom")),
            P(("gz", "dom")),
        ),
        out_specs=(P(("gz", "dom")), P(("gz", "dom"), None, None)),
        check_vma=False,
    )
```

```python
import functools
import math

import jax
import jax.numpy as jnp
import numpy as np
from jax import lax
from jax.experimental import pallas as pl
from jax.experimental.pallas import tpu as pltpu
from jax.sharding import PartitionSpec as P

NZ = 768
NB_DEV = 8
NCTF = 32
ITERS = 3
EPS = 1e-05
TILE = 128
GROUP = 4
SPREAD_GROUP = 8
EDGE_GROUP = 8
CHUNK = 512
f32 = jnp.float32
bf16 = jnp.bfloat16
NT = (((1,), (1,)), ((), ()))


def round_up(n, m):
    return -(-n // m) * m


def make_plan(devices, bins, samples, columns):
    planes = NZ // devices
    middle = NZ // 2
    ut_count, xt_count = samples // TILE, columns // TILE
    theta = -0.5 * math.pi + math.pi * (np.arange(bins) + 0.5) / bins
    trig = np.concatenate([np.sin(theta), np.cos(theta)]).astype(np.float32)
    u = np.arange(samples)
    slack = 1e-3
    reach = 0
    plans = []
    for spread, size in ((False, GROUP), (True, SPREAD_GROUP)):
        rows = []
        for device in range(devices):
            z0 = device * planes
            z1 = z0 + planes
            lists = [[] for _ in range(xt_count)]
            edge = []
            for b in range(bins):
                s, c = math.sin(theta[b]), math.cos(theta[b])
                centre = middle + u * s
                near = (centre > z0 - slack - (1 if spread else 0)) & (centre < z1 + slack)
                if spread:
                    near[0] = z0 - 1 < middle < z1
                else:
                    near[0] = z0 <= middle < z1 if s > 0 else z0 < middle <= z1
                if not near.any():
                    continue
                if spread and s < 0 and z0 == middle:
                    edge.append(b * 4)
                    reach = max(reach, int(u[near].max()) + 1)
                    continue
                for ut in range(ut_count):
                    hit = u[ut * TILE : (ut + 1) * TILE][near[ut * TILE : (ut + 1) * TILE]]
                    if hit.size == 0:
                        continue
                    first = max(0, int((hit.min() * c - 1.01) // TILE))
                    last = min(xt_count - 1, int((hit.max() * c + 1.01) // TILE))
                    for xt in range(first, last + 1):
                        lists[xt].append(b * 4 + ut)
            idle = (bins - 1 if z0 < middle else 0) * 4 + ut_count - 1
            tiles, codes = [], []
            for xt, entries in enumerate(lists):
                entries = entries + [idle] * (-len(entries) % size)
                tiles += [xt] * (len(entries) // size)
                codes += entries
            rows.append((tiles, codes, edge))
        groups = max(len(tiles) for tiles, _, _ in rows)
        start = 1 + groups * (1 + size)
        table = np.zeros((devices, start + 1 + max(len(edge) for _, _, edge in rows)), np.int32)
        for device, (tiles, codes, edge) in enumerate(rows):
            table[device, 0] = len(tiles)
            table[device, 1 : 1 + len(tiles)] = tiles
            table[device, 1 + groups : 1 + groups + len(codes)] = codes
            table[device, start] = len(edge) // EDGE_GROUP
            table[device, start + 1 : start + 1 + len(edge)] = edge
        plans.append((table, groups))
    edge_samples = round_up(reach, 16)
    assert edge_samples <= TILE and (bins // 2) % EDGE_GROUP == 0
    return plans[0], plans[1], edge_samples, trig


def lanes_of(shape, axis):
    return lax.broadcasted_iota(jnp.int32, shape, axis).astype(f32)


def block_of(table, trig, at, bins):
    code = table[at]
    b = lax.shift_right_logical(code, 2)
    ut = lax.bitwise_and(code, 3)
    return b, ut, trig[b], trig[bins + b], (ut * TILE).astype(f32)


def split3(x):
    hi = x.astype(bf16)
    rest = x - hi.astype(f32)
    mid = rest.astype(bf16)
    return [hi, mid, (rest - mid.astype(f32)).astype(bf16)]


def bump(t):
    falloff = jnp.maximum(1.0 - t * t, 0.0)
    return falloff * falloff, t * falloff


def row_weights(z0, rows, u, s, c, samples):
    centre = 0.5 * NZ + u * s
    kz, kzd = bump((z0 + lanes_of((rows, TILE), 0)) - centre)
    return centre, kz, kzd, u * (c * (4.0 / samples)), u * (s * (-4.0 / samples))


def reorder(x, device, mine):
    lane = lax.broadcasted_iota(jnp.int32, x.shape, 1)
    rows = x.shape[0]
    size = mine
    bit = 0
    while size < rows // 2 * TILE:
        if size < TILE:
            moved = jnp.where(
                lax.bitwise_and(lane, size) != 0,
                pltpu.roll(x, size, 1),
                pltpu.roll(x, TILE - size, 1),
            )
        else:
            step = size // TILE
            moved = jnp.concatenate([x[r ^ step : (r ^ step) + 1] for r in range(rows)], 0)
        flag = lax.bitwise_and(lax.shift_right_logical(device, bit), 1)
        x = jnp.where(flag == 1, moved, x)
        size, bit = 2 * size, bit + 1
    return x


def position(n_gz, n_dom):
    dom = lax.axis_index("dom")
    n_z = n_dom // 2
    core, z = lax.bitwise_and(dom, 1), lax.shift_right_logical(dom, 1)
    return (core * n_gz + lax.axis_index("gz")) * n_z + z


def fetch(pairs, sems):
    copies = [pltpu.make_async_copy(a, b, sems.at[n]) for n, (a, b) in enumerate(pairs)]
    for copy in copies:
        copy.start()
    return copies


def pack_kernel(
    planes, observed_hbm, classes_hbm, bins_hbm, volume,
    packed, plane, field, observed, classes, bin_ids, sems,
):
    dom = lax.axis_index("dom")
    after = jnp.minimum((dom + 1) * planes, volume.shape[0] - 1)
    copies = fetch(
        [
            (observed_hbm, observed),
            (classes_hbm, classes),
            (bins_hbm, bin_ids),
            (volume.at[pl.ds(0, 1)], plane),
            (volume.at[pl.ds(dom * planes, planes)], field.at[pl.ds(0, planes)]),
            (volume.at[pl.ds(after, 1)], field.at[pl.ds(planes, 1)]),
        ],
        sems,
    )
    for z in range(planes + 1, field.shape[0]):
        field[z] = jnp.zeros(field.shape[1:], f32)
    for copy in copies[:3]:
        copy.wait()
    count, rows, samples = observed.shape
    values = observed[...].astype(f32)
    for r in range(rows):
        packed[:, r * samples : (r + 1) * samples] = values[:, r, :].astype(bf16)
    diagonal = lanes_of((count, count), 0) == lanes_of((count, count), 1)
    lane = lanes_of((count, TILE), 1)
    tail = jnp.zeros((count, TILE), f32)
    for n, ids in enumerate((classes, bin_ids)):
        column = jnp.where(diagonal, ids[...].astype(f32), 0.0)
        tail = jnp.where(lane == n, jnp.sum(column, axis=1, keepdims=True), tail)
    packed[:, rows * samples :] = tail.astype(bf16)
    for copy in copies[3:]:
        copy.wait()


def extract_kernel(
    groups, length, samples, bins, planes, n_dom,
    table_hbm, trig_hbm, field, above, ctf_hbm, slope, pairs, flat,
    table, trig, ctf, vhi, vlo, out, sems,
):
    depth = field.shape[0]
    xt_count = vhi.shape[0]
    ut_count = samples // TILE
    dom = lax.axis_index("dom")
    device = lax.axis_index("gz") * n_dom + dom
    row = device * length
    first = device * planes
    z0, z1 = first.astype(f32), (first + planes).astype(f32)

    copies = fetch(
        [
            (table_hbm, table),
            (trig_hbm, trig),
            (ctf_hbm, ctf),
        ],
        sems,
    )
    out[...] = jnp.zeros_like(out)
    for copy in copies:
        copy.wait()
    last = dom == n_dom - 1
    for xt in range(xt_count):
        lanes = slice(xt * TILE, (xt + 1) * TILE)
        halo = (lax.broadcasted_iota(jnp.int32, (depth, TILE), 0) == planes) & last
        stacked = jnp.concatenate(
            [jnp.where(halo, above[0, r : r + 1, lanes], field[:, r, lanes]) for r in range(4)], 0
        )
        hi = stacked.astype(bf16)
        vhi[xt] = hi
        vlo[xt] = (stacked - hi.astype(f32)).astype(bf16)

    def step(j, carry):
        xt = table[row + 1 + j]
        hi_rows, lo_rows = vhi[xt], vlo[xt]
        xx = lanes_of((TILE, TILE), 0) + (xt * TILE).astype(f32)
        for k in range(GROUP):
            at = row + 1 + groups + j * GROUP + k
            b, ut, s, c, base = block_of(table, trig, at, bins)
            u = lanes_of((1, TILE), 1) + base
            centre, kz, kzd, z_factor, x_factor = row_weights(z0, depth, u, s, c, samples)
            below = s < 0.0
            place = centre * jnp.where(below, -1.0, 1.0)
            least, most = jnp.where(below, -z1, z0), jnp.where(below, -z0, z1)
            own = jnp.where((place >= least) & (place < most), 1.0, 0.0)
            z_factor, x_factor = z_factor * own, x_factor * own
            weights = jnp.concatenate(bump(xx - u * c), 1)
            whi = weights.astype(bf16)
            wlo = (weights - whi.astype(f32)).astype(bf16)
            sampled = (
                jnp.dot(hi_rows, whi, preferred_element_type=f32)
                + jnp.dot(lo_rows, whi, preferred_element_type=f32)
                + jnp.dot(hi_rows, wlo, preferred_element_type=f32)
            )
            leading, second = [], []
            for r in range(4):
                direct = sampled[r * depth : (r + 1) * depth, :TILE]
                tilted = sampled[r * depth : (r + 1) * depth, TILE:]
                leading.append(own * jnp.sum(direct * kz, axis=0, keepdims=True))
                second.append(
                    z_factor * jnp.sum(direct * kzd, axis=0, keepdims=True)
                    + x_factor * jnp.sum(tilted * kz, axis=0, keepdims=True)
                )
            span = pl.ds(pl.multiple_of((b * ut_count + ut) * 8, 8), 8)
            out[span, :] = out[span, :] + jnp.concatenate(leading + second, 0)
        return carry

    lax.fori_loop(0, table[row], step, 0)

    slope[...] = jnp.zeros_like(slope)
    square, mixed = [], []
    for y in range(2):
        for ut in range(ut_count):
            square_sum, mixed_sum = 0.0, 0.0
            for r in (y, 2 + y):
                direct = out[pl.ds(ut * 8 + r, bins, stride=ut_count * 8), :].astype(bf16).astype(f32)
                tilted = out[pl.ds(ut * 8 + 4 + r, bins, stride=ut_count * 8), :].astype(bf16)
                at = (r * ut_count + ut) * TILE
                slope[bins:, at : at + TILE] = tilted
                tilted = tilted.astype(f32)
                square_sum = square_sum + tilted * tilted
                mixed_sum = mixed_sum - direct * tilted
            square.append(square_sum)
            mixed.append(mixed_sum)
    moments = jnp.concatenate([jnp.concatenate(square, 1), jnp.concatenate(mixed, 1)], 0)
    contrast = jnp.concatenate([ctf[:, 0, :], ctf[:, 1, :]], 1)
    flat[...] = contrast
    product = lax.dot_general(
        contrast * contrast, moments, NT, precision=lax.Precision.HIGHEST, preferred_element_type=f32
    )
    pairs[...] = jnp.concatenate(split3(product), 1)


def particle_kernel(width, mine, n_gz, n_dom, *refs):
    blocks = refs[: 2 * n_gz]
    ctf, slope, pairs, weighted, parts, bins_row = refs[2 * n_gz :]
    size = blocks[0].shape[0]
    joined = max(1, CHUNK // size)
    both = slope.shape[0]
    bins = both // 2
    flat = ctf[...]
    ctf_hi = flat.astype(bf16)
    ctf_lo = (flat - ctf_hi.astype(f32)).astype(bf16)
    upper = jnp.where(lanes_of((8, both), 1) >= bins, 1.0, 0.0)
    select = jnp.where(lanes_of((8, both), 0) == upper, 1.0, 0.0).astype(bf16)
    select = jnp.concatenate([select] * 3, 1)
    slopes = slope[...]
    scalars = [[], []]

    for i in range(0, 2 * n_gz, joined):
        packed = jnp.concatenate([ref[...] for ref in blocks[i : i + joined]], 0)
        count = packed.shape[0]
        span = slice(i * size, i * size + count)
        ids = packed[:, width:]
        classes = ids[:, 0:1].astype(f32)
        onehot_class = jnp.where(lanes_of((count, NCTF), 1) == classes, 1.0, 0.0).astype(bf16)
        bin_of = ids[:, 1:2].astype(f32)
        lane = lanes_of((count, both), 1)
        chosen = (lane == bin_of) | (lane == bin_of + bins)
        contrast = jnp.dot(onehot_class, ctf_hi, preferred_element_type=f32) + jnp.dot(
            onehot_class, ctf_lo, preferred_element_type=f32
        )
        contrast = jnp.concatenate([contrast, contrast], 1)
        w = contrast * packed[:, :width].astype(f32)
        whi = w.astype(bf16)
        wlo = (w - whi.astype(f32)).astype(bf16)
        weighted[span, :] = whi
        along = lax.dot_general(whi, slopes, NT, preferred_element_type=f32) + lax.dot_general(
            wlo, slopes, NT, preferred_element_type=f32
        )
        tables = jnp.dot(onehot_class, pairs[...], preferred_element_type=f32)
        tables = tables[:, :both] + tables[:, both : 2 * both] + tables[:, 2 * both :]
        terms = jnp.concatenate(split3(jnp.where(chosen, along + tables, 0.0)), 1)
        rows = lax.dot_general(select, terms, NT, preferred_element_type=f32)
        for n in range(2):
            for q in range(count // TILE):
                scalars[n].append(rows[n : n + 1, q * TILE : (q + 1) * TILE])
        pick = jnp.where(lanes_of((8, TILE), 1) == 1.0, 1.0, 0.0).astype(bf16)
        bins_row[:, span] = lax.dot_general(pick, ids, NT, preferred_element_type=f32)[0:1]

    scalars = jnp.concatenate(scalars[0] + scalars[1], 0)
    scalars = reorder(scalars, position(n_gz, n_dom), mine)
    rows = scalars.shape[0]
    for n in range(parts.shape[0] // rows):
        parts[n * rows : (n + 1) * rows, :] = scalars


def weight_kernel(groups, length, bins, planes, n_dom, edge_samples, table, trig, right, edges):
    device = lax.axis_index("gz") * n_dom + lax.axis_index("dom")
    row = device * length
    uu = lanes_of((TILE, TILE), 0)

    def step(j, carry):
        xx = lanes_of((1, TILE), 1) + (table[row + 1 + j] * TILE).astype(f32)
        for k in range(SPREAD_GROUP):
            at = row + 1 + groups + j * SPREAD_GROUP + k
            _, _, _, c, base = block_of(table, trig, at, bins)
            for n, part in enumerate(bump((xx - base * c) - uu * c)):
                right[j, (2 * k + n) * TILE : (2 * k + n + 1) * TILE, :] = part.astype(bf16)
        return carry

    lax.fori_loop(0, table[row], step, 0)
    tail = row + 1 + groups * (1 + SPREAD_GROUP)

    def edge(j, carry):
        for k in range(EDGE_GROUP):
            at = j * EDGE_GROUP + k
            _, _, _, c, _ = block_of(table, trig, tail + 1 + at, bins)
            uu = lanes_of((edge_samples, TILE), 0)
            for n, part in enumerate(bump(lanes_of((1, TILE), 1) - uu * c)):
                edges[at, n * edge_samples : (n + 1) * edge_samples, :] = part.astype(bf16)
        return carry

    lax.fori_loop(0, table[tail], edge, 0)


def spread_kernel(
    groups, length, planes, samples, edge_samples, mine, n_gz, n_dom,
    table, trig, right, edges, parts, bins_row, weighted, pose, out, sums, total, poses,
):
    tiles, bins = sums.shape[0] // 2, sums.shape[1]
    ut_count = samples // TILE
    depth = total.shape[1] // 4
    count = bins_row.shape[1]
    chunk = min(CHUNK, count)
    device = lax.axis_index("gz") * n_dom + lax.axis_index("dom")
    row = device * length
    z0 = (device * planes).astype(f32)

    rows = count // TILE
    scalars = jnp.sum(parts[...].reshape(parts.shape[0] // (2 * rows), 2 * rows, TILE), axis=0)
    square, pull = scalars[:rows], scalars[rows:]
    curvature = square + EPS
    shift = jnp.zeros_like(square)
    for _ in range(ITERS):
        shift = shift + 0.5 * (pull - shift * square) / curvature
    here = position(n_gz, n_dom)
    poses[...] = shift * jnp.sqrt(curvature)
    first = here * mine
    line = poses[pl.ds(lax.div(first, TILE), 1), :]
    pose[...] = pltpu.roll(line, TILE - lax.rem(first, TILE), 1)[:, :mine]
    shift = reorder(jnp.concatenate([shift, shift], 0), here, mine)
    shift = jnp.concatenate([shift[q : q + 1] for q in range(rows)], 1)

    bin_sums = jnp.zeros((3 * bins, tiles * TILE), f32)
    for i in range(count // chunk):
        span = slice(i * chunk, (i + 1) * chunk)
        belongs = lanes_of((bins, chunk), 0) == bins_row[:, span]
        scaled = jnp.where(belongs, shift[:, span], 0.0)
        hi = scaled.astype(bf16)
        lo = (scaled - hi.astype(f32)).astype(bf16)
        onehot = jnp.where(belongs, 1.0, 0.0).astype(bf16)
        bin_sums = bin_sums + jnp.dot(
            jnp.concatenate([onehot, hi, lo], 0), weighted[span, :], preferred_element_type=f32
        )
    plain = bin_sums[:bins]
    slope_sum = bin_sums[bins : 2 * bins] + bin_sums[2 * bins :]
    for q in range(tiles):
        sums[q] = plain[:, q * TILE : (q + 1) * TILE]
        sums[tiles + q] = slope_sum[:, q * TILE : (q + 1) * TILE]
    total[...] = jnp.zeros_like(total)

    def step(j, carry):
        xt = table[row + 1 + j]
        left = []
        for k in range(SPREAD_GROUP):
            at = row + 1 + groups + j * SPREAD_GROUP + k
            b, ut, s, c, base = block_of(table, trig, at, bins)
            u = lanes_of((1, TILE), 1) + base
            _, kz, kzd, z_factor, x_factor = row_weights(z0, depth, u, s, c, samples)
            first, second = [], []
            for r in range(4):
                direct = sums[r * ut_count + ut, pl.ds(b, 1), :]
                tilted = sums[tiles + r * ut_count + ut, pl.ds(b, 1), :]
                first.append(kz * direct + kzd * (tilted * z_factor))
                second.append(kz * (tilted * x_factor))
            left += [jnp.concatenate(first, 0), jnp.concatenate(second, 0)]
        left = jnp.concatenate(left, 1)
        hi = left.astype(bf16)
        lo = (left - hi.astype(f32)).astype(bf16)
        both = jnp.dot(
            jnp.concatenate([hi, lo], 0), right[j], preferred_element_type=f32
        )
        total[xt] = total[xt] + both[: 4 * depth] + both[4 * depth :]
        return carry

    lax.fori_loop(0, table[row], step, 0)
    tail = row + 1 + groups * (1 + SPREAD_GROUP)

    def edge(j, carry):
        left, below = [], []
        rest = jnp.zeros((TILE - edge_samples, TILE), bf16)
        for k in range(EDGE_GROUP):
            b, _, s, c, _ = block_of(table, trig, tail + 1 + j * EDGE_GROUP + k, bins)
            u = lanes_of((1, TILE), 1)
            _, kz, kzd, z_factor, x_factor = row_weights(z0, 1, u, s, c, samples)
            direct = jnp.concatenate(
                [sums[r * ut_count, pl.ds(b, 1), :] for r in range(4)], 0
            )
            tilted = jnp.concatenate(
                [sums[tiles + r * ut_count, pl.ds(b, 1), :] for r in range(4)], 0
            )
            left += [kz * direct + (kzd * z_factor) * tilted, (kz * x_factor) * tilted]
            part = edges[j * EDGE_GROUP + k]
            below += [part[:edge_samples], rest, part[edge_samples:], rest]
        left = jnp.concatenate(left, 1)
        hi = left.astype(bf16).astype(f32)
        split = jnp.concatenate([hi, left - hi], 0).astype(bf16)
        both = jnp.dot(split, jnp.concatenate(below, 0), preferred_element_type=f32)
        return carry + both[:4] + both[4:]

    extra = lax.fori_loop(0, table[tail], edge, jnp.zeros((4, TILE), f32))
    for xt in range(total.shape[0]):
        for r in range(4):
            out[:, r, xt * TILE : (xt + 1) * TILE] = total[xt, r * depth : r * depth + planes, :]
    out[0, :, :TILE] = out[0, :, :TILE] + extra


def swap(x, axis, size, distance):
    return lax.ppermute(x, axis, [(i, i ^ distance) for i in range(size)])


def local(volume, observed, ctf_table, ctf_class, bin_ids):
    slab, rows, columns = volume.shape
    mine, _, samples = observed.shape
    n_gz, n_dom = lax.axis_size("gz"), lax.axis_size("dom")
    devices = n_gz * n_dom
    bins = NB_DEV * n_dom
    planes = NZ // devices
    count = mine * devices
    width = rows * samples
    xt_count, ut_count = columns // TILE, samples // TILE
    smem = pl.BlockSpec(memory_space=pltpu.SMEM)
    vmem = pl.BlockSpec(memory_space=pltpu.VMEM)
    hbm = pl.BlockSpec(memory_space=pltpu.HBM)
    wide = pltpu.CompilerParams(vmem_limit_bytes=60 * 2**20)
    params = pltpu.CompilerParams(vmem_limit_bytes=min(56, 19 + 37 * count // 4096) * 2**20)
    extract_plan, spread_plan, edge_samples, trig = make_plan(devices, bins, samples, columns)
    trig = jnp.asarray(trig)
    depth_in = round_up(planes + 1, 8)
    packed, plane, field = pl.pallas_call(
        functools.partial(pack_kernel, planes),
        out_shape=[
            jax.ShapeDtypeStruct((mine, width + TILE), bf16),
            jax.ShapeDtypeStruct((1, rows, columns), f32),
            jax.ShapeDtypeStruct((depth_in, rows, columns), f32),
        ],
        in_specs=[hbm] * 4,
        out_specs=[vmem] * 3,
        scratch_shapes=[
            pltpu.VMEM(observed.shape, bf16),
            pltpu.VMEM((1, mine), jnp.int32),
            pltpu.VMEM((1, mine), jnp.int32),
            pltpu.SemaphoreType.DMA((6,)),
        ],
        compiler_params=wide,
        name="pack",
    )(observed, ctf_class.reshape(1, mine), bin_ids.reshape(1, mine), volume)

    n_z = n_dom // 2
    above = lax.ppermute(plane, "gz", [(i, i - 1) for i in range(1, n_gz)])
    column = jnp.concatenate(
        [packed] + [swap(packed, "dom", n_dom, 2 * k) for k in range(1, n_z)], 0
    )
    spread_table, spread_groups = spread_plan
    spread_table_flat = jnp.asarray(spread_table.reshape(-1))
    right, edges = pl.pallas_call(
        functools.partial(
            weight_kernel, spread_groups, spread_table.shape[1], bins, planes, n_dom, edge_samples
        ),
        out_shape=[
            jax.ShapeDtypeStruct((spread_groups, SPREAD_GROUP * 2 * TILE, TILE), bf16),
            jax.ShapeDtypeStruct((bins // 2, 2 * edge_samples, TILE), bf16),
        ],
        in_specs=[smem, smem],
        out_specs=[vmem, vmem],
        compiler_params=wide,
        cost_estimate=pl.CostEstimate(flops=3 * 10**9, bytes_accessed=2**21, transcendentals=0),
        name="weights",
    )(spread_table_flat, trig)
    column, above, right, edges = lax.optimization_barrier((column, above, right, edges))
    planes_of = [column] + [swap(column, "gz", n_gz, j) for j in range(1, n_gz)]


    table, groups = extract_plan
    slope, pairs, flat_ctf = pl.pallas_call(
        functools.partial(
            extract_kernel, groups, table.shape[1], samples, bins, planes, n_dom
        ),
        out_shape=[
            jax.ShapeDtypeStruct((2 * bins, width), bf16),
            jax.ShapeDtypeStruct((NCTF, 6 * bins), bf16),
            jax.ShapeDtypeStruct((NCTF, width // 2), f32),
        ],
        in_specs=[hbm, hbm, vmem, vmem, hbm],
        out_specs=[vmem, vmem, vmem],
        scratch_shapes=[
            pltpu.SMEM((table.size,), jnp.int32),
            pltpu.SMEM(trig.shape, f32),
            pltpu.VMEM(ctf_table.shape, f32),
            pltpu.VMEM((xt_count, rows * depth_in, TILE), bf16),
            pltpu.VMEM((xt_count, rows * depth_in, TILE), bf16),
            pltpu.VMEM((bins * ut_count * 2 * rows, TILE), f32),
            pltpu.SemaphoreType.DMA((3,)),
        ],
        compiler_params=params,
        cost_estimate=pl.CostEstimate(flops=6 * 10**9, bytes_accessed=2**20, transcendentals=0),
        name="extract",
    )(jnp.asarray(table.reshape(-1)), trig, field, above, ctf_table)

    planes_of, slope = lax.optimization_barrier((planes_of, slope))
    gathered = planes_of + [swap(part, "dom", n_dom, 1) for part in planes_of]
    weighted, parts, bins_row = pl.pallas_call(
        functools.partial(particle_kernel, width, mine, n_gz, n_dom),
        out_shape=[
            jax.ShapeDtypeStruct((count, width), bf16),
            jax.ShapeDtypeStruct((devices * 2 * count // TILE, TILE), f32),
            jax.ShapeDtypeStruct((1, count), f32),
        ],
        in_specs=[vmem] * (len(gathered) + 3),
        out_specs=[vmem] * 3,
        compiler_params=params,
        name="particles",
    )(*gathered, flat_ctf, slope, pairs)

    parts = lax.all_to_all(parts, ("gz", "dom"), 0, 0, tiled=True)

    depth = round_up(planes, 8)
    pose, spread = pl.pallas_call(
        functools.partial(
            spread_kernel, spread_groups, spread_table.shape[1], planes, samples, edge_samples, mine, n_gz, n_dom
        ),
        out_shape=[
            jax.ShapeDtypeStruct((1, mine), f32),
            jax.ShapeDtypeStruct((planes, rows, columns), f32),
        ],
        in_specs=[smem, smem] + [vmem] * 5,
        out_specs=[vmem, vmem],
        scratch_shapes=[
            pltpu.VMEM((2 * width // TILE, bins, TILE), f32),
            pltpu.VMEM((xt_count, rows * depth, TILE), f32),
            pltpu.VMEM((count // TILE, TILE), f32),
        ],
        compiler_params=params,
        name="spread",
    )(spread_table_flat, trig, right, edges, parts, bins_row, weighted)
    pose = pose.reshape(mine)
    return pose, spread


def solution(mesh):
    return jax.shard_map(
        local,
        mesh=mesh,
        in_specs=(
            P("gz", None, None),
            P(("gz", "dom"), None, None),
            P(),
            P(("gz", "dom")),
            P(("gz", "dom")),
        ),
        out_specs=(P(("gz", "dom")), P(("gz", "dom"), None, None)),
        check_vma=False,
    )
```

```python
import functools
import math

import jax
import jax.numpy as jnp
import numpy as np
from jax import lax
from jax.experimental import pallas as pl
from jax.experimental.pallas import tpu as pltpu
from jax.sharding import PartitionSpec as P

NZ = 768
NB_DEV = 8
NCTF = 32
ITERS = 3
EPS = 1e-05
TILE = 128
GROUP = 4
SPREAD_GROUP = 8
EDGE_GROUP = 8
CHUNK = 512
f32 = jnp.float32
bf16 = jnp.bfloat16
NT = (((1,), (1,)), ((), ()))


def round_up(n, m):
    return -(-n // m) * m


def make_plan(devices, bins, samples, columns):
    planes = NZ // devices
    middle = NZ // 2
    ut_count, xt_count = samples // TILE, columns // TILE
    theta = -0.5 * math.pi + math.pi * (np.arange(bins) + 0.5) / bins
    trig = np.concatenate([np.sin(theta), np.cos(theta)]).astype(np.float32)
    u = np.arange(samples)
    slack = 1e-3
    reach = 0
    plans = []
    for spread, size in ((False, GROUP), (True, SPREAD_GROUP)):
        rows = []
        for device in range(devices):
            z0 = device * planes
            z1 = z0 + planes
            lists = [[] for _ in range(xt_count)]
            edge = []
            for b in range(bins):
                s, c = math.sin(theta[b]), math.cos(theta[b])
                centre = middle + u * s
                near = (centre > z0 - slack - (1 if spread else 0)) & (centre < z1 + slack)
                if spread:
                    near[0] = z0 - 1 < middle < z1
                else:
                    near[0] = z0 <= middle < z1 if s > 0 else z0 < middle <= z1
                if not near.any():
                    continue
                if spread and s < 0 and z0 == middle:
                    edge.append(b * 4)
                    reach = max(reach, int(u[near].max()) + 1)
                    continue
                for ut in range(ut_count):
                    hit = u[ut * TILE : (ut + 1) * TILE][near[ut * TILE : (ut + 1) * TILE]]
                    if hit.size == 0:
                        continue
                    first = max(0, int((hit.min() * c - 1.01) // TILE))
                    last = min(xt_count - 1, int((hit.max() * c + 1.01) // TILE))
                    for xt in range(first, last + 1):
                        lists[xt].append(b * 4 + ut)
            idle = (bins - 1 if z0 < middle else 0) * 4 + ut_count - 1
            tiles, codes = [], []
            for xt, entries in enumerate(lists):
                entries = entries + [idle] * (-len(entries) % size)
                tiles += [xt] * (len(entries) // size)
                codes += entries
            rows.append((tiles, codes, edge))
        groups = max(len(tiles) for tiles, _, _ in rows)
        start = 1 + groups * (1 + size)
        table = np.zeros((devices, start + 1 + max(len(edge) for _, _, edge in rows)), np.int32)
        for device, (tiles, codes, edge) in enumerate(rows):
            table[device, 0] = len(tiles)
            table[device, 1 : 1 + len(tiles)] = tiles
            table[device, 1 + groups : 1 + groups + len(codes)] = codes
            table[device, start] = len(edge) // EDGE_GROUP
            table[device, start + 1 : start + 1 + len(edge)] = edge
        plans.append((table, groups))
    edge_samples = round_up(reach, 16)
    assert edge_samples <= TILE and (bins // 2) % EDGE_GROUP == 0
    return plans[0], plans[1], edge_samples, trig


def lanes_of(shape, axis):
    return lax.broadcasted_iota(jnp.int32, shape, axis).astype(f32)


def block_of(table, trig, at, bins):
    code = table[at]
    b = lax.shift_right_logical(code, 2)
    ut = lax.bitwise_and(code, 3)
    return b, ut, trig[b], trig[bins + b], (ut * TILE).astype(f32)


def split3(x):
    hi = x.astype(bf16)
    rest = x - hi.astype(f32)
    mid = rest.astype(bf16)
    return [hi, mid, (rest - mid.astype(f32)).astype(bf16)]


def bump(t):
    falloff = jnp.maximum(1.0 - t * t, 0.0)
    return falloff * falloff, t * falloff


def row_weights(z0, rows, u, s, c, samples):
    centre = 0.5 * NZ + u * s
    kz, kzd = bump((z0 + lanes_of((rows, TILE), 0)) - centre)
    return centre, kz, kzd, u * (c * (4.0 / samples)), u * (s * (-4.0 / samples))


def reorder(x, device, mine):
    lane = lax.broadcasted_iota(jnp.int32, x.shape, 1)
    rows = x.shape[0]
    size = mine
    bit = 0
    while size < rows // 2 * TILE:
        if size < TILE:
            moved = jnp.where(
                lax.bitwise_and(lane, size) != 0,
                pltpu.roll(x, size, 1),
                pltpu.roll(x, TILE - size, 1),
            )
        else:
            step = size // TILE
            moved = jnp.concatenate([x[r ^ step : (r ^ step) + 1] for r in range(rows)], 0)
        flag = lax.bitwise_and(lax.shift_right_logical(device, bit), 1)
        x = jnp.where(flag == 1, moved, x)
        size, bit = 2 * size, bit + 1
    return x


def position(n_gz, n_dom):
    dom = lax.axis_index("dom")
    n_z = n_dom // 2
    core, z = lax.bitwise_and(dom, 1), lax.shift_right_logical(dom, 1)
    return (core * n_gz + lax.axis_index("gz")) * n_z + z


def fetch(pairs, sems):
    copies = [pltpu.make_async_copy(a, b, sems.at[n]) for n, (a, b) in enumerate(pairs)]
    for copy in copies:
        copy.start()
    return copies


def pack_kernel(
    planes, observed_hbm, classes_hbm, bins_hbm, volume,
    packed, plane, field, observed, classes, bin_ids, sems,
):
    dom = lax.axis_index("dom")
    after = jnp.minimum((dom + 1) * planes, volume.shape[0] - 1)
    copies = fetch(
        [
            (observed_hbm, observed),
            (classes_hbm, classes),
            (bins_hbm, bin_ids),
            (volume.at[pl.ds(0, 1)], plane),
            (volume.at[pl.ds(dom * planes, planes)], field.at[pl.ds(0, planes)]),
            (volume.at[pl.ds(after, 1)], field.at[pl.ds(planes, 1)]),
        ],
        sems,
    )
    for z in range(planes + 1, field.shape[0]):
        field[z] = jnp.zeros(field.shape[1:], f32)
    for copy in copies[:3]:
        copy.wait()
    count, rows, samples = observed.shape
    values = observed[...].astype(f32)
    for r in range(rows):
        packed[:, r * samples : (r + 1) * samples] = values[:, r, :].astype(bf16)
    diagonal = lanes_of((count, count), 0) == lanes_of((count, count), 1)
    lane = lanes_of((count, TILE), 1)
    tail = jnp.zeros((count, TILE), f32)
    for n, ids in enumerate((classes, bin_ids)):
        column = jnp.where(diagonal, ids[...].astype(f32), 0.0)
        tail = jnp.where(lane == n, jnp.sum(column, axis=1, keepdims=True), tail)
    packed[:, rows * samples :] = tail.astype(bf16)
    for copy in copies[3:]:
        copy.wait()


def extract_kernel(
    groups, length, samples, bins, planes, n_dom,
    table_hbm, trig_hbm, field, above, ctf_hbm, slope, pairs, flat,
    table, trig, ctf, vhi, vlo, out, sems,
):
    depth = field.shape[0]
    xt_count = vhi.shape[0]
    ut_count = samples // TILE
    dom = lax.axis_index("dom")
    device = lax.axis_index("gz") * n_dom + dom
    row = device * length
    first = device * planes
    z0, z1 = first.astype(f32), (first + planes).astype(f32)

    copies = fetch(
        [
            (table_hbm, table),
            (trig_hbm, trig),
            (ctf_hbm, ctf),
        ],
        sems,
    )
    out[...] = jnp.zeros_like(out)
    for copy in copies:
        copy.wait()
    last = dom == n_dom - 1
    for xt in range(xt_count):
        lanes = slice(xt * TILE, (xt + 1) * TILE)
        halo = (lax.broadcasted_iota(jnp.int32, (depth, TILE), 0) == planes) & last
        stacked = jnp.concatenate(
            [jnp.where(halo, above[0, r : r + 1, lanes], field[:, r, lanes]) for r in range(4)], 0
        )
        hi = stacked.astype(bf16)
        vhi[xt] = hi
        vlo[xt] = (stacked - hi.astype(f32)).astype(bf16)

    def step(j, carry):
        xt = table[row + 1 + j]
        hi_rows, lo_rows = vhi[xt], vlo[xt]
        xx = lanes_of((TILE, TILE), 0) + (xt * TILE).astype(f32)
        for k in range(GROUP):
            at = row + 1 + groups + j * GROUP + k
            b, ut, s, c, base = block_of(table, trig, at, bins)
            u = lanes_of((1, TILE), 1) + base
            centre, kz, kzd, z_factor, x_factor = row_weights(z0, depth, u, s, c, samples)
            below = s < 0.0
            place = centre * jnp.where(below, -1.0, 1.0)
            least, most = jnp.where(below, -z1, z0), jnp.where(below, -z0, z1)
            own = jnp.where((place >= least) & (place < most), 1.0, 0.0)
            z_factor, x_factor = z_factor * own, x_factor * own
            weights = jnp.concatenate(bump(xx - u * c), 1)
            whi = weights.astype(bf16)
            wlo = (weights - whi.astype(f32)).astype(bf16)
            sampled = (
                jnp.dot(hi_rows, whi, preferred_element_type=f32)
                + jnp.dot(lo_rows, whi, preferred_element_type=f32)
                + jnp.dot(hi_rows, wlo, preferred_element_type=f32)
            )
            leading, second = [], []
            for r in range(4):
                direct = sampled[r * depth : (r + 1) * depth, :TILE]
                tilted = sampled[r * depth : (r + 1) * depth, TILE:]
                leading.append(own * jnp.sum(direct * kz, axis=0, keepdims=True))
                second.append(
                    z_factor * jnp.sum(direct * kzd, axis=0, keepdims=True)
                    + x_factor * jnp.sum(tilted * kz, axis=0, keepdims=True)
                )
            span = pl.ds(pl.multiple_of((b * ut_count + ut) * 8, 8), 8)
            out[span, :] = out[span, :] + jnp.concatenate(leading + second, 0)
        return carry

    lax.fori_loop(0, table[row], step, 0)

    slope[...] = jnp.zeros_like(slope)
    square, mixed = [], []
    for y in range(2):
        for ut in range(ut_count):
            square_sum, mixed_sum = 0.0, 0.0
            for r in (y, 2 + y):
                direct = out[pl.ds(ut * 8 + r, bins, stride=ut_count * 8), :].astype(bf16).astype(f32)
                tilted = out[pl.ds(ut * 8 + 4 + r, bins, stride=ut_count * 8), :].astype(bf16)
                at = (r * ut_count + ut) * TILE
                slope[bins:, at : at + TILE] = tilted
                tilted = tilted.astype(f32)
                square_sum = square_sum + tilted * tilted
                mixed_sum = mixed_sum - direct * tilted
            square.append(square_sum)
            mixed.append(mixed_sum)
    moments = jnp.concatenate([jnp.concatenate(square, 1), jnp.concatenate(mixed, 1)], 0)
    contrast = jnp.concatenate([ctf[:, 0, :], ctf[:, 1, :]], 1)
    flat[...] = contrast
    product = lax.dot_general(
        contrast * contrast, moments, NT, precision=lax.Precision.HIGHEST, preferred_element_type=f32
    )
    pairs[...] = jnp.concatenate(split3(product), 1)


def particle_kernel(width, mine, n_gz, n_dom, *refs):
    blocks = refs[: 2 * n_gz]
    ctf, slope, pairs, weighted, parts, bins_row = refs[2 * n_gz :]
    size = blocks[0].shape[0]
    joined = max(1, CHUNK // size)
    both = slope.shape[0]
    bins = both // 2
    flat = ctf[...]
    ctf_hi = flat.astype(bf16)
    ctf_lo = (flat - ctf_hi.astype(f32)).astype(bf16)
    upper = jnp.where(lanes_of((8, both), 1) >= bins, 1.0, 0.0)
    select = jnp.where(lanes_of((8, both), 0) == upper, 1.0, 0.0).astype(bf16)
    select = jnp.concatenate([select] * 3, 1)
    slopes = slope[...]
    scalars = [[], []]

    for i in range(0, 2 * n_gz, joined):
        packed = jnp.concatenate([ref[...] for ref in blocks[i : i + joined]], 0)
        count = packed.shape[0]
        span = slice(i * size, i * size + count)
        ids = packed[:, width:]
        classes = ids[:, 0:1].astype(f32)
        onehot_class = jnp.where(lanes_of((count, NCTF), 1) == classes, 1.0, 0.0).astype(bf16)
        bin_of = ids[:, 1:2].astype(f32)
        lane = lanes_of((count, both), 1)
        chosen = (lane == bin_of) | (lane == bin_of + bins)
        contrast = jnp.dot(onehot_class, ctf_hi, preferred_element_type=f32) + jnp.dot(
            onehot_class, ctf_lo, preferred_element_type=f32
        )
        contrast = jnp.concatenate([contrast, contrast], 1)
        w = contrast * packed[:, :width].astype(f32)
        whi = w.astype(bf16)
        wlo = (w - whi.astype(f32)).astype(bf16)
        weighted[span, :] = whi
        along = lax.dot_general(whi, slopes, NT, preferred_element_type=f32) + lax.dot_general(
            wlo, slopes, NT, preferred_element_type=f32
        )
        tables = jnp.dot(onehot_class, pairs[...], preferred_element_type=f32)
        tables = tables[:, :both] + tables[:, both : 2 * both] + tables[:, 2 * both :]
        terms = jnp.concatenate(split3(jnp.where(chosen, along + tables, 0.0)), 1)
        rows = lax.dot_general(select, terms, NT, preferred_element_type=f32)
        for n in range(2):
            for q in range(count // TILE):
                scalars[n].append(rows[n : n + 1, q * TILE : (q + 1) * TILE])
        pick = jnp.where(lanes_of((8, TILE), 1) == 1.0, 1.0, 0.0).astype(bf16)
        bins_row[:, span] = lax.dot_general(pick, ids, NT, preferred_element_type=f32)[0:1]

    scalars = jnp.concatenate(scalars[0] + scalars[1], 0)
    scalars = reorder(scalars, position(n_gz, n_dom), mine)
    rows = scalars.shape[0]
    for n in range(parts.shape[0] // rows):
        parts[n * rows : (n + 1) * rows, :] = scalars


def weight_kernel(groups, length, bins, planes, n_dom, edge_samples, table, trig, right, edges):
    device = lax.axis_index("gz") * n_dom + lax.axis_index("dom")
    row = device * length
    uu = lanes_of((TILE, TILE), 0)

    def step(j, carry):
        xx = lanes_of((1, TILE), 1) + (table[row + 1 + j] * TILE).astype(f32)
        for k in range(SPREAD_GROUP):
            at = row + 1 + groups + j * SPREAD_GROUP + k
            _, _, _, c, base = block_of(table, trig, at, bins)
            for n, part in enumerate(bump((xx - base * c) - uu * c)):
                right[j, (2 * k + n) * TILE : (2 * k + n + 1) * TILE, :] = part.astype(bf16)
        return carry

    lax.fori_loop(0, table[row], step, 0)
    tail = row + 1 + groups * (1 + SPREAD_GROUP)

    def edge(j, carry):
        for k in range(EDGE_GROUP):
            at = j * EDGE_GROUP + k
            _, _, _, c, _ = block_of(table, trig, tail + 1 + at, bins)
            uu = lanes_of((edge_samples, TILE), 0)
            for n, part in enumerate(bump(lanes_of((1, TILE), 1) - uu * c)):
                edges[at, n * edge_samples : (n + 1) * edge_samples, :] = part.astype(bf16)
        return carry

    lax.fori_loop(0, table[tail], edge, 0)


def spread_kernel(
    groups, length, planes, samples, edge_samples, mine, n_gz, n_dom,
    table, trig, right, edges, parts, bins_row, weighted, pose, out, sums, total, poses,
):
    tiles, bins = sums.shape[0] // 2, sums.shape[1]
    ut_count = samples // TILE
    depth = total.shape[1] // 4
    count = bins_row.shape[1]
    chunk = min(CHUNK, count)
    device = lax.axis_index("gz") * n_dom + lax.axis_index("dom")
    row = device * length
    z0 = (device * planes).astype(f32)

    rows = count // TILE
    scalars = jnp.sum(parts[...].reshape(parts.shape[0] // (2 * rows), 2 * rows, TILE), axis=0)
    square, pull = scalars[:rows], scalars[rows:]
    curvature = square + EPS
    shift = jnp.zeros_like(square)
    for _ in range(ITERS):
        shift = shift + 0.5 * (pull - shift * square) / curvature
    here = position(n_gz, n_dom)
    poses[...] = shift * jnp.sqrt(curvature)
    first = here * mine
    line = poses[pl.ds(lax.div(first, TILE), 1), :]
    pose[...] = pltpu.roll(line, TILE - lax.rem(first, TILE), 1)[:, :mine]
    shift = reorder(jnp.concatenate([shift, shift], 0), here, mine)
    shift = jnp.concatenate([shift[q : q + 1] for q in range(rows)], 1)

    bin_sums = jnp.zeros((3 * bins, tiles * TILE), f32)
    for i in range(count // chunk):
        span = slice(i * chunk, (i + 1) * chunk)
        belongs = lanes_of((bins, chunk), 0) == bins_row[:, span]
        scaled = jnp.where(belongs, shift[:, span], 0.0)
        hi = scaled.astype(bf16)
        lo = (scaled - hi.astype(f32)).astype(bf16)
        onehot = jnp.where(belongs, 1.0, 0.0).astype(bf16)
        bin_sums = bin_sums + jnp.dot(
            jnp.concatenate([onehot, hi, lo], 0), weighted[span, :], preferred_element_type=f32
        )
    plain = bin_sums[:bins]
    slope_sum = bin_sums[bins : 2 * bins] + bin_sums[2 * bins :]
    for q in range(tiles):
        sums[q] = plain[:, q * TILE : (q + 1) * TILE]
        sums[tiles + q] = slope_sum[:, q * TILE : (q + 1) * TILE]
    total[...] = jnp.zeros_like(total)

    def step(j, carry):
        xt = table[row + 1 + j]
        left = []
        for k in range(SPREAD_GROUP):
            at = row + 1 + groups + j * SPREAD_GROUP + k
            b, ut, s, c, base = block_of(table, trig, at, bins)
            u = lanes_of((1, TILE), 1) + base
            _, kz, kzd, z_factor, x_factor = row_weights(z0, depth, u, s, c, samples)
            first, second = [], []
            for r in range(4):
                direct = sums[r * ut_count + ut, pl.ds(b, 1), :]
                tilted = sums[tiles + r * ut_count + ut, pl.ds(b, 1), :]
                first.append(kz * direct + kzd * (tilted * z_factor))
                second.append(kz * (tilted * x_factor))
            left += [jnp.concatenate(first, 0), jnp.concatenate(second, 0)]
        left = jnp.concatenate(left, 1)
        hi = left.astype(bf16)
        lo = (left - hi.astype(f32)).astype(bf16)
        both = jnp.dot(
            jnp.concatenate([hi, lo], 0), right[j], preferred_element_type=f32
        )
        total[xt] = total[xt] + both[: 4 * depth] + both[4 * depth :]
        return carry

    lax.fori_loop(0, table[row], step, 0)
    tail = row + 1 + groups * (1 + SPREAD_GROUP)

    def edge(j, carry):
        left, below = [], []
        rest = jnp.zeros((TILE - edge_samples, TILE), bf16)
        for k in range(EDGE_GROUP):
            b, _, s, c, _ = block_of(table, trig, tail + 1 + j * EDGE_GROUP + k, bins)
            u = lanes_of((1, TILE), 1)
            _, kz, kzd, z_factor, x_factor = row_weights(z0, 1, u, s, c, samples)
            direct = jnp.concatenate(
                [sums[r * ut_count, pl.ds(b, 1), :] for r in range(4)], 0
            )
            tilted = jnp.concatenate(
                [sums[tiles + r * ut_count, pl.ds(b, 1), :] for r in range(4)], 0
            )
            left += [kz * direct + (kzd * z_factor) * tilted, (kz * x_factor) * tilted]
            part = edges[j * EDGE_GROUP + k]
            below += [part[:edge_samples], rest, part[edge_samples:], rest]
        left = jnp.concatenate(left, 1)
        hi = left.astype(bf16).astype(f32)
        split = jnp.concatenate([hi, left - hi], 0).astype(bf16)
        both = jnp.dot(split, jnp.concatenate(below, 0), preferred_element_type=f32)
        return carry + both[:4] + both[4:]

    extra = lax.fori_loop(0, table[tail], edge, jnp.zeros((4, TILE), f32))
    for xt in range(total.shape[0]):
        for r in range(4):
            out[:, r, xt * TILE : (xt + 1) * TILE] = total[xt, r * depth : r * depth + planes, :]
    out[0, :, :TILE] = out[0, :, :TILE] + extra


def swap(x, axis, size, distance):
    return lax.ppermute(x, axis, [(i, i ^ distance) for i in range(size)])


def local(volume, observed, ctf_table, ctf_class, bin_ids):
    slab, rows, columns = volume.shape
    mine, _, samples = observed.shape
    n_gz, n_dom = lax.axis_size("gz"), lax.axis_size("dom")
    devices = n_gz * n_dom
    bins = NB_DEV * n_dom
    planes = NZ // devices
    count = mine * devices
    width = rows * samples
    xt_count, ut_count = columns // TILE, samples // TILE
    smem = pl.BlockSpec(memory_space=pltpu.SMEM)
    vmem = pl.BlockSpec(memory_space=pltpu.VMEM)
    hbm = pl.BlockSpec(memory_space=pltpu.HBM)
    wide = pltpu.CompilerParams(vmem_limit_bytes=60 * 2**20)
    params = pltpu.CompilerParams(vmem_limit_bytes=min(56, 19 + 37 * count // 4096) * 2**20)
    extract_plan, spread_plan, edge_samples, trig = make_plan(devices, bins, samples, columns)
    trig = jnp.asarray(trig)
    depth_in = round_up(planes + 1, 8)
    packed, plane, field = pl.pallas_call(
        functools.partial(pack_kernel, planes),
        out_shape=[
            jax.ShapeDtypeStruct((mine, width + TILE), bf16),
            jax.ShapeDtypeStruct((1, rows, columns), f32),
            jax.ShapeDtypeStruct((depth_in, rows, columns), f32),
        ],
        in_specs=[hbm] * 4,
        out_specs=[vmem] * 3,
        scratch_shapes=[
            pltpu.VMEM(observed.shape, bf16),
            pltpu.VMEM((1, mine), jnp.int32),
            pltpu.VMEM((1, mine), jnp.int32),
            pltpu.SemaphoreType.DMA((6,)),
        ],
        compiler_params=wide,
        name="pack",
    )(observed, ctf_class.reshape(1, mine), bin_ids.reshape(1, mine), volume)

    n_z = n_dom // 2
    above = lax.ppermute(plane, "gz", [(i, i - 1) for i in range(1, n_gz)])
    column = jnp.concatenate(
        [packed] + [swap(packed, "dom", n_dom, 2 * k) for k in range(1, n_z)], 0
    )
    column, above, trig = lax.optimization_barrier((column, above, trig))
    planes_of = [column] + [swap(column, "gz", n_gz, j) for j in range(1, n_gz)]


    table, groups = extract_plan
    slope, pairs, flat_ctf = pl.pallas_call(
        functools.partial(
            extract_kernel, groups, table.shape[1], samples, bins, planes, n_dom
        ),
        out_shape=[
            jax.ShapeDtypeStruct((2 * bins, width), bf16),
            jax.ShapeDtypeStruct((NCTF, 6 * bins), bf16),
            jax.ShapeDtypeStruct((NCTF, width // 2), f32),
        ],
        in_specs=[hbm, hbm, vmem, vmem, hbm],
        out_specs=[vmem, vmem, vmem],
        scratch_shapes=[
            pltpu.SMEM((table.size,), jnp.int32),
            pltpu.SMEM(trig.shape, f32),
            pltpu.VMEM(ctf_table.shape, f32),
            pltpu.VMEM((xt_count, rows * depth_in, TILE), bf16),
            pltpu.VMEM((xt_count, rows * depth_in, TILE), bf16),
            pltpu.VMEM((bins * ut_count * 2 * rows, TILE), f32),
            pltpu.SemaphoreType.DMA((3,)),
        ],
        compiler_params=params,
        cost_estimate=pl.CostEstimate(flops=6 * 10**9, bytes_accessed=2**20, transcendentals=0),
        name="extract",
    )(jnp.asarray(table.reshape(-1)), trig, field, above, ctf_table)

    spread_table, spread_groups = spread_plan
    spread_table_flat = jnp.asarray(spread_table.reshape(-1))
    right, edges = pl.pallas_call(
        functools.partial(
            weight_kernel, spread_groups, spread_table.shape[1], bins, planes, n_dom, edge_samples
        ),
        out_shape=[
            jax.ShapeDtypeStruct((spread_groups, SPREAD_GROUP * 2 * TILE, TILE), bf16),
            jax.ShapeDtypeStruct((bins // 2, 2 * edge_samples, TILE), bf16),
        ],
        in_specs=[smem, smem],
        out_specs=[vmem, vmem],
        compiler_params=params,
        cost_estimate=pl.CostEstimate(flops=3 * 10**9, bytes_accessed=2**21, transcendentals=0),
        name="weights",
    )(spread_table_flat, trig)
    planes_of, slope, right, edges = lax.optimization_barrier((planes_of, slope, right, edges))
    gathered = planes_of + [swap(part, "dom", n_dom, 1) for part in planes_of]
    weighted, parts, bins_row = pl.pallas_call(
        functools.partial(particle_kernel, width, mine, n_gz, n_dom),
        out_shape=[
            jax.ShapeDtypeStruct((count, width), bf16),
            jax.ShapeDtypeStruct((devices * 2 * count // TILE, TILE), f32),
            jax.ShapeDtypeStruct((1, count), f32),
        ],
        in_specs=[vmem] * (len(gathered) + 3),
        out_specs=[vmem] * 3,
        compiler_params=params,
        name="particles",
    )(*gathered, flat_ctf, slope, pairs)

    parts = lax.all_to_all(parts, ("gz", "dom"), 0, 0, tiled=True)

    depth = round_up(planes, 8)
    pose, spread = pl.pallas_call(
        functools.partial(
            spread_kernel, spread_groups, spread_table.shape[1], planes, samples, edge_samples, mine, n_gz, n_dom
        ),
        out_shape=[
            jax.ShapeDtypeStruct((1, mine), f32),
            jax.ShapeDtypeStruct((planes, rows, columns), f32),
        ],
        in_specs=[smem, smem] + [vmem] * 5,
        out_specs=[vmem, vmem],
        scratch_shapes=[
            pltpu.VMEM((2 * width // TILE, bins, TILE), f32),
            pltpu.VMEM((xt_count, rows * depth, TILE), f32),
            pltpu.VMEM((count // TILE, TILE), f32),
        ],
        compiler_params=params,
        name="spread",
    )(spread_table_flat, trig, right, edges, parts, bins_row, weighted)
    pose = pose.reshape(mine)
    return pose, spread


def solution(mesh):
    return jax.shard_map(
        local,
        mesh=mesh,
        in_specs=(
            P("gz", None, None),
            P(("gz", "dom"), None, None),
            P(),
            P(("gz", "dom")),
            P(("gz", "dom")),
        ),
        out_specs=(P(("gz", "dom")), P(("gz", "dom"), None, None)),
        check_vma=False,
    )
```

```python
import functools
import math

import jax
import jax.numpy as jnp
import numpy as np
from jax import lax
from jax.experimental import pallas as pl
from jax.experimental.pallas import tpu as pltpu
from jax.sharding import PartitionSpec as P

NZ = 768
NB_DEV = 8
NCTF = 32
ITERS = 3
EPS = 1e-05
TILE = 128
GROUP = 8
SPREAD_GROUP = 8
EDGE_GROUP = 8
CHUNK = 512
f32 = jnp.float32
bf16 = jnp.bfloat16
NT = (((1,), (1,)), ((), ()))


def round_up(n, m):
    return -(-n // m) * m


def make_plan(devices, bins, samples, columns):
    planes = NZ // devices
    middle = NZ // 2
    ut_count, xt_count = samples // TILE, columns // TILE
    theta = -0.5 * math.pi + math.pi * (np.arange(bins) + 0.5) / bins
    trig = np.concatenate([np.sin(theta), np.cos(theta)]).astype(np.float32)
    u = np.arange(samples)
    slack = 1e-3
    reach = 0
    plans = []
    for spread, size in ((False, GROUP), (True, SPREAD_GROUP)):
        rows = []
        for device in range(devices):
            z0 = device * planes
            z1 = z0 + planes
            lists = [[] for _ in range(xt_count)]
            edge = []
            for b in range(bins):
                s, c = math.sin(theta[b]), math.cos(theta[b])
                centre = middle + u * s
                near = (centre > z0 - slack - (1 if spread else 0)) & (centre < z1 + slack)
                if spread:
                    near[0] = z0 - 1 < middle < z1
                else:
                    near[0] = z0 <= middle < z1 if s > 0 else z0 < middle <= z1
                if not near.any():
                    continue
                if spread and s < 0 and z0 == middle:
                    edge.append(b * 4)
                    reach = max(reach, int(u[near].max()) + 1)
                    continue
                for ut in range(ut_count):
                    hit = u[ut * TILE : (ut + 1) * TILE][near[ut * TILE : (ut + 1) * TILE]]
                    if hit.size == 0:
                        continue
                    first = max(0, int((hit.min() * c - 1.01) // TILE))
                    last = min(xt_count - 1, int((hit.max() * c + 1.01) // TILE))
                    for xt in range(first, last + 1):
                        lists[xt].append(b * 4 + ut)
            idle = (bins - 1 if z0 < middle else 0) * 4 + ut_count - 1
            tiles, codes = [], []
            for xt, entries in enumerate(lists):
                entries = entries + [idle] * (-len(entries) % size)
                tiles += [xt] * (len(entries) // size)
                codes += entries
            rows.append((tiles, codes, edge))
        groups = max(len(tiles) for tiles, _, _ in rows)
        start = 1 + groups * (1 + size)
        table = np.zeros((devices, start + 1 + max(len(edge) for _, _, edge in rows)), np.int32)
        for device, (tiles, codes, edge) in enumerate(rows):
            table[device, 0] = len(tiles)
            table[device, 1 : 1 + len(tiles)] = tiles
            table[device, 1 + groups : 1 + groups + len(codes)] = codes
            table[device, start] = len(edge) // EDGE_GROUP
            table[device, start + 1 : start + 1 + len(edge)] = edge
        plans.append((table, groups))
    edge_samples = round_up(reach, 16)
    assert edge_samples <= TILE and (bins // 2) % EDGE_GROUP == 0
    return plans[0], plans[1], edge_samples, trig


def lanes_of(shape, axis):
    return lax.broadcasted_iota(jnp.int32, shape, axis).astype(f32)


def block_of(table, trig, at, bins):
    code = table[at]
    b = lax.shift_right_logical(code, 2)
    ut = lax.bitwise_and(code, 3)
    return b, ut, trig[b], trig[bins + b], (ut * TILE).astype(f32)


def split3(x):
    hi = x.astype(bf16)
    rest = x - hi.astype(f32)
    mid = rest.astype(bf16)
    return [hi, mid, (rest - mid.astype(f32)).astype(bf16)]


def bump(t):
    falloff = jnp.maximum(1.0 - t * t, 0.0)
    return falloff * falloff, t * falloff


def row_weights(z0, rows, u, s, c, samples):
    centre = 0.5 * NZ + u * s
    kz, kzd = bump((z0 + lanes_of((rows, TILE), 0)) - centre)
    return centre, kz, kzd, u * (c * (4.0 / samples)), u * (s * (-4.0 / samples))


def reorder(x, device, mine):
    lane = lax.broadcasted_iota(jnp.int32, x.shape, 1)
    rows = x.shape[0]
    size = mine
    bit = 0
    while size < rows // 2 * TILE:
        if size < TILE:
            moved = jnp.where(
                lax.bitwise_and(lane, size) != 0,
                pltpu.roll(x, size, 1),
                pltpu.roll(x, TILE - size, 1),
            )
        else:
            step = size // TILE
            moved = jnp.concatenate([x[r ^ step : (r ^ step) + 1] for r in range(rows)], 0)
        flag = lax.bitwise_and(lax.shift_right_logical(device, bit), 1)
        x = jnp.where(flag == 1, moved, x)
        size, bit = 2 * size, bit + 1
    return x


def position(n_gz, n_dom):
    dom = lax.axis_index("dom")
    n_z = n_dom // 2
    core, z = lax.bitwise_and(dom, 1), lax.shift_right_logical(dom, 1)
    return (core * n_gz + lax.axis_index("gz")) * n_z + z


def fetch(pairs, sems):
    copies = [pltpu.make_async_copy(a, b, sems.at[n]) for n, (a, b) in enumerate(pairs)]
    for copy in copies:
        copy.start()
    return copies


def pack_kernel(
    planes, observed_hbm, classes_hbm, bins_hbm, volume,
    packed, plane, field, observed, classes, bin_ids, sems,
):
    dom = lax.axis_index("dom")
    after = jnp.minimum((dom + 1) * planes, volume.shape[0] - 1)
    copies = fetch(
        [
            (observed_hbm, observed),
            (classes_hbm, classes),
            (bins_hbm, bin_ids),
            (volume.at[pl.ds(0, 1)], plane),
            (volume.at[pl.ds(dom * planes, planes)], field.at[pl.ds(0, planes)]),
            (volume.at[pl.ds(after, 1)], field.at[pl.ds(planes, 1)]),
        ],
        sems,
    )
    for z in range(planes + 1, field.shape[0]):
        field[z] = jnp.zeros(field.shape[1:], f32)
    for copy in copies[:3]:
        copy.wait()
    count, rows, samples = observed.shape
    values = observed[...].astype(f32)
    for r in range(rows):
        packed[:, r * samples : (r + 1) * samples] = values[:, r, :].astype(bf16)
    diagonal = lanes_of((count, count), 0) == lanes_of((count, count), 1)
    lane = lanes_of((count, TILE), 1)
    tail = jnp.zeros((count, TILE), f32)
    for n, ids in enumerate((classes, bin_ids)):
        column = jnp.where(diagonal, ids[...].astype(f32), 0.0)
        tail = jnp.where(lane == n, jnp.sum(column, axis=1, keepdims=True), tail)
    packed[:, rows * samples :] = tail.astype(bf16)
    for copy in copies[3:]:
        copy.wait()


def extract_kernel(
    groups, length, samples, bins, planes, n_dom,
    table_hbm, trig_hbm, field, above, ctf_hbm, slope, pairs, flat,
    table, trig, ctf, vhi, vlo, out, sems,
):
    depth = field.shape[0]
    xt_count = vhi.shape[0]
    ut_count = samples // TILE
    dom = lax.axis_index("dom")
    device = lax.axis_index("gz") * n_dom + dom
    row = device * length
    first = device * planes
    z0, z1 = first.astype(f32), (first + planes).astype(f32)

    copies = fetch(
        [
            (table_hbm, table),
            (trig_hbm, trig),
            (ctf_hbm, ctf),
        ],
        sems,
    )
    out[...] = jnp.zeros_like(out)
    for copy in copies:
        copy.wait()
    last = dom == n_dom - 1
    for xt in range(xt_count):
        lanes = slice(xt * TILE, (xt + 1) * TILE)
        halo = (lax.broadcasted_iota(jnp.int32, (depth, TILE), 0) == planes) & last
        stacked = jnp.concatenate(
            [jnp.where(halo, above[0, r : r + 1, lanes], field[:, r, lanes]) for r in range(4)], 0
        )
        hi = stacked.astype(bf16)
        vhi[xt] = hi
        vlo[xt] = (stacked - hi.astype(f32)).astype(bf16)

    def step(j, carry):
        xt = table[row + 1 + j]
        hi_rows, lo_rows = vhi[xt], vlo[xt]
        xx = lanes_of((TILE, TILE), 0) + (xt * TILE).astype(f32)
        for k in range(GROUP):
            at = row + 1 + groups + j * GROUP + k
            b, ut, s, c, base = block_of(table, trig, at, bins)
            u = lanes_of((1, TILE), 1) + base
            centre, kz, kzd, z_factor, x_factor = row_weights(z0, depth, u, s, c, samples)
            below = s < 0.0
            place = centre * jnp.where(below, -1.0, 1.0)
            least, most = jnp.where(below, -z1, z0), jnp.where(below, -z0, z1)
            own = jnp.where((place >= least) & (place < most), 1.0, 0.0)
            z_factor, x_factor = z_factor * own, x_factor * own
            weights = jnp.concatenate(bump(xx - u * c), 1)
            whi = weights.astype(bf16)
            wlo = (weights - whi.astype(f32)).astype(bf16)
            sampled = (
                jnp.dot(hi_rows, whi, preferred_element_type=f32)
                + jnp.dot(lo_rows, whi, preferred_element_type=f32)
                + jnp.dot(hi_rows, wlo, preferred_element_type=f32)
            )
            leading, second = [], []
            for r in range(4):
                direct = sampled[r * depth : (r + 1) * depth, :TILE]
                tilted = sampled[r * depth : (r + 1) * depth, TILE:]
                leading.append(own * jnp.sum(direct * kz, axis=0, keepdims=True))
                second.append(
                    z_factor * jnp.sum(direct * kzd, axis=0, keepdims=True)
                    + x_factor * jnp.sum(tilted * kz, axis=0, keepdims=True)
                )
            span = pl.ds(pl.multiple_of((b * ut_count + ut) * 8, 8), 8)
            out[span, :] = out[span, :] + jnp.concatenate(leading + second, 0)
        return carry

    lax.fori_loop(0, table[row], step, 0)

    slope[...] = jnp.zeros_like(slope)
    square, mixed = [], []
    for y in range(2):
        for ut in range(ut_count):
            square_sum, mixed_sum = 0.0, 0.0
            for r in (y, 2 + y):
                direct = out[pl.ds(ut * 8 + r, bins, stride=ut_count * 8), :].astype(bf16).astype(f32)
                tilted = out[pl.ds(ut * 8 + 4 + r, bins, stride=ut_count * 8), :].astype(bf16)
                at = (r * ut_count + ut) * TILE
                slope[bins:, at : at + TILE] = tilted
                tilted = tilted.astype(f32)
                square_sum = square_sum + tilted * tilted
                mixed_sum = mixed_sum - direct * tilted
            square.append(square_sum)
            mixed.append(mixed_sum)
    moments = jnp.concatenate([jnp.concatenate(square, 1), jnp.concatenate(mixed, 1)], 0)
    contrast = jnp.concatenate([ctf[:, 0, :], ctf[:, 1, :]], 1)
    flat[...] = contrast
    product = lax.dot_general(
        contrast * contrast, moments, NT, precision=lax.Precision.HIGHEST, preferred_element_type=f32
    )
    pairs[...] = jnp.concatenate(split3(product), 1)


def particle_kernel(width, mine, n_gz, n_dom, *refs):
    blocks = refs[: 2 * n_gz]
    ctf, slope, pairs, weighted, parts, bins_row = refs[2 * n_gz :]
    size = blocks[0].shape[0]
    joined = max(1, CHUNK // size)
    both = slope.shape[0]
    bins = both // 2
    flat = ctf[...]
    ctf_hi = flat.astype(bf16)
    ctf_lo = (flat - ctf_hi.astype(f32)).astype(bf16)
    upper = jnp.where(lanes_of((8, both), 1) >= bins, 1.0, 0.0)
    select = jnp.where(lanes_of((8, both), 0) == upper, 1.0, 0.0).astype(bf16)
    select = jnp.concatenate([select] * 3, 1)
    slopes = slope[...]
    scalars = [[], []]

    for i in range(0, 2 * n_gz, joined):
        packed = jnp.concatenate([ref[...] for ref in blocks[i : i + joined]], 0)
        count = packed.shape[0]
        span = slice(i * size, i * size + count)
        ids = packed[:, width:]
        classes = ids[:, 0:1].astype(f32)
        onehot_class = jnp.where(lanes_of((count, NCTF), 1) == classes, 1.0, 0.0).astype(bf16)
        bin_of = ids[:, 1:2].astype(f32)
        lane = lanes_of((count, both), 1)
        chosen = (lane == bin_of) | (lane == bin_of + bins)
        contrast = jnp.dot(onehot_class, ctf_hi, preferred_element_type=f32) + jnp.dot(
            onehot_class, ctf_lo, preferred_element_type=f32
        )
        contrast = jnp.concatenate([contrast, contrast], 1)
        w = contrast * packed[:, :width].astype(f32)
        whi = w.astype(bf16)
        wlo = (w - whi.astype(f32)).astype(bf16)
        weighted[span, :] = whi
        along = lax.dot_general(whi, slopes, NT, preferred_element_type=f32) + lax.dot_general(
            wlo, slopes, NT, preferred_element_type=f32
        )
        tables = jnp.dot(onehot_class, pairs[...], preferred_element_type=f32)
        tables = tables[:, :both] + tables[:, both : 2 * both] + tables[:, 2 * both :]
        terms = jnp.concatenate(split3(jnp.where(chosen, along + tables, 0.0)), 1)
        rows = lax.dot_general(select, terms, NT, preferred_element_type=f32)
        for n in range(2):
            for q in range(count // TILE):
                scalars[n].append(rows[n : n + 1, q * TILE : (q + 1) * TILE])
        pick = jnp.where(lanes_of((8, TILE), 1) == 1.0, 1.0, 0.0).astype(bf16)
        bins_row[:, span] = lax.dot_general(pick, ids, NT, preferred_element_type=f32)[0:1]

    scalars = jnp.concatenate(scalars[0] + scalars[1], 0)
    scalars = reorder(scalars, position(n_gz, n_dom), mine)
    rows = scalars.shape[0]
    for n in range(parts.shape[0] // rows):
        parts[n * rows : (n + 1) * rows, :] = scalars


def weight_kernel(groups, length, bins, planes, n_dom, edge_samples, table, trig, right, edges):
    device = lax.axis_index("gz") * n_dom + lax.axis_index("dom")
    row = device * length
    uu = lanes_of((TILE, TILE), 0)

    def step(j, carry):
        xx = lanes_of((1, TILE), 1) + (table[row + 1 + j] * TILE).astype(f32)
        for k in range(SPREAD_GROUP):
            at = row + 1 + groups + j * SPREAD_GROUP + k
            _, _, _, c, base = block_of(table, trig, at, bins)
            for n, part in enumerate(bump((xx - base * c) - uu * c)):
                right[j, (2 * k + n) * TILE : (2 * k + n + 1) * TILE, :] = part.astype(bf16)
        return carry

    lax.fori_loop(0, table[row], step, 0)
    tail = row + 1 + groups * (1 + SPREAD_GROUP)

    def edge(j, carry):
        for k in range(EDGE_GROUP):
            at = j * EDGE_GROUP + k
            _, _, _, c, _ = block_of(table, trig, tail + 1 + at, bins)
            uu = lanes_of((edge_samples, TILE), 0)
            for n, part in enumerate(bump(lanes_of((1, TILE), 1) - uu * c)):
                edges[at, n * edge_samples : (n + 1) * edge_samples, :] = part.astype(bf16)
        return carry

    lax.fori_loop(0, table[tail], edge, 0)


def spread_kernel(
    groups, length, planes, samples, edge_samples, mine, n_gz, n_dom,
    table, trig, right, edges, parts, bins_row, weighted, pose, out, sums, total, poses,
):
    tiles, bins = sums.shape[0] // 2, sums.shape[1]
    ut_count = samples // TILE
    depth = total.shape[1] // 4
    count = bins_row.shape[1]
    chunk = min(CHUNK, count)
    device = lax.axis_index("gz") * n_dom + lax.axis_index("dom")
    row = device * length
    z0 = (device * planes).astype(f32)

    rows = count // TILE
    scalars = jnp.sum(parts[...].reshape(parts.shape[0] // (2 * rows), 2 * rows, TILE), axis=0)
    square, pull = scalars[:rows], scalars[rows:]
    curvature = square + EPS
    shift = jnp.zeros_like(square)
    for _ in range(ITERS):
        shift = shift + 0.5 * (pull - shift * square) / curvature
    here = position(n_gz, n_dom)
    poses[...] = shift * jnp.sqrt(curvature)
    first = here * mine
    line = poses[pl.ds(lax.div(first, TILE), 1), :]
    pose[...] = pltpu.roll(line, TILE - lax.rem(first, TILE), 1)[:, :mine]
    shift = reorder(jnp.concatenate([shift, shift], 0), here, mine)
    shift = jnp.concatenate([shift[q : q + 1] for q in range(rows)], 1)

    bin_sums = jnp.zeros((3 * bins, tiles * TILE), f32)
    for i in range(count // chunk):
        span = slice(i * chunk, (i + 1) * chunk)
        belongs = lanes_of((bins, chunk), 0) == bins_row[:, span]
        scaled = jnp.where(belongs, shift[:, span], 0.0)
        hi = scaled.astype(bf16)
        lo = (scaled - hi.astype(f32)).astype(bf16)
        onehot = jnp.where(belongs, 1.0, 0.0).astype(bf16)
        bin_sums = bin_sums + jnp.dot(
            jnp.concatenate([onehot, hi, lo], 0), weighted[span, :], preferred_element_type=f32
        )
    plain = bin_sums[:bins]
    slope_sum = bin_sums[bins : 2 * bins] + bin_sums[2 * bins :]
    for q in range(tiles):
        sums[q] = plain[:, q * TILE : (q + 1) * TILE]
        sums[tiles + q] = slope_sum[:, q * TILE : (q + 1) * TILE]
    total[...] = jnp.zeros_like(total)

    def step(j, carry):
        xt = table[row + 1 + j]
        left = []
        for k in range(SPREAD_GROUP):
            at = row + 1 + groups + j * SPREAD_GROUP + k
            b, ut, s, c, base = block_of(table, trig, at, bins)
            u = lanes_of((1, TILE), 1) + base
            _, kz, kzd, z_factor, x_factor = row_weights(z0, depth, u, s, c, samples)
            first, second = [], []
            for r in range(4):
                direct = sums[r * ut_count + ut, pl.ds(b, 1), :]
                tilted = sums[tiles + r * ut_count + ut, pl.ds(b, 1), :]
                first.append(kz * direct + kzd * (tilted * z_factor))
                second.append(kz * (tilted * x_factor))
            left += [jnp.concatenate(first, 0), jnp.concatenate(second, 0)]
        left = jnp.concatenate(left, 1)
        hi = left.astype(bf16)
        lo = (left - hi.astype(f32)).astype(bf16)
        both = jnp.dot(
            jnp.concatenate([hi, lo], 0), right[j], preferred_element_type=f32
        )
        total[xt] = total[xt] + both[: 4 * depth] + both[4 * depth :]
        return carry

    lax.fori_loop(0, table[row], step, 0)
    tail = row + 1 + groups * (1 + SPREAD_GROUP)

    def edge(j, carry):
        left, below = [], []
        rest = jnp.zeros((TILE - edge_samples, TILE), bf16)
        for k in range(EDGE_GROUP):
            b, _, s, c, _ = block_of(table, trig, tail + 1 + j * EDGE_GROUP + k, bins)
            u = lanes_of((1, TILE), 1)
            _, kz, kzd, z_factor, x_factor = row_weights(z0, 1, u, s, c, samples)
            direct = jnp.concatenate(
                [sums[r * ut_count, pl.ds(b, 1), :] for r in range(4)], 0
            )
            tilted = jnp.concatenate(
                [sums[tiles + r * ut_count, pl.ds(b, 1), :] for r in range(4)], 0
            )
            left += [kz * direct + (kzd * z_factor) * tilted, (kz * x_factor) * tilted]
            part = edges[j * EDGE_GROUP + k]
            below += [part[:edge_samples], rest, part[edge_samples:], rest]
        left = jnp.concatenate(left, 1)
        hi = left.astype(bf16).astype(f32)
        split = jnp.concatenate([hi, left - hi], 0).astype(bf16)
        both = jnp.dot(split, jnp.concatenate(below, 0), preferred_element_type=f32)
        return carry + both[:4] + both[4:]

    extra = lax.fori_loop(0, table[tail], edge, jnp.zeros((4, TILE), f32))
    for xt in range(total.shape[0]):
        for r in range(4):
            out[:, r, xt * TILE : (xt + 1) * TILE] = total[xt, r * depth : r * depth + planes, :]
    out[0, :, :TILE] = out[0, :, :TILE] + extra


def swap(x, axis, size, distance):
    return lax.ppermute(x, axis, [(i, i ^ distance) for i in range(size)])


def local(volume, observed, ctf_table, ctf_class, bin_ids):
    slab, rows, columns = volume.shape
    mine, _, samples = observed.shape
    n_gz, n_dom = lax.axis_size("gz"), lax.axis_size("dom")
    devices = n_gz * n_dom
    bins = NB_DEV * n_dom
    planes = NZ // devices
    count = mine * devices
    width = rows * samples
    xt_count, ut_count = columns // TILE, samples // TILE
    smem = pl.BlockSpec(memory_space=pltpu.SMEM)
    vmem = pl.BlockSpec(memory_space=pltpu.VMEM)
    hbm = pl.BlockSpec(memory_space=pltpu.HBM)
    wide = pltpu.CompilerParams(vmem_limit_bytes=60 * 2**20)
    params = pltpu.CompilerParams(vmem_limit_bytes=min(56, 19 + 37 * count // 4096) * 2**20)
    extract_plan, spread_plan, edge_samples, trig = make_plan(devices, bins, samples, columns)
    trig = jnp.asarray(trig)
    depth_in = round_up(planes + 1, 8)
    packed, plane, field = pl.pallas_call(
        functools.partial(pack_kernel, planes),
        out_shape=[
            jax.ShapeDtypeStruct((mine, width + TILE), bf16),
            jax.ShapeDtypeStruct((1, rows, columns), f32),
            jax.ShapeDtypeStruct((depth_in, rows, columns), f32),
        ],
        in_specs=[hbm] * 4,
        out_specs=[vmem] * 3,
        scratch_shapes=[
            pltpu.VMEM(observed.shape, bf16),
            pltpu.VMEM((1, mine), jnp.int32),
            pltpu.VMEM((1, mine), jnp.int32),
            pltpu.SemaphoreType.DMA((6,)),
        ],
        compiler_params=wide,
        name="pack",
    )(observed, ctf_class.reshape(1, mine), bin_ids.reshape(1, mine), volume)

    n_z = n_dom // 2
    above = lax.ppermute(plane, "gz", [(i, i - 1) for i in range(1, n_gz)])
    column = jnp.concatenate(
        [packed] + [swap(packed, "dom", n_dom, 2 * k) for k in range(1, n_z)], 0
    )
    spread_table, spread_groups = spread_plan
    spread_table_flat = jnp.asarray(spread_table.reshape(-1))
    right, edges = pl.pallas_call(
        functools.partial(
            weight_kernel, spread_groups, spread_table.shape[1], bins, planes, n_dom, edge_samples
        ),
        out_shape=[
            jax.ShapeDtypeStruct((spread_groups, SPREAD_GROUP * 2 * TILE, TILE), bf16),
            jax.ShapeDtypeStruct((bins // 2, 2 * edge_samples, TILE), bf16),
        ],
        in_specs=[smem, smem],
        out_specs=[vmem, vmem],
        compiler_params=params,
        cost_estimate=pl.CostEstimate(flops=3 * 10**9, bytes_accessed=2**21, transcendentals=0),
        name="weights",
    )(spread_table_flat, trig)
    column, above, right, edges = lax.optimization_barrier((column, above, right, edges))
    planes_of = [column] + [swap(column, "gz", n_gz, j) for j in range(1, n_gz)]


    table, groups = extract_plan
    slope, pairs, flat_ctf = pl.pallas_call(
        functools.partial(
            extract_kernel, groups, table.shape[1], samples, bins, planes, n_dom
        ),
        out_shape=[
            jax.ShapeDtypeStruct((2 * bins, width), bf16),
            jax.ShapeDtypeStruct((NCTF, 6 * bins), bf16),
            jax.ShapeDtypeStruct((NCTF, width // 2), f32),
        ],
        in_specs=[hbm, hbm, vmem, vmem, hbm],
        out_specs=[vmem, vmem, vmem],
        scratch_shapes=[
            pltpu.SMEM((table.size,), jnp.int32),
            pltpu.SMEM(trig.shape, f32),
            pltpu.VMEM(ctf_table.shape, f32),
            pltpu.VMEM((xt_count, rows * depth_in, TILE), bf16),
            pltpu.VMEM((xt_count, rows * depth_in, TILE), bf16),
            pltpu.VMEM((bins * ut_count * 2 * rows, TILE), f32),
            pltpu.SemaphoreType.DMA((3,)),
        ],
        compiler_params=params,
        cost_estimate=pl.CostEstimate(flops=6 * 10**9, bytes_accessed=2**20, transcendentals=0),
        name="extract",
    )(jnp.asarray(table.reshape(-1)), trig, field, above, ctf_table)

    planes_of, slope = lax.optimization_barrier((planes_of, slope))
    gathered = planes_of + [swap(part, "dom", n_dom, 1) for part in planes_of]
    weighted, parts, bins_row = pl.pallas_call(
        functools.partial(particle_kernel, width, mine, n_gz, n_dom),
        out_shape=[
            jax.ShapeDtypeStruct((count, width), bf16),
            jax.ShapeDtypeStruct((devices * 2 * count // TILE, TILE), f32),
            jax.ShapeDtypeStruct((1, count), f32),
        ],
        in_specs=[vmem] * (len(gathered) + 3),
        out_specs=[vmem] * 3,
        compiler_params=params,
        name="particles",
    )(*gathered, flat_ctf, slope, pairs)

    parts = lax.all_to_all(parts, ("gz", "dom"), 0, 0, tiled=True)

    depth = round_up(planes, 8)
    pose, spread = pl.pallas_call(
        functools.partial(
            spread_kernel, spread_groups, spread_table.shape[1], planes, samples, edge_samples, mine, n_gz, n_dom
        ),
        out_shape=[
            jax.ShapeDtypeStruct((1, mine), f32),
            jax.ShapeDtypeStruct((planes, rows, columns), f32),
        ],
        in_specs=[smem, smem] + [vmem] * 5,
        out_specs=[vmem, vmem],
        scratch_shapes=[
            pltpu.VMEM((2 * width // TILE, bins, TILE), f32),
            pltpu.VMEM((xt_count, rows * depth, TILE), f32),
            pltpu.VMEM((count // TILE, TILE), f32),
        ],
        compiler_params=params,
        name="spread",
    )(spread_table_flat, trig, right, edges, parts, bins_row, weighted)
    pose = pose.reshape(mine)
    return pose, spread


def solution(mesh):
    return jax.shard_map(
        local,
        mesh=mesh,
        in_specs=(
            P("gz", None, None),
            P(("gz", "dom"), None, None),
            P(),
            P(("gz", "dom")),
            P(("gz", "dom")),
        ),
        out_specs=(P(("gz", "dom")), P(("gz", "dom"), None, None)),
        check_vma=False,
    )
```

```python
import functools
import math

import jax
import jax.numpy as jnp
import numpy as np
from jax import lax
from jax.experimental import pallas as pl
from jax.experimental.pallas import tpu as pltpu
from jax.sharding import PartitionSpec as P

NZ = 768
NB_DEV = 8
NCTF = 32
ITERS = 3
EPS = 1e-05
TILE = 128
GROUP = 8
SPREAD_GROUP = 8
EDGE_GROUP = 8
CHUNK = 512
f32 = jnp.float32
bf16 = jnp.bfloat16
NT = (((1,), (1,)), ((), ()))


def round_up(n, m):
    return -(-n // m) * m


def make_plan(devices, bins, samples, columns):
    planes = NZ // devices
    middle = NZ // 2
    ut_count, xt_count = samples // TILE, columns // TILE
    theta = -0.5 * math.pi + math.pi * (np.arange(bins) + 0.5) / bins
    trig = np.concatenate([np.sin(theta), np.cos(theta)]).astype(np.float32)
    u = np.arange(samples)
    slack = 1e-3
    reach = 0
    plans = []
    for spread, size in ((False, GROUP), (True, SPREAD_GROUP)):
        rows = []
        for device in range(devices):
            z0 = device * planes
            z1 = z0 + planes
            lists = [[] for _ in range(xt_count)]
            edge = []
            for b in range(bins):
                s, c = math.sin(theta[b]), math.cos(theta[b])
                centre = middle + u * s
                near = (centre > z0 - slack - (1 if spread else 0)) & (centre < z1 + slack)
                if spread:
                    near[0] = z0 - 1 < middle < z1
                else:
                    near[0] = z0 <= middle < z1 if s > 0 else z0 < middle <= z1
                if not near.any():
                    continue
                if spread and s < 0 and z0 == middle:
                    edge.append(b * 4)
                    reach = max(reach, int(u[near].max()) + 1)
                    continue
                for ut in range(ut_count):
                    hit = u[ut * TILE : (ut + 1) * TILE][near[ut * TILE : (ut + 1) * TILE]]
                    if hit.size == 0:
                        continue
                    first = max(0, int((hit.min() * c - 1.01) // TILE))
                    last = min(xt_count - 1, int((hit.max() * c + 1.01) // TILE))
                    for xt in range(first, last + 1):
                        lists[xt].append(b * 4 + ut)
            idle = (bins - 1 if z0 < middle else 0) * 4 + ut_count - 1
            tiles, codes = [], []
            for xt, entries in enumerate(lists):
                entries = entries + [idle] * (-len(entries) % size)
                tiles += [xt] * (len(entries) // size)
                codes += entries
            rows.append((tiles, codes, edge))
        groups = max(len(tiles) for tiles, _, _ in rows)
        start = 1 + groups * (1 + size)
        table = np.zeros((devices, start + 1 + max(len(edge) for _, _, edge in rows)), np.int32)
        for device, (tiles, codes, edge) in enumerate(rows):
            table[device, 0] = len(tiles)
            table[device, 1 : 1 + len(tiles)] = tiles
            table[device, 1 + groups : 1 + groups + len(codes)] = codes
            table[device, start] = len(edge) // EDGE_GROUP
            table[device, start + 1 : start + 1 + len(edge)] = edge
        plans.append((table, groups))
    edge_samples = round_up(reach, 16)
    assert edge_samples <= TILE and (bins // 2) % EDGE_GROUP == 0
    return plans[0], plans[1], edge_samples, trig


def lanes_of(shape, axis):
    return lax.broadcasted_iota(jnp.int32, shape, axis).astype(f32)


def block_of(table, trig, at, bins):
    code = table[at]
    b = lax.shift_right_logical(code, 2)
    ut = lax.bitwise_and(code, 3)
    return b, ut, trig[b], trig[bins + b], (ut * TILE).astype(f32)


def split3(x):
    hi = x.astype(bf16)
    rest = x - hi.astype(f32)
    mid = rest.astype(bf16)
    return [hi, mid, (rest - mid.astype(f32)).astype(bf16)]


def bump(t):
    falloff = jnp.maximum(1.0 - t * t, 0.0)
    return falloff * falloff, t * falloff


def row_weights(z0, rows, u, s, c, samples):
    centre = 0.5 * NZ + u * s
    kz, kzd = bump((z0 + lanes_of((rows, TILE), 0)) - centre)
    return centre, kz, kzd, u * (c * (4.0 / samples)), u * (s * (-4.0 / samples))


def reorder(x, device, mine):
    lane = lax.broadcasted_iota(jnp.int32, x.shape, 1)
    rows = x.shape[0]
    size = mine
    bit = 0
    while size < rows // 2 * TILE:
        if size < TILE:
            moved = jnp.where(
                lax.bitwise_and(lane, size) != 0,
                pltpu.roll(x, size, 1),
                pltpu.roll(x, TILE - size, 1),
            )
        else:
            step = size // TILE
            moved = jnp.concatenate([x[r ^ step : (r ^ step) + 1] for r in range(rows)], 0)
        flag = lax.bitwise_and(lax.shift_right_logical(device, bit), 1)
        x = jnp.where(flag == 1, moved, x)
        size, bit = 2 * size, bit + 1
    return x


def position(n_gz, n_dom):
    dom = lax.axis_index("dom")
    n_z = n_dom // 2
    core, z = lax.bitwise_and(dom, 1), lax.shift_right_logical(dom, 1)
    return (core * n_gz + lax.axis_index("gz")) * n_z + z


def fetch(pairs, sems):
    copies = [pltpu.make_async_copy(a, b, sems.at[n]) for n, (a, b) in enumerate(pairs)]
    for copy in copies:
        copy.start()
    return copies


def pack_kernel(
    planes, observed_hbm, classes_hbm, bins_hbm, volume,
    packed, plane, field, observed, classes, bin_ids, sems,
):
    dom = lax.axis_index("dom")
    after = jnp.minimum((dom + 1) * planes, volume.shape[0] - 1)
    copies = fetch(
        [
            (observed_hbm, observed),
            (classes_hbm, classes),
            (bins_hbm, bin_ids),
            (volume.at[pl.ds(0, 1)], plane),
            (volume.at[pl.ds(dom * planes, planes)], field.at[pl.ds(0, planes)]),
            (volume.at[pl.ds(after, 1)], field.at[pl.ds(planes, 1)]),
        ],
        sems,
    )
    for z in range(planes + 1, field.shape[0]):
        field[z] = jnp.zeros(field.shape[1:], f32)
    for copy in copies[:3]:
        copy.wait()
    count, rows, samples = observed.shape
    values = observed[...].astype(f32)
    for r in range(rows):
        packed[:, r * samples : (r + 1) * samples] = values[:, r, :].astype(bf16)
    diagonal = lanes_of((count, count), 0) == lanes_of((count, count), 1)
    lane = lanes_of((count, TILE), 1)
    tail = jnp.zeros((count, TILE), f32)
    for n, ids in enumerate((classes, bin_ids)):
        column = jnp.where(diagonal, ids[...].astype(f32), 0.0)
        tail = jnp.where(lane == n, jnp.sum(column, axis=1, keepdims=True), tail)
    packed[:, rows * samples :] = tail.astype(bf16)
    for copy in copies[3:]:
        copy.wait()


def extract_kernel(
    groups, length, samples, bins, planes, n_dom,
    table_hbm, trig_hbm, field, above, ctf_hbm, slope, pairs, flat,
    table, trig, ctf, vhi, vlo, out, sems,
):
    depth = field.shape[0]
    xt_count = vhi.shape[0]
    ut_count = samples // TILE
    dom = lax.axis_index("dom")
    device = lax.axis_index("gz") * n_dom + dom
    row = device * length
    first = device * planes
    z0, z1 = first.astype(f32), (first + planes).astype(f32)

    copies = fetch(
        [
            (table_hbm, table),
            (trig_hbm, trig),
            (ctf_hbm, ctf),
        ],
        sems,
    )
    out[...] = jnp.zeros_like(out)
    for copy in copies:
        copy.wait()
    last = dom == n_dom - 1
    for xt in range(xt_count):
        lanes = slice(xt * TILE, (xt + 1) * TILE)
        halo = (lax.broadcasted_iota(jnp.int32, (depth, TILE), 0) == planes) & last
        stacked = jnp.concatenate(
            [jnp.where(halo, above[0, r : r + 1, lanes], field[:, r, lanes]) for r in range(4)], 0
        )
        hi = stacked.astype(bf16)
        vhi[xt] = hi
        vlo[xt] = (stacked - hi.astype(f32)).astype(bf16)

    def step(j, carry):
        xt = table[row + 1 + j]
        hi_rows, lo_rows = vhi[xt], vlo[xt]
        xx = lanes_of((TILE, TILE), 0) + (xt * TILE).astype(f32)
        for k in range(GROUP):
            at = row + 1 + groups + j * GROUP + k
            b, ut, s, c, base = block_of(table, trig, at, bins)
            u = lanes_of((1, TILE), 1) + base
            centre, kz, kzd, z_factor, x_factor = row_weights(z0, depth, u, s, c, samples)
            below = s < 0.0
            place = centre * jnp.where(below, -1.0, 1.0)
            least, most = jnp.where(below, -z1, z0), jnp.where(below, -z0, z1)
            own = jnp.where((place >= least) & (place < most), 1.0, 0.0)
            z_factor, x_factor = z_factor * own, x_factor * own
            weights = jnp.concatenate(bump(xx - u * c), 1)
            whi = weights.astype(bf16)
            wlo = (weights - whi.astype(f32)).astype(bf16)
            sampled = (
                jnp.dot(hi_rows, whi, preferred_element_type=f32)
                + jnp.dot(lo_rows, whi, preferred_element_type=f32)
                + jnp.dot(hi_rows, wlo, preferred_element_type=f32)
            )
            leading, second = [], []
            for r in range(4):
                direct = sampled[r * depth : (r + 1) * depth, :TILE]
                tilted = sampled[r * depth : (r + 1) * depth, TILE:]
                leading.append(own * jnp.sum(direct * kz, axis=0, keepdims=True))
                second.append(
                    z_factor * jnp.sum(direct * kzd, axis=0, keepdims=True)
                    + x_factor * jnp.sum(tilted * kz, axis=0, keepdims=True)
                )
            span = pl.ds(pl.multiple_of((b * ut_count + ut) * 8, 8), 8)
            out[span, :] = out[span, :] + jnp.concatenate(leading + second, 0)
        return carry

    lax.fori_loop(0, table[row], step, 0)

    slope[...] = jnp.zeros_like(slope)
    square, mixed = [], []
    for y in range(2):
        for ut in range(ut_count):
            square_sum, mixed_sum = 0.0, 0.0
            for r in (y, 2 + y):
                direct = out[pl.ds(ut * 8 + r, bins, stride=ut_count * 8), :].astype(bf16).astype(f32)
                tilted = out[pl.ds(ut * 8 + 4 + r, bins, stride=ut_count * 8), :].astype(bf16)
                at = (r * ut_count + ut) * TILE
                slope[bins:, at : at + TILE] = tilted
                tilted = tilted.astype(f32)
                square_sum = square_sum + tilted * tilted
                mixed_sum = mixed_sum - direct * tilted
            square.append(square_sum)
            mixed.append(mixed_sum)
    moments = jnp.concatenate([jnp.concatenate(square, 1), jnp.concatenate(mixed, 1)], 0)
    contrast = jnp.concatenate([ctf[:, 0, :], ctf[:, 1, :]], 1)
    flat[...] = contrast
    product = lax.dot_general(
        contrast * contrast, moments, NT, precision=lax.Precision.HIGHEST, preferred_element_type=f32
    )
    pairs[...] = jnp.concatenate(split3(product), 1)


def particle_kernel(width, mine, n_gz, n_dom, final, *refs):
    blocks = refs[:n_gz]
    if final:
        ctf, slope, pairs, before, weighted, bins_row, parts = refs[n_gz:]
    else:
        ctf, slope, pairs, weighted, bins_row, parts = refs[n_gz:]
    size = blocks[0].shape[0]
    joined = max(1, CHUNK // size)
    both = slope.shape[0]
    bins = both // 2
    flat = ctf[...]
    ctf_hi = flat.astype(bf16)
    ctf_lo = (flat - ctf_hi.astype(f32)).astype(bf16)
    upper = jnp.where(lanes_of((8, both), 1) >= bins, 1.0, 0.0)
    select = jnp.where(lanes_of((8, both), 0) == upper, 1.0, 0.0).astype(bf16)
    select = jnp.concatenate([select] * 3, 1)
    slopes = slope[...]
    scalars = [[], []]

    for i in range(0, n_gz, joined):
        packed = jnp.concatenate([ref[...] for ref in blocks[i : i + joined]], 0)
        count = packed.shape[0]
        span = slice(i * size, i * size + count)
        ids = packed[:, width:]
        classes = ids[:, 0:1].astype(f32)
        onehot_class = jnp.where(lanes_of((count, NCTF), 1) == classes, 1.0, 0.0).astype(bf16)
        bin_of = ids[:, 1:2].astype(f32)
        lane = lanes_of((count, both), 1)
        chosen = (lane == bin_of) | (lane == bin_of + bins)
        contrast = jnp.dot(onehot_class, ctf_hi, preferred_element_type=f32) + jnp.dot(
            onehot_class, ctf_lo, preferred_element_type=f32
        )
        contrast = jnp.concatenate([contrast, contrast], 1)
        w = contrast * packed[:, :width].astype(f32)
        whi = w.astype(bf16)
        wlo = (w - whi.astype(f32)).astype(bf16)
        weighted[span, :] = whi
        along = lax.dot_general(whi, slopes, NT, preferred_element_type=f32) + lax.dot_general(
            wlo, slopes, NT, preferred_element_type=f32
        )
        tables = jnp.dot(onehot_class, pairs[...], preferred_element_type=f32)
        tables = tables[:, :both] + tables[:, both : 2 * both] + tables[:, 2 * both :]
        terms = jnp.concatenate(split3(jnp.where(chosen, along + tables, 0.0)), 1)
        rows = lax.dot_general(select, terms, NT, preferred_element_type=f32)
        for n in range(2):
            for q in range(count // TILE):
                scalars[n].append(rows[n : n + 1, q * TILE : (q + 1) * TILE])
        pick = jnp.where(lanes_of((8, TILE), 1) == 1.0, 1.0, 0.0).astype(bf16)
        bins_row[:, span] = lax.dot_general(pick, ids, NT, preferred_element_type=f32)[0:1]

    if not final:
        parts[...] = jnp.concatenate(scalars[0] + scalars[1], 0)
        return
    half = before.shape[0] // 2
    scalars = jnp.concatenate(
        [before[:half]] + scalars[0] + [before[half:]] + scalars[1], 0
    )
    scalars = reorder(scalars, position(n_gz, n_dom), mine)
    rows = scalars.shape[0]
    for n in range(parts.shape[0] // rows):
        parts[n * rows : (n + 1) * rows, :] = scalars


def weight_kernel(groups, length, bins, planes, n_dom, edge_samples, table, trig, right, edges):
    device = lax.axis_index("gz") * n_dom + lax.axis_index("dom")
    row = device * length
    uu = lanes_of((TILE, TILE), 0)

    def step(j, carry):
        xx = lanes_of((1, TILE), 1) + (table[row + 1 + j] * TILE).astype(f32)
        for k in range(SPREAD_GROUP):
            at = row + 1 + groups + j * SPREAD_GROUP + k
            _, _, _, c, base = block_of(table, trig, at, bins)
            for n, part in enumerate(bump((xx - base * c) - uu * c)):
                right[j, (2 * k + n) * TILE : (2 * k + n + 1) * TILE, :] = part.astype(bf16)
        return carry

    lax.fori_loop(0, table[row], step, 0)
    tail = row + 1 + groups * (1 + SPREAD_GROUP)

    def edge(j, carry):
        for k in range(EDGE_GROUP):
            at = j * EDGE_GROUP + k
            _, _, _, c, _ = block_of(table, trig, tail + 1 + at, bins)
            uu = lanes_of((edge_samples, TILE), 0)
            for n, part in enumerate(bump(lanes_of((1, TILE), 1) - uu * c)):
                edges[at, n * edge_samples : (n + 1) * edge_samples, :] = part.astype(bf16)
        return carry

    lax.fori_loop(0, table[tail], edge, 0)


def spread_kernel(
    groups, length, planes, samples, edge_samples, mine, n_gz, n_dom,
    table, trig, right, edges, parts, bins_own, weighted_own, bins_row, weighted,
    pose, out, sums, total, poses,
):
    tiles, bins = sums.shape[0] // 2, sums.shape[1]
    ut_count = samples // TILE
    depth = total.shape[1] // 4
    half = bins_row.shape[1]
    count = 2 * half
    chunk = min(CHUNK, half)
    device = lax.axis_index("gz") * n_dom + lax.axis_index("dom")
    row = device * length
    z0 = (device * planes).astype(f32)

    rows = count // TILE
    scalars = jnp.sum(parts[...].reshape(parts.shape[0] // (2 * rows), 2 * rows, TILE), axis=0)
    square, pull = scalars[:rows], scalars[rows:]
    curvature = square + EPS
    shift = jnp.zeros_like(square)
    for _ in range(ITERS):
        shift = shift + 0.5 * (pull - shift * square) / curvature
    here = position(n_gz, n_dom)
    poses[...] = shift * jnp.sqrt(curvature)
    first = here * mine
    line = poses[pl.ds(lax.div(first, TILE), 1), :]
    pose[...] = pltpu.roll(line, TILE - lax.rem(first, TILE), 1)[:, :mine]
    shift = reorder(jnp.concatenate([shift, shift], 0), here, mine)
    shift = jnp.concatenate([shift[q : q + 1] for q in range(rows)], 1)

    bin_sums = jnp.zeros((3 * bins, tiles * TILE), f32)
    for i in range(count // chunk):
        ids, values = (bins_own, weighted_own) if i * chunk < half else (bins_row, weighted)
        span = slice(i * chunk % half, i * chunk % half + chunk)
        belongs = lanes_of((bins, chunk), 0) == ids[:, span]
        scaled = jnp.where(belongs, shift[:, i * chunk : (i + 1) * chunk], 0.0)
        hi = scaled.astype(bf16)
        lo = (scaled - hi.astype(f32)).astype(bf16)
        onehot = jnp.where(belongs, 1.0, 0.0).astype(bf16)
        bin_sums = bin_sums + jnp.dot(
            jnp.concatenate([onehot, hi, lo], 0), values[span, :], preferred_element_type=f32
        )
    plain = bin_sums[:bins]
    slope_sum = bin_sums[bins : 2 * bins] + bin_sums[2 * bins :]
    for q in range(tiles):
        sums[q] = plain[:, q * TILE : (q + 1) * TILE]
        sums[tiles + q] = slope_sum[:, q * TILE : (q + 1) * TILE]
    total[...] = jnp.zeros_like(total)

    def step(j, carry):
        xt = table[row + 1 + j]
        left = []
        for k in range(SPREAD_GROUP):
            at = row + 1 + groups + j * SPREAD_GROUP + k
            b, ut, s, c, base = block_of(table, trig, at, bins)
            u = lanes_of((1, TILE), 1) + base
            _, kz, kzd, z_factor, x_factor = row_weights(z0, depth, u, s, c, samples)
            first, second = [], []
            for r in range(4):
                direct = sums[r * ut_count + ut, pl.ds(b, 1), :]
                tilted = sums[tiles + r * ut_count + ut, pl.ds(b, 1), :]
                first.append(kz * direct + kzd * (tilted * z_factor))
                second.append(kz * (tilted * x_factor))
            left += [jnp.concatenate(first, 0), jnp.concatenate(second, 0)]
        left = jnp.concatenate(left, 1)
        hi = left.astype(bf16)
        lo = (left - hi.astype(f32)).astype(bf16)
        both = jnp.dot(
            jnp.concatenate([hi, lo], 0), right[j], preferred_element_type=f32
        )
        total[xt] = total[xt] + both[: 4 * depth] + both[4 * depth :]
        return carry

    lax.fori_loop(0, table[row], step, 0)
    tail = row + 1 + groups * (1 + SPREAD_GROUP)

    def edge(j, carry):
        left, below = [], []
        rest = jnp.zeros((TILE - edge_samples, TILE), bf16)
        for k in range(EDGE_GROUP):
            b, _, s, c, _ = block_of(table, trig, tail + 1 + j * EDGE_GROUP + k, bins)
            u = lanes_of((1, TILE), 1)
            _, kz, kzd, z_factor, x_factor = row_weights(z0, 1, u, s, c, samples)
            direct = jnp.concatenate(
                [sums[r * ut_count, pl.ds(b, 1), :] for r in range(4)], 0
            )
            tilted = jnp.concatenate(
                [sums[tiles + r * ut_count, pl.ds(b, 1), :] for r in range(4)], 0
            )
            left += [kz * direct + (kzd * z_factor) * tilted, (kz * x_factor) * tilted]
            part = edges[j * EDGE_GROUP + k]
            below += [part[:edge_samples], rest, part[edge_samples:], rest]
        left = jnp.concatenate(left, 1)
        hi = left.astype(bf16).astype(f32)
        split = jnp.concatenate([hi, left - hi], 0).astype(bf16)
        both = jnp.dot(split, jnp.concatenate(below, 0), preferred_element_type=f32)
        return carry + both[:4] + both[4:]

    extra = lax.fori_loop(0, table[tail], edge, jnp.zeros((4, TILE), f32))
    for xt in range(total.shape[0]):
        for r in range(4):
            out[:, r, xt * TILE : (xt + 1) * TILE] = total[xt, r * depth : r * depth + planes, :]
    out[0, :, :TILE] = out[0, :, :TILE] + extra


def swap(x, axis, size, distance):
    return lax.ppermute(x, axis, [(i, i ^ distance) for i in range(size)])


def local(volume, observed, ctf_table, ctf_class, bin_ids):
    slab, rows, columns = volume.shape
    mine, _, samples = observed.shape
    n_gz, n_dom = lax.axis_size("gz"), lax.axis_size("dom")
    devices = n_gz * n_dom
    bins = NB_DEV * n_dom
    planes = NZ // devices
    count = mine * devices
    width = rows * samples
    xt_count, ut_count = columns // TILE, samples // TILE
    smem = pl.BlockSpec(memory_space=pltpu.SMEM)
    vmem = pl.BlockSpec(memory_space=pltpu.VMEM)
    hbm = pl.BlockSpec(memory_space=pltpu.HBM)
    wide = pltpu.CompilerParams(vmem_limit_bytes=60 * 2**20)
    params = pltpu.CompilerParams(vmem_limit_bytes=min(56, 19 + 37 * count // 4096) * 2**20)
    extract_plan, spread_plan, edge_samples, trig = make_plan(devices, bins, samples, columns)
    trig = jnp.asarray(trig)
    depth_in = round_up(planes + 1, 8)
    packed, plane, field = pl.pallas_call(
        functools.partial(pack_kernel, planes),
        out_shape=[
            jax.ShapeDtypeStruct((mine, width + TILE), bf16),
            jax.ShapeDtypeStruct((1, rows, columns), f32),
            jax.ShapeDtypeStruct((depth_in, rows, columns), f32),
        ],
        in_specs=[hbm] * 4,
        out_specs=[vmem] * 3,
        scratch_shapes=[
            pltpu.VMEM(observed.shape, bf16),
            pltpu.VMEM((1, mine), jnp.int32),
            pltpu.VMEM((1, mine), jnp.int32),
            pltpu.SemaphoreType.DMA((6,)),
        ],
        compiler_params=wide,
        name="pack",
    )(observed, ctf_class.reshape(1, mine), bin_ids.reshape(1, mine), volume)

    n_z = n_dom // 2
    above = lax.ppermute(plane, "gz", [(i, i - 1) for i in range(1, n_gz)])
    column = jnp.concatenate(
        [packed] + [swap(packed, "dom", n_dom, 2 * k) for k in range(1, n_z)], 0
    )
    spread_table, spread_groups = spread_plan
    spread_table_flat = jnp.asarray(spread_table.reshape(-1))
    right, edges = pl.pallas_call(
        functools.partial(
            weight_kernel, spread_groups, spread_table.shape[1], bins, planes, n_dom, edge_samples
        ),
        out_shape=[
            jax.ShapeDtypeStruct((spread_groups, SPREAD_GROUP * 2 * TILE, TILE), bf16),
            jax.ShapeDtypeStruct((bins // 2, 2 * edge_samples, TILE), bf16),
        ],
        in_specs=[smem, smem],
        out_specs=[vmem, vmem],
        compiler_params=params,
        cost_estimate=pl.CostEstimate(flops=3 * 10**9, bytes_accessed=2**21, transcendentals=0),
        name="weights",
    )(spread_table_flat, trig)
    column, above, right, edges = lax.optimization_barrier((column, above, right, edges))
    planes_of = [column] + [swap(column, "gz", n_gz, j) for j in range(1, n_gz)]


    table, groups = extract_plan
    slope, pairs, flat_ctf = pl.pallas_call(
        functools.partial(
            extract_kernel, groups, table.shape[1], samples, bins, planes, n_dom
        ),
        out_shape=[
            jax.ShapeDtypeStruct((2 * bins, width), bf16),
            jax.ShapeDtypeStruct((NCTF, 6 * bins), bf16),
            jax.ShapeDtypeStruct((NCTF, width // 2), f32),
        ],
        in_specs=[hbm, hbm, vmem, vmem, hbm],
        out_specs=[vmem, vmem, vmem],
        scratch_shapes=[
            pltpu.SMEM((table.size,), jnp.int32),
            pltpu.SMEM(trig.shape, f32),
            pltpu.VMEM(ctf_table.shape, f32),
            pltpu.VMEM((xt_count, rows * depth_in, TILE), bf16),
            pltpu.VMEM((xt_count, rows * depth_in, TILE), bf16),
            pltpu.VMEM((bins * ut_count * 2 * rows, TILE), f32),
            pltpu.SemaphoreType.DMA((3,)),
        ],
        compiler_params=params,
        cost_estimate=pl.CostEstimate(flops=6 * 10**9, bytes_accessed=2**20, transcendentals=0),
        name="extract",
    )(jnp.asarray(table.reshape(-1)), trig, field, above, ctf_table)

    planes_of, slope = lax.optimization_barrier((planes_of, slope))
    others = [swap(part, "dom", n_dom, 1) for part in planes_of]
    per_device = 2 * count // TILE

    def particles(blocks, before):
        final = len(before) > 0
        return pl.pallas_call(
            functools.partial(particle_kernel, width, mine, n_gz, n_dom, final),
            out_shape=[
                jax.ShapeDtypeStruct((count // 2, width), bf16),
                jax.ShapeDtypeStruct((1, count // 2), f32),
                jax.ShapeDtypeStruct(
                    (devices * per_device if final else per_device // 2, TILE), f32
                ),
            ],
            in_specs=[vmem] * (len(blocks) + 3 + len(before)),
            out_specs=[vmem] * 3,
            compiler_params=params,
            cost_estimate=pl.CostEstimate(
                flops=2 * 10**9, bytes_accessed=2**20, transcendentals=0
            ),
            name="particles",
        )(*blocks, flat_ctf, slope, pairs, *before)

    weighted_own, bins_own, before = particles(planes_of, [])
    weighted, bins_row, parts = particles(others, [before])

    parts = lax.all_to_all(parts, ("gz", "dom"), 0, 0, tiled=True)

    depth = round_up(planes, 8)
    pose, spread = pl.pallas_call(
        functools.partial(
            spread_kernel, spread_groups, spread_table.shape[1], planes, samples, edge_samples, mine, n_gz, n_dom
        ),
        out_shape=[
            jax.ShapeDtypeStruct((1, mine), f32),
            jax.ShapeDtypeStruct((planes, rows, columns), f32),
        ],
        in_specs=[smem, smem] + [vmem] * 7,
        out_specs=[vmem, vmem],
        scratch_shapes=[
            pltpu.VMEM((2 * width // TILE, bins, TILE), f32),
            pltpu.VMEM((xt_count, rows * depth, TILE), f32),
            pltpu.VMEM((count // TILE, TILE), f32),
        ],
        compiler_params=params,
        name="spread",
    )(
        spread_table_flat, trig, right, edges, parts, bins_own, weighted_own, bins_row, weighted
    )
    pose = pose.reshape(mine)
    return pose, spread


def solution(mesh):
    return jax.shard_map(
        local,
        mesh=mesh,
        in_specs=(
            P("gz", None, None),
            P(("gz", "dom"), None, None),
            P(),
            P(("gz", "dom")),
            P(("gz", "dom")),
        ),
        out_specs=(P(("gz", "dom")), P(("gz", "dom"), None, None)),
        check_vma=False,
    )
```

```python
import functools
import math

import jax
import jax.numpy as jnp
import numpy as np
from jax import lax
from jax.experimental import pallas as pl
from jax.experimental.pallas import tpu as pltpu
from jax.sharding import PartitionSpec as P

NZ = 768
NB_DEV = 8
NCTF = 32
ITERS = 3
EPS = 1e-05
TILE = 128
GROUP = 8
SPREAD_GROUP = 8
EDGE_GROUP = 8
CHUNK = 512
f32 = jnp.float32
bf16 = jnp.bfloat16
NT = (((1,), (1,)), ((), ()))


def round_up(n, m):
    return -(-n // m) * m


def make_plan(devices, bins, samples, columns):
    planes = NZ // devices
    middle = NZ // 2
    ut_count, xt_count = samples // TILE, columns // TILE
    theta = -0.5 * math.pi + math.pi * (np.arange(bins) + 0.5) / bins
    trig = np.concatenate([np.sin(theta), np.cos(theta)]).astype(np.float32)
    u = np.arange(samples)
    slack = 1e-3
    reach = 0
    plans = []
    for spread, size in ((False, GROUP), (True, SPREAD_GROUP)):
        rows = []
        for device in range(devices):
            z0 = device * planes
            z1 = z0 + planes
            lists = [[] for _ in range(xt_count)]
            edge = []
            for b in range(bins):
                s, c = math.sin(theta[b]), math.cos(theta[b])
                centre = middle + u * s
                near = (centre > z0 - slack - (1 if spread else 0)) & (centre < z1 + slack)
                if spread:
                    near[0] = z0 - 1 < middle < z1
                else:
                    near[0] = z0 <= middle < z1 if s > 0 else z0 < middle <= z1
                if not near.any():
                    continue
                if spread and s < 0 and z0 == middle:
                    edge.append(b * 4)
                    reach = max(reach, int(u[near].max()) + 1)
                    continue
                for ut in range(ut_count):
                    hit = u[ut * TILE : (ut + 1) * TILE][near[ut * TILE : (ut + 1) * TILE]]
                    if hit.size == 0:
                        continue
                    first = max(0, int((hit.min() * c - 1.01) // TILE))
                    last = min(xt_count - 1, int((hit.max() * c + 1.01) // TILE))
                    for xt in range(first, last + 1):
                        lists[xt].append(b * 4 + ut)
            idle = (bins - 1 if z0 < middle else 0) * 4 + ut_count - 1
            tiles, codes = [], []
            for xt, entries in enumerate(lists):
                entries = entries + [idle] * (-len(entries) % size)
                tiles += [xt] * (len(entries) // size)
                codes += entries
            rows.append((tiles, codes, edge))
        groups = max(len(tiles) for tiles, _, _ in rows)
        start = 1 + groups * (1 + size)
        table = np.zeros((devices, start + 1 + max(len(edge) for _, _, edge in rows)), np.int32)
        for device, (tiles, codes, edge) in enumerate(rows):
            table[device, 0] = len(tiles)
            table[device, 1 : 1 + len(tiles)] = tiles
            table[device, 1 + groups : 1 + groups + len(codes)] = codes
            table[device, start] = len(edge) // EDGE_GROUP
            table[device, start + 1 : start + 1 + len(edge)] = edge
        plans.append((table, groups))
    edge_samples = round_up(reach, 16)
    assert edge_samples <= TILE and (bins // 2) % EDGE_GROUP == 0
    return plans[0], plans[1], edge_samples, trig


def lanes_of(shape, axis):
    return lax.broadcasted_iota(jnp.int32, shape, axis).astype(f32)


def block_of(table, trig, at, bins):
    code = table[at]
    b = lax.shift_right_logical(code, 2)
    ut = lax.bitwise_and(code, 3)
    return b, ut, trig[b], trig[bins + b], (ut * TILE).astype(f32)


def split3(x):
    hi = x.astype(bf16)
    rest = x - hi.astype(f32)
    mid = rest.astype(bf16)
    return [hi, mid, (rest - mid.astype(f32)).astype(bf16)]


def bump(t):
    falloff = jnp.maximum(1.0 - t * t, 0.0)
    return falloff * falloff, t * falloff


def row_weights(z0, rows, u, s, c, samples):
    centre = 0.5 * NZ + u * s
    kz, kzd = bump((z0 + lanes_of((rows, TILE), 0)) - centre)
    return centre, kz, kzd, u * (c * (4.0 / samples)), u * (s * (-4.0 / samples))


def reorder(x, device, mine):
    lane = lax.broadcasted_iota(jnp.int32, x.shape, 1)
    rows = x.shape[0]
    size = mine
    bit = 0
    while size < rows // 2 * TILE:
        if size < TILE:
            moved = jnp.where(
                lax.bitwise_and(lane, size) != 0,
                pltpu.roll(x, size, 1),
                pltpu.roll(x, TILE - size, 1),
            )
        else:
            step = size // TILE
            moved = jnp.concatenate([x[r ^ step : (r ^ step) + 1] for r in range(rows)], 0)
        flag = lax.bitwise_and(lax.shift_right_logical(device, bit), 1)
        x = jnp.where(flag == 1, moved, x)
        size, bit = 2 * size, bit + 1
    return x


def position(n_gz, n_dom):
    dom = lax.axis_index("dom")
    n_z = n_dom // 2
    core, z = lax.bitwise_and(dom, 1), lax.shift_right_logical(dom, 1)
    return (core * n_gz + lax.axis_index("gz")) * n_z + z


def fetch(pairs, sems):
    copies = [pltpu.make_async_copy(a, b, sems.at[n]) for n, (a, b) in enumerate(pairs)]
    for copy in copies:
        copy.start()
    return copies


def pack_kernel(
    planes, observed_hbm, classes_hbm, bins_hbm, volume,
    packed, plane, field, observed, classes, bin_ids, sems,
):
    dom = lax.axis_index("dom")
    after = jnp.minimum((dom + 1) * planes, volume.shape[0] - 1)
    copies = fetch(
        [
            (observed_hbm, observed),
            (classes_hbm, classes),
            (bins_hbm, bin_ids),
            (volume.at[pl.ds(0, 1)], plane),
            (volume.at[pl.ds(dom * planes, planes)], field.at[pl.ds(0, planes)]),
            (volume.at[pl.ds(after, 1)], field.at[pl.ds(planes, 1)]),
        ],
        sems,
    )
    for z in range(planes + 1, field.shape[0]):
        field[z] = jnp.zeros(field.shape[1:], f32)
    for copy in copies[:3]:
        copy.wait()
    count, rows, samples = observed.shape
    values = observed[...].astype(f32)
    for r in range(rows):
        packed[:, r * samples : (r + 1) * samples] = values[:, r, :].astype(bf16)
    diagonal = lanes_of((count, count), 0) == lanes_of((count, count), 1)
    lane = lanes_of((count, TILE), 1)
    tail = jnp.zeros((count, TILE), f32)
    for n, ids in enumerate((classes, bin_ids)):
        column = jnp.where(diagonal, ids[...].astype(f32), 0.0)
        tail = jnp.where(lane == n, jnp.sum(column, axis=1, keepdims=True), tail)
    packed[:, rows * samples :] = tail.astype(bf16)
    for copy in copies[3:]:
        copy.wait()


def extract_kernel(
    groups, length, samples, bins, planes, n_dom,
    table_hbm, trig_hbm, field, above, ctf_hbm, slope, pairs, flat,
    table, trig, ctf, vhi, vlo, out, sems,
):
    depth = field.shape[0]
    xt_count = vhi.shape[0]
    ut_count = samples // TILE
    dom = lax.axis_index("dom")
    device = lax.axis_index("gz") * n_dom + dom
    row = device * length
    first = device * planes
    z0, z1 = first.astype(f32), (first + planes).astype(f32)

    copies = fetch(
        [
            (table_hbm, table),
            (trig_hbm, trig),
            (ctf_hbm, ctf),
        ],
        sems,
    )
    out[...] = jnp.zeros_like(out)
    for copy in copies:
        copy.wait()
    last = dom == n_dom - 1
    for xt in range(xt_count):
        lanes = slice(xt * TILE, (xt + 1) * TILE)
        halo = (lax.broadcasted_iota(jnp.int32, (depth, TILE), 0) == planes) & last
        stacked = jnp.concatenate(
            [jnp.where(halo, above[0, r : r + 1, lanes], field[:, r, lanes]) for r in range(4)], 0
        )
        hi = stacked.astype(bf16)
        vhi[xt] = hi
        vlo[xt] = (stacked - hi.astype(f32)).astype(bf16)

    def step(j, carry):
        xt = table[row + 1 + j]
        hi_rows, lo_rows = vhi[xt], vlo[xt]
        xx = lanes_of((TILE, TILE), 0) + (xt * TILE).astype(f32)
        for k in range(GROUP):
            at = row + 1 + groups + j * GROUP + k
            b, ut, s, c, base = block_of(table, trig, at, bins)
            u = lanes_of((1, TILE), 1) + base
            centre, kz, kzd, z_factor, x_factor = row_weights(z0, depth, u, s, c, samples)
            below = s < 0.0
            place = centre * jnp.where(below, -1.0, 1.0)
            least, most = jnp.where(below, -z1, z0), jnp.where(below, -z0, z1)
            own = jnp.where((place >= least) & (place < most), 1.0, 0.0)
            z_factor, x_factor = z_factor * own, x_factor * own
            weights = jnp.concatenate(bump(xx - u * c), 1)
            whi = weights.astype(bf16)
            wlo = (weights - whi.astype(f32)).astype(bf16)
            sampled = (
                jnp.dot(hi_rows, whi, preferred_element_type=f32)
                + jnp.dot(lo_rows, whi, preferred_element_type=f32)
                + jnp.dot(hi_rows, wlo, preferred_element_type=f32)
            )
            leading, second = [], []
            for r in range(4):
                direct = sampled[r * depth : (r + 1) * depth, :TILE]
                tilted = sampled[r * depth : (r + 1) * depth, TILE:]
                leading.append(own * jnp.sum(direct * kz, axis=0, keepdims=True))
                second.append(
                    z_factor * jnp.sum(direct * kzd, axis=0, keepdims=True)
                    + x_factor * jnp.sum(tilted * kz, axis=0, keepdims=True)
                )
            span = pl.ds(pl.multiple_of((b * ut_count + ut) * 8, 8), 8)
            out[span, :] = out[span, :] + jnp.concatenate(leading + second, 0)
        return carry

    lax.fori_loop(0, table[row], step, 0)

    slope[...] = jnp.zeros_like(slope)
    square, mixed = [], []
    for y in range(2):
        for ut in range(ut_count):
            square_sum, mixed_sum = 0.0, 0.0
            for r in (y, 2 + y):
                direct = out[pl.ds(ut * 8 + r, bins, stride=ut_count * 8), :].astype(bf16).astype(f32)
                tilted = out[pl.ds(ut * 8 + 4 + r, bins, stride=ut_count * 8), :].astype(bf16)
                at = (r * ut_count + ut) * TILE
                slope[bins:, at : at + TILE] = tilted
                tilted = tilted.astype(f32)
                square_sum = square_sum + tilted * tilted
                mixed_sum = mixed_sum - direct * tilted
            square.append(square_sum)
            mixed.append(mixed_sum)
    moments = jnp.concatenate([jnp.concatenate(square, 1), jnp.concatenate(mixed, 1)], 0)
    contrast = jnp.concatenate([ctf[:, 0, :], ctf[:, 1, :]], 1)
    flat[...] = contrast
    product = lax.dot_general(
        contrast * contrast, moments, NT, precision=lax.Precision.HIGHEST, preferred_element_type=f32
    )
    pairs[...] = jnp.concatenate(split3(product), 1)


def particle_kernel(width, mine, n_gz, n_dom, final, *refs):
    blocks = refs[:n_gz]
    if final:
        ctf, slope, pairs, before, weighted, bins_row, parts = refs[n_gz:]
    else:
        ctf, slope, pairs, weighted, bins_row, parts = refs[n_gz:]
    size = blocks[0].shape[0]
    joined = max(1, CHUNK // size)
    both = slope.shape[0]
    bins = both // 2
    flat = ctf[...]
    ctf_hi = flat.astype(bf16)
    ctf_lo = (flat - ctf_hi.astype(f32)).astype(bf16)
    upper = jnp.where(lanes_of((8, both), 1) >= bins, 1.0, 0.0)
    select = jnp.where(lanes_of((8, both), 0) == upper, 1.0, 0.0).astype(bf16)
    select = jnp.concatenate([select] * 3, 1)
    slopes = slope[...]
    scalars = [[], []]

    for i in range(0, n_gz, joined):
        packed = jnp.concatenate([ref[...] for ref in blocks[i : i + joined]], 0)
        count = packed.shape[0]
        span = slice(i * size, i * size + count)
        ids = packed[:, width:]
        classes = ids[:, 0:1].astype(f32)
        onehot_class = jnp.where(lanes_of((count, NCTF), 1) == classes, 1.0, 0.0).astype(bf16)
        bin_of = ids[:, 1:2].astype(f32)
        lane = lanes_of((count, both), 1)
        chosen = (lane == bin_of) | (lane == bin_of + bins)
        contrast = jnp.dot(onehot_class, ctf_hi, preferred_element_type=f32) + jnp.dot(
            onehot_class, ctf_lo, preferred_element_type=f32
        )
        contrast = jnp.concatenate([contrast, contrast], 1)
        w = contrast * packed[:, :width].astype(f32)
        whi = w.astype(bf16)
        wlo = (w - whi.astype(f32)).astype(bf16)
        weighted[span, :] = whi
        along = lax.dot_general(whi, slopes, NT, preferred_element_type=f32) + lax.dot_general(
            wlo, slopes, NT, preferred_element_type=f32
        )
        tables = jnp.dot(onehot_class, pairs[...], preferred_element_type=f32)
        tables = tables[:, :both] + tables[:, both : 2 * both] + tables[:, 2 * both :]
        terms = jnp.concatenate(split3(jnp.where(chosen, along + tables, 0.0)), 1)
        rows = lax.dot_general(select, terms, NT, preferred_element_type=f32)
        for n in range(2):
            for q in range(count // TILE):
                scalars[n].append(rows[n : n + 1, q * TILE : (q + 1) * TILE])
        pick = jnp.where(lanes_of((8, TILE), 1) == 1.0, 1.0, 0.0).astype(bf16)
        bins_row[:, span] = lax.dot_general(pick, ids, NT, preferred_element_type=f32)[0:1]

    if not final:
        parts[...] = jnp.concatenate(scalars[0] + scalars[1], 0)
        return
    half = before.shape[0] // 2
    scalars = jnp.concatenate(
        [before[:half]] + scalars[0] + [before[half:]] + scalars[1], 0
    )
    scalars = reorder(scalars, position(n_gz, n_dom), mine)
    rows = scalars.shape[0]
    for n in range(parts.shape[0] // rows):
        parts[n * rows : (n + 1) * rows, :] = scalars


def weight_kernel(groups, length, bins, planes, n_dom, edge_samples, table, trig, right, edges):
    device = lax.axis_index("gz") * n_dom + lax.axis_index("dom")
    row = device * length
    uu = lanes_of((TILE, TILE), 0)

    def step(j, carry):
        xx = lanes_of((1, TILE), 1) + (table[row + 1 + j] * TILE).astype(f32)
        for k in range(SPREAD_GROUP):
            at = row + 1 + groups + j * SPREAD_GROUP + k
            _, _, _, c, base = block_of(table, trig, at, bins)
            for n, part in enumerate(bump((xx - base * c) - uu * c)):
                right[j, (2 * k + n) * TILE : (2 * k + n + 1) * TILE, :] = part.astype(bf16)
        return carry

    lax.fori_loop(0, table[row], step, 0)
    tail = row + 1 + groups * (1 + SPREAD_GROUP)

    def edge(j, carry):
        for k in range(EDGE_GROUP):
            at = j * EDGE_GROUP + k
            _, _, _, c, _ = block_of(table, trig, tail + 1 + at, bins)
            uu = lanes_of((edge_samples, TILE), 0)
            for n, part in enumerate(bump(lanes_of((1, TILE), 1) - uu * c)):
                edges[at, n * edge_samples : (n + 1) * edge_samples, :] = part.astype(bf16)
        return carry

    lax.fori_loop(0, table[tail], edge, 0)


def spread_kernel(
    groups, length, planes, samples, edge_samples, mine, n_gz, n_dom,
    table, trig, right, edges, parts, bins_own, weighted_own, bins_row, weighted,
    pose, out, sums, total, poses,
):
    tiles, bins = sums.shape[0] // 2, sums.shape[1]
    ut_count = samples // TILE
    depth = total.shape[1] // 4
    half = bins_row.shape[1]
    count = 2 * half
    chunk = min(CHUNK, half)
    device = lax.axis_index("gz") * n_dom + lax.axis_index("dom")
    row = device * length
    z0 = (device * planes).astype(f32)

    rows = count // TILE
    scalars = jnp.sum(parts[...].reshape(parts.shape[0] // (2 * rows), 2 * rows, TILE), axis=0)
    square, pull = scalars[:rows], scalars[rows:]
    curvature = square + EPS
    shift = jnp.zeros_like(square)
    for _ in range(ITERS):
        shift = shift + 0.5 * (pull - shift * square) / curvature
    here = position(n_gz, n_dom)
    poses[...] = shift * jnp.sqrt(curvature)
    first = here * mine
    line = poses[pl.ds(lax.div(first, TILE), 1), :]
    pose[...] = pltpu.roll(line, TILE - lax.rem(first, TILE), 1)[:, :mine]
    shift = reorder(jnp.concatenate([shift, shift], 0), here, mine)
    shift = jnp.concatenate([shift[q : q + 1] for q in range(rows)], 1)

    bin_sums = jnp.zeros((3 * bins, tiles * TILE), f32)
    for i in range(count // chunk):
        ids, values = (bins_own, weighted_own) if i * chunk < half else (bins_row, weighted)
        span = slice(i * chunk % half, i * chunk % half + chunk)
        belongs = lanes_of((bins, chunk), 0) == ids[:, span]
        scaled = jnp.where(belongs, shift[:, i * chunk : (i + 1) * chunk], 0.0)
        hi = scaled.astype(bf16)
        lo = (scaled - hi.astype(f32)).astype(bf16)
        onehot = jnp.where(belongs, 1.0, 0.0).astype(bf16)
        bin_sums = bin_sums + jnp.dot(
            jnp.concatenate([onehot, hi, lo], 0), values[span, :], preferred_element_type=f32
        )
    plain = bin_sums[:bins]
    slope_sum = bin_sums[bins : 2 * bins] + bin_sums[2 * bins :]
    for q in range(tiles):
        sums[q] = plain[:, q * TILE : (q + 1) * TILE]
        sums[tiles + q] = slope_sum[:, q * TILE : (q + 1) * TILE]
    total[...] = jnp.zeros_like(total)

    def step(j, carry):
        xt = table[row + 1 + j]
        left = []
        for k in range(SPREAD_GROUP):
            at = row + 1 + groups + j * SPREAD_GROUP + k
            b, ut, s, c, base = block_of(table, trig, at, bins)
            u = lanes_of((1, TILE), 1) + base
            _, kz, kzd, z_factor, x_factor = row_weights(z0, depth, u, s, c, samples)
            first, second = [], []
            for r in range(4):
                direct = sums[r * ut_count + ut, pl.ds(b, 1), :]
                tilted = sums[tiles + r * ut_count + ut, pl.ds(b, 1), :]
                first.append(kz * direct + kzd * (tilted * z_factor))
                second.append(kz * (tilted * x_factor))
            left += [jnp.concatenate(first, 0), jnp.concatenate(second, 0)]
        left = jnp.concatenate(left, 1)
        hi = left.astype(bf16)
        lo = (left - hi.astype(f32)).astype(bf16)
        both = jnp.dot(
            jnp.concatenate([hi, lo], 0), right[j], preferred_element_type=f32
        )
        total[xt] = total[xt] + both[: 4 * depth] + both[4 * depth :]
        return carry

    lax.fori_loop(0, table[row], step, 0)
    tail = row + 1 + groups * (1 + SPREAD_GROUP)

    def edge(j, carry):
        left, below = [], []
        rest = jnp.zeros((TILE - edge_samples, TILE), bf16)
        for k in range(EDGE_GROUP):
            b, _, s, c, _ = block_of(table, trig, tail + 1 + j * EDGE_GROUP + k, bins)
            u = lanes_of((1, TILE), 1)
            _, kz, kzd, z_factor, x_factor = row_weights(z0, 1, u, s, c, samples)
            direct = jnp.concatenate(
                [sums[r * ut_count, pl.ds(b, 1), :] for r in range(4)], 0
            )
            tilted = jnp.concatenate(
                [sums[tiles + r * ut_count, pl.ds(b, 1), :] for r in range(4)], 0
            )
            left += [kz * direct + (kzd * z_factor) * tilted, (kz * x_factor) * tilted]
            part = edges[j * EDGE_GROUP + k]
            below += [part[:edge_samples], rest, part[edge_samples:], rest]
        left = jnp.concatenate(left, 1)
        hi = left.astype(bf16).astype(f32)
        split = jnp.concatenate([hi, left - hi], 0).astype(bf16)
        both = jnp.dot(split, jnp.concatenate(below, 0), preferred_element_type=f32)
        return carry + both[:4] + both[4:]

    extra = lax.fori_loop(0, table[tail], edge, jnp.zeros((4, TILE), f32))
    for xt in range(total.shape[0]):
        for r in range(4):
            out[:, r, xt * TILE : (xt + 1) * TILE] = total[xt, r * depth : r * depth + planes, :]
    out[0, :, :TILE] = out[0, :, :TILE] + extra


def swap(x, axis, size, distance):
    return lax.ppermute(x, axis, [(i, i ^ distance) for i in range(size)])


def local(volume, observed, ctf_table, ctf_class, bin_ids):
    slab, rows, columns = volume.shape
    mine, _, samples = observed.shape
    n_gz, n_dom = lax.axis_size("gz"), lax.axis_size("dom")
    devices = n_gz * n_dom
    bins = NB_DEV * n_dom
    planes = NZ // devices
    count = mine * devices
    width = rows * samples
    xt_count, ut_count = columns // TILE, samples // TILE
    smem = pl.BlockSpec(memory_space=pltpu.SMEM)
    vmem = pl.BlockSpec(memory_space=pltpu.VMEM)
    hbm = pl.BlockSpec(memory_space=pltpu.HBM)
    wide = pltpu.CompilerParams(vmem_limit_bytes=60 * 2**20)
    params = pltpu.CompilerParams(vmem_limit_bytes=min(56, 19 + 37 * count // 4096) * 2**20)
    extract_plan, spread_plan, edge_samples, trig = make_plan(devices, bins, samples, columns)
    trig = jnp.asarray(trig)
    depth_in = round_up(planes + 1, 8)
    packed, plane, field = pl.pallas_call(
        functools.partial(pack_kernel, planes),
        out_shape=[
            jax.ShapeDtypeStruct((mine, width + TILE), bf16),
            jax.ShapeDtypeStruct((1, rows, columns), f32),
            jax.ShapeDtypeStruct((depth_in, rows, columns), f32),
        ],
        in_specs=[hbm] * 4,
        out_specs=[vmem] * 3,
        scratch_shapes=[
            pltpu.VMEM(observed.shape, bf16),
            pltpu.VMEM((1, mine), jnp.int32),
            pltpu.VMEM((1, mine), jnp.int32),
            pltpu.SemaphoreType.DMA((6,)),
        ],
        compiler_params=wide,
        name="pack",
    )(observed, ctf_class.reshape(1, mine), bin_ids.reshape(1, mine), volume)

    n_z = n_dom // 2
    above = lax.ppermute(plane, "gz", [(i, i - 1) for i in range(1, n_gz)])
    column = jnp.concatenate(
        [packed] + [swap(packed, "dom", n_dom, 2 * k) for k in range(1, n_z)], 0
    )
    spread_table, spread_groups = spread_plan
    spread_table_flat = jnp.asarray(spread_table.reshape(-1))
    right, edges = pl.pallas_call(
        functools.partial(
            weight_kernel, spread_groups, spread_table.shape[1], bins, planes, n_dom, edge_samples
        ),
        out_shape=[
            jax.ShapeDtypeStruct((spread_groups, SPREAD_GROUP * 2 * TILE, TILE), bf16),
            jax.ShapeDtypeStruct((bins // 2, 2 * edge_samples, TILE), bf16),
        ],
        in_specs=[smem, smem],
        out_specs=[vmem, vmem],
        compiler_params=params,
        cost_estimate=pl.CostEstimate(flops=3 * 10**9, bytes_accessed=2**21, transcendentals=0),
        name="weights",
    )(spread_table_flat, trig)
    column, above, right, edges = lax.optimization_barrier((column, above, right, edges))
    planes_of = [column] + [swap(column, "gz", n_gz, j) for j in range(1, n_gz)]


    table, groups = extract_plan
    slope, pairs, flat_ctf = pl.pallas_call(
        functools.partial(
            extract_kernel, groups, table.shape[1], samples, bins, planes, n_dom
        ),
        out_shape=[
            jax.ShapeDtypeStruct((2 * bins, width), bf16),
            jax.ShapeDtypeStruct((NCTF, 6 * bins), bf16),
            jax.ShapeDtypeStruct((NCTF, width // 2), f32),
        ],
        in_specs=[hbm, hbm, vmem, vmem, hbm],
        out_specs=[vmem, vmem, vmem],
        scratch_shapes=[
            pltpu.SMEM((table.size,), jnp.int32),
            pltpu.SMEM(trig.shape, f32),
            pltpu.VMEM(ctf_table.shape, f32),
            pltpu.VMEM((xt_count, rows * depth_in, TILE), bf16),
            pltpu.VMEM((xt_count, rows * depth_in, TILE), bf16),
            pltpu.VMEM((bins * ut_count * 2 * rows, TILE), f32),
            pltpu.SemaphoreType.DMA((3,)),
        ],
        compiler_params=params,
        cost_estimate=pl.CostEstimate(flops=6 * 10**9, bytes_accessed=2**20, transcendentals=0),
        name="extract",
    )(jnp.asarray(table.reshape(-1)), trig, field, above, ctf_table)

    early = swap(column, "dom", n_dom, 1)
    planes_of, slope, early = lax.optimization_barrier((planes_of, slope, early))
    others = [early] + [swap(part, "dom", n_dom, 1) for part in planes_of[1:]]
    per_device = 2 * count // TILE

    def particles(blocks, before):
        final = len(before) > 0
        return pl.pallas_call(
            functools.partial(particle_kernel, width, mine, n_gz, n_dom, final),
            out_shape=[
                jax.ShapeDtypeStruct((count // 2, width), bf16),
                jax.ShapeDtypeStruct((1, count // 2), f32),
                jax.ShapeDtypeStruct(
                    (devices * per_device if final else per_device // 2, TILE), f32
                ),
            ],
            in_specs=[vmem] * (len(blocks) + 3 + len(before)),
            out_specs=[vmem] * 3,
            compiler_params=params,
            cost_estimate=pl.CostEstimate(
                flops=2 * 10**9, bytes_accessed=2**20, transcendentals=0
            ),
            name="particles",
        )(*blocks, flat_ctf, slope, pairs, *before)

    weighted_own, bins_own, before = particles(planes_of, [])
    weighted, bins_row, parts = particles(others, [before])

    parts = lax.all_to_all(parts, ("gz", "dom"), 0, 0, tiled=True)

    depth = round_up(planes, 8)
    pose, spread = pl.pallas_call(
        functools.partial(
            spread_kernel, spread_groups, spread_table.shape[1], planes, samples, edge_samples, mine, n_gz, n_dom
        ),
        out_shape=[
            jax.ShapeDtypeStruct((1, mine), f32),
            jax.ShapeDtypeStruct((planes, rows, columns), f32),
        ],
        in_specs=[smem, smem] + [vmem] * 7,
        out_specs=[vmem, vmem],
        scratch_shapes=[
            pltpu.VMEM((2 * width // TILE, bins, TILE), f32),
            pltpu.VMEM((xt_count, rows * depth, TILE), f32),
            pltpu.VMEM((count // TILE, TILE), f32),
        ],
        compiler_params=params,
        name="spread",
    )(
        spread_table_flat, trig, right, edges, parts, bins_own, weighted_own, bins_row, weighted
    )
    pose = pose.reshape(mine)
    return pose, spread


def solution(mesh):
    return jax.shard_map(
        local,
        mesh=mesh,
        in_specs=(
            P("gz", None, None),
            P(("gz", "dom"), None, None),
            P(),
            P(("gz", "dom")),
            P(("gz", "dom")),
        ),
        out_specs=(P(("gz", "dom")), P(("gz", "dom"), None, None)),
        check_vma=False,
    )
```

```python
import functools
import math

import jax
import jax.numpy as jnp
import numpy as np
from jax import lax
from jax.experimental import pallas as pl
from jax.experimental.pallas import tpu as pltpu
from jax.sharding import PartitionSpec as P

NZ = 768
NB_DEV = 8
NCTF = 32
ITERS = 3
EPS = 1e-05
TILE = 128
GROUP = 8
SPREAD_GROUP = 8
EDGE_GROUP = 8
CHUNK = 512
f32 = jnp.float32
bf16 = jnp.bfloat16
NT = (((1,), (1,)), ((), ()))


def round_up(n, m):
    return -(-n // m) * m


def make_plan(devices, bins, samples, columns):
    planes = NZ // devices
    middle = NZ // 2
    ut_count, xt_count = samples // TILE, columns // TILE
    theta = -0.5 * math.pi + math.pi * (np.arange(bins) + 0.5) / bins
    trig = np.concatenate([np.sin(theta), np.cos(theta)]).astype(np.float32)
    u = np.arange(samples)
    slack = 1e-3
    reach = 0
    plans = []
    for spread, size in ((False, GROUP), (True, SPREAD_GROUP)):
        rows = []
        for device in range(devices):
            z0 = device * planes
            z1 = z0 + planes
            lists = [[] for _ in range(xt_count)]
            edge = []
            for b in range(bins):
                s, c = math.sin(theta[b]), math.cos(theta[b])
                centre = middle + u * s
                near = (centre > z0 - slack - (1 if spread else 0)) & (centre < z1 + slack)
                if spread:
                    near[0] = z0 - 1 < middle < z1
                else:
                    near[0] = z0 <= middle < z1 if s > 0 else z0 < middle <= z1
                if not near.any():
                    continue
                if spread and s < 0 and z0 == middle:
                    edge.append(b * 4)
                    reach = max(reach, int(u[near].max()) + 1)
                    continue
                for ut in range(ut_count):
                    hit = u[ut * TILE : (ut + 1) * TILE][near[ut * TILE : (ut + 1) * TILE]]
                    if hit.size == 0:
                        continue
                    first = max(0, int((hit.min() * c - 1.01) // TILE))
                    last = min(xt_count - 1, int((hit.max() * c + 1.01) // TILE))
                    for xt in range(first, last + 1):
                        lists[xt].append(b * 4 + ut)
            idle = (bins - 1 if z0 < middle else 0) * 4 + ut_count - 1
            tiles, codes = [], []
            for xt, entries in enumerate(lists):
                entries = entries + [idle] * (-len(entries) % size)
                tiles += [xt] * (len(entries) // size)
                codes += entries
            rows.append((tiles, codes, edge))
        groups = max(len(tiles) for tiles, _, _ in rows)
        start = 1 + groups * (1 + size)
        table = np.zeros((devices, start + 1 + max(len(edge) for _, _, edge in rows)), np.int32)
        for device, (tiles, codes, edge) in enumerate(rows):
            table[device, 0] = len(tiles)
            table[device, 1 : 1 + len(tiles)] = tiles
            table[device, 1 + groups : 1 + groups + len(codes)] = codes
            table[device, start] = len(edge) // EDGE_GROUP
            table[device, start + 1 : start + 1 + len(edge)] = edge
        plans.append((table, groups))
    edge_samples = round_up(reach, 16)
    assert edge_samples <= TILE and (bins // 2) % EDGE_GROUP == 0
    return plans[0], plans[1], edge_samples, trig


def lanes_of(shape, axis):
    return lax.broadcasted_iota(jnp.int32, shape, axis).astype(f32)


def block_of(table, trig, at, bins):
    code = table[at]
    b = lax.shift_right_logical(code, 2)
    ut = lax.bitwise_and(code, 3)
    return b, ut, trig[b], trig[bins + b], (ut * TILE).astype(f32)


def split3(x):
    hi = x.astype(bf16)
    rest = x - hi.astype(f32)
    mid = rest.astype(bf16)
    return [hi, mid, (rest - mid.astype(f32)).astype(bf16)]


def bump(t):
    falloff = jnp.maximum(1.0 - t * t, 0.0)
    return falloff * falloff, t * falloff


def row_weights(z0, rows, u, s, c, samples):
    centre = 0.5 * NZ + u * s
    kz, kzd = bump((z0 + lanes_of((rows, TILE), 0)) - centre)
    return centre, kz, kzd, u * (c * (4.0 / samples)), u * (s * (-4.0 / samples))


def reorder(x, device, mine):
    lane = lax.broadcasted_iota(jnp.int32, x.shape, 1)
    rows = x.shape[0]
    size = mine
    bit = 0
    while size < rows // 2 * TILE:
        if size < TILE:
            moved = jnp.where(
                lax.bitwise_and(lane, size) != 0,
                pltpu.roll(x, size, 1),
                pltpu.roll(x, TILE - size, 1),
            )
        else:
            step = size // TILE
            moved = jnp.concatenate([x[r ^ step : (r ^ step) + 1] for r in range(rows)], 0)
        flag = lax.bitwise_and(lax.shift_right_logical(device, bit), 1)
        x = jnp.where(flag == 1, moved, x)
        size, bit = 2 * size, bit + 1
    return x


def position(n_gz, n_dom):
    dom = lax.axis_index("dom")
    n_z = n_dom // 2
    core, z = lax.bitwise_and(dom, 1), lax.shift_right_logical(dom, 1)
    return (core * n_gz + lax.axis_index("gz")) * n_z + z


def fetch(pairs, sems):
    copies = [pltpu.make_async_copy(a, b, sems.at[n]) for n, (a, b) in enumerate(pairs)]
    for copy in copies:
        copy.start()
    return copies


def pack_kernel(
    planes, observed_hbm, classes_hbm, bins_hbm, volume,
    packed, plane, field, observed, classes, bin_ids, sems,
):
    dom = lax.axis_index("dom")
    after = jnp.minimum((dom + 1) * planes, volume.shape[0] - 1)
    copies = fetch(
        [
            (observed_hbm, observed),
            (classes_hbm, classes),
            (bins_hbm, bin_ids),
            (volume.at[pl.ds(0, 1)], plane),
            (volume.at[pl.ds(dom * planes, planes)], field.at[pl.ds(0, planes)]),
            (volume.at[pl.ds(after, 1)], field.at[pl.ds(planes, 1)]),
        ],
        sems,
    )
    for z in range(planes + 1, field.shape[0]):
        field[z] = jnp.zeros(field.shape[1:], f32)
    for copy in copies[:3]:
        copy.wait()
    count, rows, samples = observed.shape
    values = observed[...].astype(f32)
    for r in range(rows):
        packed[:, r * samples : (r + 1) * samples] = values[:, r, :].astype(bf16)
    diagonal = lanes_of((count, count), 0) == lanes_of((count, count), 1)
    lane = lanes_of((count, TILE), 1)
    tail = jnp.zeros((count, TILE), f32)
    for n, ids in enumerate((classes, bin_ids)):
        column = jnp.where(diagonal, ids[...].astype(f32), 0.0)
        tail = jnp.where(lane == n, jnp.sum(column, axis=1, keepdims=True), tail)
    packed[:, rows * samples :] = tail.astype(bf16)
    for copy in copies[3:]:
        copy.wait()


def extract_kernel(
    groups, length, samples, bins, planes, n_dom,
    table_hbm, trig_hbm, field, above, ctf_hbm, slope, pairs, flat,
    table, trig, ctf, vhi, vlo, out, sems,
):
    depth = field.shape[0]
    xt_count = vhi.shape[0]
    ut_count = samples // TILE
    dom = lax.axis_index("dom")
    device = lax.axis_index("gz") * n_dom + dom
    row = device * length
    first = device * planes
    z0, z1 = first.astype(f32), (first + planes).astype(f32)

    copies = fetch(
        [
            (table_hbm, table),
            (trig_hbm, trig),
            (ctf_hbm, ctf),
        ],
        sems,
    )
    out[...] = jnp.zeros_like(out)
    for copy in copies:
        copy.wait()
    last = dom == n_dom - 1
    for xt in range(xt_count):
        lanes = slice(xt * TILE, (xt + 1) * TILE)
        halo = (lax.broadcasted_iota(jnp.int32, (depth, TILE), 0) == planes) & last
        stacked = jnp.concatenate(
            [jnp.where(halo, above[0, r : r + 1, lanes], field[:, r, lanes]) for r in range(4)], 0
        )
        hi = stacked.astype(bf16)
        vhi[xt] = hi
        vlo[xt] = (stacked - hi.astype(f32)).astype(bf16)

    def step(j, carry):
        xt = table[row + 1 + j]
        hi_rows, lo_rows = vhi[xt], vlo[xt]
        xx = lanes_of((TILE, TILE), 0) + (xt * TILE).astype(f32)
        for k in range(GROUP):
            at = row + 1 + groups + j * GROUP + k
            b, ut, s, c, base = block_of(table, trig, at, bins)
            u = lanes_of((1, TILE), 1) + base
            centre, kz, kzd, z_factor, x_factor = row_weights(z0, depth, u, s, c, samples)
            below = s < 0.0
            place = centre * jnp.where(below, -1.0, 1.0)
            least, most = jnp.where(below, -z1, z0), jnp.where(below, -z0, z1)
            own = jnp.where((place >= least) & (place < most), 1.0, 0.0)
            z_factor, x_factor = z_factor * own, x_factor * own
            weights = jnp.concatenate(bump(xx - u * c), 1)
            whi = weights.astype(bf16)
            wlo = (weights - whi.astype(f32)).astype(bf16)
            sampled = (
                jnp.dot(hi_rows, whi, preferred_element_type=f32)
                + jnp.dot(lo_rows, whi, preferred_element_type=f32)
                + jnp.dot(hi_rows, wlo, preferred_element_type=f32)
            )
            leading, second = [], []
            for r in range(4):
                direct = sampled[r * depth : (r + 1) * depth, :TILE]
                tilted = sampled[r * depth : (r + 1) * depth, TILE:]
                leading.append(own * jnp.sum(direct * kz, axis=0, keepdims=True))
                second.append(
                    z_factor * jnp.sum(direct * kzd, axis=0, keepdims=True)
                    + x_factor * jnp.sum(tilted * kz, axis=0, keepdims=True)
                )
            span = pl.ds(pl.multiple_of((b * ut_count + ut) * 8, 8), 8)
            out[span, :] = out[span, :] + jnp.concatenate(leading + second, 0)
        return carry

    lax.fori_loop(0, table[row], step, 0)

    slope[...] = jnp.zeros_like(slope)
    square, mixed = [], []
    for y in range(2):
        for ut in range(ut_count):
            square_sum, mixed_sum = 0.0, 0.0
            for r in (y, 2 + y):
                direct = out[pl.ds(ut * 8 + r, bins, stride=ut_count * 8), :].astype(bf16).astype(f32)
                tilted = out[pl.ds(ut * 8 + 4 + r, bins, stride=ut_count * 8), :].astype(bf16)
                at = (r * ut_count + ut) * TILE
                slope[bins:, at : at + TILE] = tilted
                tilted = tilted.astype(f32)
                square_sum = square_sum + tilted * tilted
                mixed_sum = mixed_sum - direct * tilted
            square.append(square_sum)
            mixed.append(mixed_sum)
    moments = jnp.concatenate([jnp.concatenate(square, 1), jnp.concatenate(mixed, 1)], 0)
    contrast = jnp.concatenate([ctf[:, 0, :], ctf[:, 1, :]], 1)
    flat[...] = contrast
    product = lax.dot_general(
        contrast * contrast, moments, NT, precision=lax.Precision.HIGHEST, preferred_element_type=f32
    )
    pairs[...] = jnp.concatenate(split3(product), 1)


def particle_kernel(width, mine, n_gz, n_dom, final, *refs):
    blocks = refs[:n_gz]
    if final:
        ctf, slope, pairs, before, weighted, bins_row, parts = refs[n_gz:]
    else:
        ctf, slope, pairs, weighted, bins_row, parts = refs[n_gz:]
    size = blocks[0].shape[0]
    joined = max(1, CHUNK // size)
    both = slope.shape[0]
    bins = both // 2
    flat = ctf[...]
    ctf_hi = flat.astype(bf16)
    ctf_lo = (flat - ctf_hi.astype(f32)).astype(bf16)
    upper = jnp.where(lanes_of((8, both), 1) >= bins, 1.0, 0.0)
    select = jnp.where(lanes_of((8, both), 0) == upper, 1.0, 0.0).astype(bf16)
    select = jnp.concatenate([select] * 3, 1)
    slopes = slope[...]
    scalars = [[], []]

    for i in range(0, n_gz, joined):
        packed = jnp.concatenate([ref[...] for ref in blocks[i : i + joined]], 0)
        count = packed.shape[0]
        span = slice(i * size, i * size + count)
        ids = packed[:, width:]
        classes = ids[:, 0:1].astype(f32)
        onehot_class = jnp.where(lanes_of((count, NCTF), 1) == classes, 1.0, 0.0).astype(bf16)
        bin_of = ids[:, 1:2].astype(f32)
        lane = lanes_of((count, both), 1)
        chosen = (lane == bin_of) | (lane == bin_of + bins)
        contrast = jnp.dot(onehot_class, ctf_hi, preferred_element_type=f32) + jnp.dot(
            onehot_class, ctf_lo, preferred_element_type=f32
        )
        contrast = jnp.concatenate([contrast, contrast], 1)
        w = contrast * packed[:, :width].astype(f32)
        whi = w.astype(bf16)
        wlo = (w - whi.astype(f32)).astype(bf16)
        weighted[span, :] = whi
        along = lax.dot_general(whi, slopes, NT, preferred_element_type=f32) + lax.dot_general(
            wlo, slopes, NT, preferred_element_type=f32
        )
        tables = jnp.dot(onehot_class, pairs[...], preferred_element_type=f32)
        tables = tables[:, :both] + tables[:, both : 2 * both] + tables[:, 2 * both :]
        terms = jnp.concatenate(split3(jnp.where(chosen, along + tables, 0.0)), 1)
        rows = lax.dot_general(select, terms, NT, preferred_element_type=f32)
        for n in range(2):
            for q in range(count // TILE):
                scalars[n].append(rows[n : n + 1, q * TILE : (q + 1) * TILE])
        pick = jnp.where(lanes_of((8, TILE), 1) == 1.0, 1.0, 0.0).astype(bf16)
        bins_row[:, span] = lax.dot_general(pick, ids, NT, preferred_element_type=f32)[0:1]

    if not final:
        parts[...] = jnp.concatenate(scalars[0] + scalars[1], 0)
        return
    half = before.shape[0] // 2
    scalars = jnp.concatenate(
        [before[:half]] + scalars[0] + [before[half:]] + scalars[1], 0
    )
    scalars = reorder(scalars, position(n_gz, n_dom), mine)
    rows = scalars.shape[0]
    for n in range(parts.shape[0] // rows):
        parts[n * rows : (n + 1) * rows, :] = scalars


def weight_kernel(groups, length, bins, planes, n_dom, edge_samples, table, trig, right, edges):
    device = lax.axis_index("gz") * n_dom + lax.axis_index("dom")
    row = device * length
    uu = lanes_of((TILE, TILE), 0)

    def step(j, carry):
        xx = lanes_of((1, TILE), 1) + (table[row + 1 + j] * TILE).astype(f32)
        for k in range(SPREAD_GROUP):
            at = row + 1 + groups + j * SPREAD_GROUP + k
            _, _, _, c, base = block_of(table, trig, at, bins)
            for n, part in enumerate(bump((xx - base * c) - uu * c)):
                right[j, (2 * k + n) * TILE : (2 * k + n + 1) * TILE, :] = part.astype(bf16)
        return carry

    lax.fori_loop(0, table[row], step, 0)
    tail = row + 1 + groups * (1 + SPREAD_GROUP)

    def edge(j, carry):
        for k in range(EDGE_GROUP):
            at = j * EDGE_GROUP + k
            _, _, _, c, _ = block_of(table, trig, tail + 1 + at, bins)
            uu = lanes_of((edge_samples, TILE), 0)
            for n, part in enumerate(bump(lanes_of((1, TILE), 1) - uu * c)):
                edges[at, n * edge_samples : (n + 1) * edge_samples, :] = part.astype(bf16)
        return carry

    lax.fori_loop(0, table[tail], edge, 0)


def spread_kernel(
    groups, length, planes, samples, edge_samples, mine, n_gz, n_dom,
    table, trig, right, edges, parts, bins_own, weighted_own, bins_row, weighted,
    pose, out, sums, total, poses,
):
    tiles, bins = sums.shape[0] // 2, sums.shape[1]
    ut_count = samples // TILE
    depth = total.shape[1] // 4
    half = bins_row.shape[1]
    count = 2 * half
    chunk = min(CHUNK, half)
    device = lax.axis_index("gz") * n_dom + lax.axis_index("dom")
    row = device * length
    z0 = (device * planes).astype(f32)

    rows = count // TILE
    scalars = jnp.sum(parts[...].reshape(parts.shape[0] // (2 * rows), 2 * rows, TILE), axis=0)
    square, pull = scalars[:rows], scalars[rows:]
    curvature = square + EPS
    shift = jnp.zeros_like(square)
    for _ in range(ITERS):
        shift = shift + 0.5 * (pull - shift * square) / curvature
    here = position(n_gz, n_dom)
    poses[...] = shift * jnp.sqrt(curvature)
    first = here * mine
    line = poses[pl.ds(lax.div(first, TILE), 1), :]
    pose[...] = pltpu.roll(line, TILE - lax.rem(first, TILE), 1)[:, :mine]
    shift = reorder(jnp.concatenate([shift, shift], 0), here, mine)
    shift = jnp.concatenate([shift[q : q + 1] for q in range(rows)], 1)

    bin_sums = jnp.zeros((3 * bins, tiles * TILE), f32)
    for i in range(count // chunk):
        ids, values = (bins_own, weighted_own) if i * chunk < half else (bins_row, weighted)
        span = slice(i * chunk % half, i * chunk % half + chunk)
        belongs = lanes_of((bins, chunk), 0) == ids[:, span]
        scaled = jnp.where(belongs, shift[:, i * chunk : (i + 1) * chunk], 0.0)
        hi = scaled.astype(bf16)
        lo = (scaled - hi.astype(f32)).astype(bf16)
        onehot = jnp.where(belongs, 1.0, 0.0).astype(bf16)
        bin_sums = bin_sums + jnp.dot(
            jnp.concatenate([onehot, hi, lo], 0), values[span, :], preferred_element_type=f32
        )
    plain = bin_sums[:bins]
    slope_sum = bin_sums[bins : 2 * bins] + bin_sums[2 * bins :]
    for q in range(tiles):
        sums[q] = plain[:, q * TILE : (q + 1) * TILE]
        sums[tiles + q] = slope_sum[:, q * TILE : (q + 1) * TILE]
    total[...] = jnp.zeros_like(total)

    def step(j, carry):
        xt = table[row + 1 + j]
        left = []
        for k in range(SPREAD_GROUP):
            at = row + 1 + groups + j * SPREAD_GROUP + k
            b, ut, s, c, base = block_of(table, trig, at, bins)
            u = lanes_of((1, TILE), 1) + base
            _, kz, kzd, z_factor, x_factor = row_weights(z0, depth, u, s, c, samples)
            first, second = [], []
            for r in range(4):
                direct = sums[r * ut_count + ut, pl.ds(b, 1), :]
                tilted = sums[tiles + r * ut_count + ut, pl.ds(b, 1), :]
                first.append(kz * direct + kzd * (tilted * z_factor))
                second.append(kz * (tilted * x_factor))
            left += [jnp.concatenate(first, 0), jnp.concatenate(second, 0)]
        left = jnp.concatenate(left, 1)
        hi = left.astype(bf16)
        lo = (left - hi.astype(f32)).astype(bf16)
        both = jnp.dot(
            jnp.concatenate([hi, lo], 0), right[j], preferred_element_type=f32
        )
        total[xt] = total[xt] + both[: 4 * depth] + both[4 * depth :]
        return carry

    lax.fori_loop(0, table[row], step, 0)
    tail = row + 1 + groups * (1 + SPREAD_GROUP)

    def edge(j, carry):
        left, below = [], []
        rest = jnp.zeros((TILE - edge_samples, TILE), bf16)
        for k in range(EDGE_GROUP):
            b, _, s, c, _ = block_of(table, trig, tail + 1 + j * EDGE_GROUP + k, bins)
            u = lanes_of((1, TILE), 1)
            _, kz, kzd, z_factor, x_factor = row_weights(z0, 1, u, s, c, samples)
            direct = jnp.concatenate(
                [sums[r * ut_count, pl.ds(b, 1), :] for r in range(4)], 0
            )
            tilted = jnp.concatenate(
                [sums[tiles + r * ut_count, pl.ds(b, 1), :] for r in range(4)], 0
            )
            left += [kz * direct + (kzd * z_factor) * tilted, (kz * x_factor) * tilted]
            part = edges[j * EDGE_GROUP + k]
            below += [part[:edge_samples], rest, part[edge_samples:], rest]
        left = jnp.concatenate(left, 1)
        hi = left.astype(bf16).astype(f32)
        split = jnp.concatenate([hi, left - hi], 0).astype(bf16)
        both = jnp.dot(split, jnp.concatenate(below, 0), preferred_element_type=f32)
        return carry + both[:4] + both[4:]

    extra = lax.fori_loop(0, table[tail], edge, jnp.zeros((4, TILE), f32))
    for xt in range(total.shape[0]):
        for r in range(4):
            out[:, r, xt * TILE : (xt + 1) * TILE] = total[xt, r * depth : r * depth + planes, :]
    out[0, :, :TILE] = out[0, :, :TILE] + extra


def swap(x, axis, size, distance):
    return lax.ppermute(x, axis, [(i, i ^ distance) for i in range(size)])


def local(volume, observed, ctf_table, ctf_class, bin_ids):
    slab, rows, columns = volume.shape
    mine, _, samples = observed.shape
    n_gz, n_dom = lax.axis_size("gz"), lax.axis_size("dom")
    devices = n_gz * n_dom
    bins = NB_DEV * n_dom
    planes = NZ // devices
    count = mine * devices
    width = rows * samples
    xt_count, ut_count = columns // TILE, samples // TILE
    smem = pl.BlockSpec(memory_space=pltpu.SMEM)
    vmem = pl.BlockSpec(memory_space=pltpu.VMEM)
    hbm = pl.BlockSpec(memory_space=pltpu.HBM)
    wide = pltpu.CompilerParams(vmem_limit_bytes=60 * 2**20)
    params = pltpu.CompilerParams(vmem_limit_bytes=min(56, 19 + 37 * count // 4096) * 2**20)
    extract_plan, spread_plan, edge_samples, trig = make_plan(devices, bins, samples, columns)
    trig = jnp.asarray(trig)
    depth_in = round_up(planes + 1, 8)
    packed, plane, field = pl.pallas_call(
        functools.partial(pack_kernel, planes),
        out_shape=[
            jax.ShapeDtypeStruct((mine, width + TILE), bf16),
            jax.ShapeDtypeStruct((1, rows, columns), f32),
            jax.ShapeDtypeStruct((depth_in, rows, columns), f32),
        ],
        in_specs=[hbm] * 4,
        out_specs=[vmem] * 3,
        scratch_shapes=[
            pltpu.VMEM(observed.shape, bf16),
            pltpu.VMEM((1, mine), jnp.int32),
            pltpu.VMEM((1, mine), jnp.int32),
            pltpu.SemaphoreType.DMA((6,)),
        ],
        compiler_params=wide,
        name="pack",
    )(observed, ctf_class.reshape(1, mine), bin_ids.reshape(1, mine), volume)

    n_z = n_dom // 2
    above = lax.ppermute(plane, "gz", [(i, i - 1) for i in range(1, n_gz)])
    column = jnp.concatenate(
        [packed] + [swap(packed, "dom", n_dom, 2 * k) for k in range(1, n_z)], 0
    )
    spread_table, spread_groups = spread_plan
    spread_table_flat = jnp.asarray(spread_table.reshape(-1))
    right, edges = pl.pallas_call(
        functools.partial(
            weight_kernel, spread_groups, spread_table.shape[1], bins, planes, n_dom, edge_samples
        ),
        out_shape=[
            jax.ShapeDtypeStruct((spread_groups, SPREAD_GROUP * 2 * TILE, TILE), bf16),
            jax.ShapeDtypeStruct((bins // 2, 2 * edge_samples, TILE), bf16),
        ],
        in_specs=[smem, smem],
        out_specs=[vmem, vmem],
        compiler_params=params,
        cost_estimate=pl.CostEstimate(flops=3 * 10**9, bytes_accessed=2**21, transcendentals=0),
        name="weights",
    )(spread_table_flat, trig)
    column, trig, right, edges = lax.optimization_barrier((column, trig, right, edges))
    planes_of = [column] + [swap(column, "gz", n_gz, j) for j in range(1, n_gz)]


    table, groups = extract_plan
    slope, pairs, flat_ctf = pl.pallas_call(
        functools.partial(
            extract_kernel, groups, table.shape[1], samples, bins, planes, n_dom
        ),
        out_shape=[
            jax.ShapeDtypeStruct((2 * bins, width), bf16),
            jax.ShapeDtypeStruct((NCTF, 6 * bins), bf16),
            jax.ShapeDtypeStruct((NCTF, width // 2), f32),
        ],
        in_specs=[hbm, hbm, vmem, vmem, hbm],
        out_specs=[vmem, vmem, vmem],
        scratch_shapes=[
            pltpu.SMEM((table.size,), jnp.int32),
            pltpu.SMEM(trig.shape, f32),
            pltpu.VMEM(ctf_table.shape, f32),
            pltpu.VMEM((xt_count, rows * depth_in, TILE), bf16),
            pltpu.VMEM((xt_count, rows * depth_in, TILE), bf16),
            pltpu.VMEM((bins * ut_count * 2 * rows, TILE), f32),
            pltpu.SemaphoreType.DMA((3,)),
        ],
        compiler_params=params,
        cost_estimate=pl.CostEstimate(flops=6 * 10**9, bytes_accessed=2**20, transcendentals=0),
        name="extract",
    )(jnp.asarray(table.reshape(-1)), trig, field, above, ctf_table)

    planes_of, slope = lax.optimization_barrier((planes_of, slope))
    others = [swap(part, "dom", n_dom, 1) for part in planes_of]
    per_device = 2 * count // TILE

    def particles(blocks, before):
        final = len(before) > 0
        return pl.pallas_call(
            functools.partial(particle_kernel, width, mine, n_gz, n_dom, final),
            out_shape=[
                jax.ShapeDtypeStruct((count // 2, width), bf16),
                jax.ShapeDtypeStruct((1, count // 2), f32),
                jax.ShapeDtypeStruct(
                    (devices * per_device if final else per_device // 2, TILE), f32
                ),
            ],
            in_specs=[vmem] * (len(blocks) + 3 + len(before)),
            out_specs=[vmem] * 3,
            compiler_params=params,
            cost_estimate=pl.CostEstimate(
                flops=2 * 10**9, bytes_accessed=2**20, transcendentals=0
            ),
            name="particles",
        )(*blocks, flat_ctf, slope, pairs, *before)

    weighted_own, bins_own, before = particles(planes_of, [])
    weighted, bins_row, parts = particles(others, [before])

    parts = lax.all_to_all(parts, ("gz", "dom"), 0, 0, tiled=True)

    depth = round_up(planes, 8)
    pose, spread = pl.pallas_call(
        functools.partial(
            spread_kernel, spread_groups, spread_table.shape[1], planes, samples, edge_samples, mine, n_gz, n_dom
        ),
        out_shape=[
            jax.ShapeDtypeStruct((1, mine), f32),
            jax.ShapeDtypeStruct((planes, rows, columns), f32),
        ],
        in_specs=[smem, smem] + [vmem] * 7,
        out_specs=[vmem, vmem],
        scratch_shapes=[
            pltpu.VMEM((2 * width // TILE, bins, TILE), f32),
            pltpu.VMEM((xt_count, rows * depth, TILE), f32),
            pltpu.VMEM((count // TILE, TILE), f32),
        ],
        compiler_params=params,
        name="spread",
    )(
        spread_table_flat, trig, right, edges, parts, bins_own, weighted_own, bins_row, weighted
    )
    pose = pose.reshape(mine)
    return pose, spread


def solution(mesh):
    return jax.shard_map(
        local,
        mesh=mesh,
        in_specs=(
            P("gz", None, None),
            P(("gz", "dom"), None, None),
            P(),
            P(("gz", "dom")),
            P(("gz", "dom")),
        ),
        out_specs=(P(("gz", "dom")), P(("gz", "dom"), None, None)),
        check_vma=False,
    )
```

```python
import functools
import math

import jax
import jax.numpy as jnp
import numpy as np
from jax import lax
from jax.experimental import pallas as pl
from jax.experimental.pallas import tpu as pltpu
from jax.sharding import PartitionSpec as P

NZ = 768
NB_DEV = 8
NCTF = 32
ITERS = 3
EPS = 1e-05
TILE = 128
GROUP = 8
SPREAD_GROUP = 8
EDGE_GROUP = 8
CHUNK = 512
f32 = jnp.float32
bf16 = jnp.bfloat16
NT = (((1,), (1,)), ((), ()))


def round_up(n, m):
    return -(-n // m) * m


def make_plan(devices, bins, samples, columns):
    planes = NZ // devices
    middle = NZ // 2
    ut_count, xt_count = samples // TILE, columns // TILE
    theta = -0.5 * math.pi + math.pi * (np.arange(bins) + 0.5) / bins
    trig = np.concatenate([np.sin(theta), np.cos(theta)]).astype(np.float32)
    u = np.arange(samples)
    slack = 1e-3
    reach = 0
    plans = []
    for spread, size in ((False, GROUP), (True, SPREAD_GROUP)):
        rows = []
        for device in range(devices):
            z0 = device * planes
            z1 = z0 + planes
            lists = [[] for _ in range(xt_count)]
            edge = []
            for b in range(bins):
                s, c = math.sin(theta[b]), math.cos(theta[b])
                centre = middle + u * s
                near = (centre > z0 - slack - (1 if spread else 0)) & (centre < z1 + slack)
                if spread:
                    near[0] = z0 - 1 < middle < z1
                else:
                    near[0] = z0 <= middle < z1 if s > 0 else z0 < middle <= z1
                if not near.any():
                    continue
                if spread and s < 0 and z0 == middle:
                    edge.append(b * 4)
                    reach = max(reach, int(u[near].max()) + 1)
                    continue
                for ut in range(ut_count):
                    hit = u[ut * TILE : (ut + 1) * TILE][near[ut * TILE : (ut + 1) * TILE]]
                    if hit.size == 0:
                        continue
                    first = max(0, int((hit.min() * c - 1.01) // TILE))
                    last = min(xt_count - 1, int((hit.max() * c + 1.01) // TILE))
                    for xt in range(first, last + 1):
                        lists[xt].append(b * 4 + ut)
            idle = (bins - 1 if z0 < middle else 0) * 4 + ut_count - 1
            tiles, codes = [], []
            for xt, entries in enumerate(lists):
                entries = entries + [idle] * (-len(entries) % size)
                tiles += [xt] * (len(entries) // size)
                codes += entries
            rows.append((tiles, codes, edge))
        groups = max(len(tiles) for tiles, _, _ in rows)
        start = 1 + groups * (1 + size)
        table = np.zeros((devices, start + 1 + max(len(edge) for _, _, edge in rows)), np.int32)
        for device, (tiles, codes, edge) in enumerate(rows):
            table[device, 0] = len(tiles)
            table[device, 1 : 1 + len(tiles)] = tiles
            table[device, 1 + groups : 1 + groups + len(codes)] = codes
            table[device, start] = len(edge) // EDGE_GROUP
            table[device, start + 1 : start + 1 + len(edge)] = edge
        plans.append((table, groups))
    edge_samples = round_up(reach, 16)
    assert edge_samples <= TILE and (bins // 2) % EDGE_GROUP == 0
    return plans[0], plans[1], edge_samples, trig


def lanes_of(shape, axis):
    return lax.broadcasted_iota(jnp.int32, shape, axis).astype(f32)


def block_of(table, trig, at, bins):
    code = table[at]
    b = lax.shift_right_logical(code, 2)
    ut = lax.bitwise_and(code, 3)
    return b, ut, trig[b], trig[bins + b], (ut * TILE).astype(f32)


def split3(x):
    hi = x.astype(bf16)
    rest = x - hi.astype(f32)
    mid = rest.astype(bf16)
    return [hi, mid, (rest - mid.astype(f32)).astype(bf16)]


def bump(t):
    falloff = jnp.maximum(1.0 - t * t, 0.0)
    return falloff * falloff, t * falloff


def row_weights(z0, rows, u, s, c, samples):
    centre = 0.5 * NZ + u * s
    kz, kzd = bump((z0 + lanes_of((rows, TILE), 0)) - centre)
    return centre, kz, kzd, u * (c * (4.0 / samples)), u * (s * (-4.0 / samples))


def reorder(x, device, mine):
    lane = lax.broadcasted_iota(jnp.int32, x.shape, 1)
    rows = x.shape[0]
    size = mine
    bit = 0
    while size < rows // 2 * TILE:
        if size < TILE:
            moved = jnp.where(
                lax.bitwise_and(lane, size) != 0,
                pltpu.roll(x, size, 1),
                pltpu.roll(x, TILE - size, 1),
            )
        else:
            step = size // TILE
            moved = jnp.concatenate([x[r ^ step : (r ^ step) + 1] for r in range(rows)], 0)
        flag = lax.bitwise_and(lax.shift_right_logical(device, bit), 1)
        x = jnp.where(flag == 1, moved, x)
        size, bit = 2 * size, bit + 1
    return x


def position(n_gz, n_dom):
    dom = lax.axis_index("dom")
    n_z = n_dom // 2
    core, z = lax.bitwise_and(dom, 1), lax.shift_right_logical(dom, 1)
    return (core * n_gz + lax.axis_index("gz")) * n_z + z


def fetch(pairs, sems):
    copies = [pltpu.make_async_copy(a, b, sems.at[n]) for n, (a, b) in enumerate(pairs)]
    for copy in copies:
        copy.start()
    return copies


def pack_kernel(
    planes, observed_hbm, classes_hbm, bins_hbm, volume,
    packed, plane, field, observed, classes, bin_ids, sems,
):
    dom = lax.axis_index("dom")
    after = jnp.minimum((dom + 1) * planes, volume.shape[0] - 1)
    copies = fetch(
        [
            (observed_hbm, observed),
            (classes_hbm, classes),
            (bins_hbm, bin_ids),
            (volume.at[pl.ds(0, 1)], plane),
            (volume.at[pl.ds(dom * planes, planes)], field.at[pl.ds(0, planes)]),
            (volume.at[pl.ds(after, 1)], field.at[pl.ds(planes, 1)]),
        ],
        sems,
    )
    for z in range(planes + 1, field.shape[0]):
        field[z] = jnp.zeros(field.shape[1:], f32)
    for copy in copies[:3]:
        copy.wait()
    count, rows, samples = observed.shape
    values = observed[...].astype(f32)
    for r in range(rows):
        packed[:, r * samples : (r + 1) * samples] = values[:, r, :].astype(bf16)
    diagonal = lanes_of((count, count), 0) == lanes_of((count, count), 1)
    lane = lanes_of((count, TILE), 1)
    tail = jnp.zeros((count, TILE), f32)
    for n, ids in enumerate((classes, bin_ids)):
        column = jnp.where(diagonal, ids[...].astype(f32), 0.0)
        tail = jnp.where(lane == n, jnp.sum(column, axis=1, keepdims=True), tail)
    packed[:, rows * samples :] = tail.astype(bf16)
    for copy in copies[3:]:
        copy.wait()


def extract_kernel(
    groups, length, samples, bins, planes, n_dom,
    table_hbm, trig_hbm, field, above, ctf_hbm, slope, pairs, flat,
    table, trig, ctf, vhi, vlo, out, sems,
):
    depth = field.shape[0]
    xt_count = vhi.shape[0]
    ut_count = samples // TILE
    dom = lax.axis_index("dom")
    device = lax.axis_index("gz") * n_dom + dom
    row = device * length
    first = device * planes
    z0, z1 = first.astype(f32), (first + planes).astype(f32)

    copies = fetch(
        [
            (table_hbm, table),
            (trig_hbm, trig),
            (ctf_hbm, ctf),
        ],
        sems,
    )
    out[...] = jnp.zeros_like(out)
    for copy in copies:
        copy.wait()
    last = dom == n_dom - 1
    for xt in range(xt_count):
        lanes = slice(xt * TILE, (xt + 1) * TILE)
        halo = (lax.broadcasted_iota(jnp.int32, (depth, TILE), 0) == planes) & last
        stacked = jnp.concatenate(
            [jnp.where(halo, above[0, r : r + 1, lanes], field[:, r, lanes]) for r in range(4)], 0
        )
        hi = stacked.astype(bf16)
        vhi[xt] = hi
        vlo[xt] = (stacked - hi.astype(f32)).astype(bf16)

    def step(j, carry):
        xt = table[row + 1 + j]
        hi_rows, lo_rows = vhi[xt], vlo[xt]
        xx = lanes_of((TILE, TILE), 0) + (xt * TILE).astype(f32)
        for k in range(GROUP):
            at = row + 1 + groups + j * GROUP + k
            b, ut, s, c, base = block_of(table, trig, at, bins)
            u = lanes_of((1, TILE), 1) + base
            centre, kz, kzd, z_factor, x_factor = row_weights(z0, depth, u, s, c, samples)
            below = s < 0.0
            place = centre * jnp.where(below, -1.0, 1.0)
            least, most = jnp.where(below, -z1, z0), jnp.where(below, -z0, z1)
            own = jnp.where((place >= least) & (place < most), 1.0, 0.0)
            z_factor, x_factor = z_factor * own, x_factor * own
            weights = jnp.concatenate(bump(xx - u * c), 1)
            whi = weights.astype(bf16)
            wlo = (weights - whi.astype(f32)).astype(bf16)
            sampled = (
                jnp.dot(hi_rows, whi, preferred_element_type=f32)
                + jnp.dot(lo_rows, whi, preferred_element_type=f32)
                + jnp.dot(hi_rows, wlo, preferred_element_type=f32)
            )
            leading, second = [], []
            for r in range(4):
                direct = sampled[r * depth : (r + 1) * depth, :TILE]
                tilted = sampled[r * depth : (r + 1) * depth, TILE:]
                leading.append(own * jnp.sum(direct * kz, axis=0, keepdims=True))
                second.append(
                    z_factor * jnp.sum(direct * kzd, axis=0, keepdims=True)
                    + x_factor * jnp.sum(tilted * kz, axis=0, keepdims=True)
                )
            span = pl.ds(pl.multiple_of((b * ut_count + ut) * 8, 8), 8)
            out[span, :] = out[span, :] + jnp.concatenate(leading + second, 0)
        return carry

    lax.fori_loop(0, table[row], step, 0)

    slope[...] = jnp.zeros_like(slope)
    square, mixed = [], []
    for y in range(2):
        for ut in range(ut_count):
            square_sum, mixed_sum = 0.0, 0.0
            for r in (y, 2 + y):
                direct = out[pl.ds(ut * 8 + r, bins, stride=ut_count * 8), :].astype(bf16).astype(f32)
                tilted = out[pl.ds(ut * 8 + 4 + r, bins, stride=ut_count * 8), :].astype(bf16)
                at = (r * ut_count + ut) * TILE
                slope[bins:, at : at + TILE] = tilted
                tilted = tilted.astype(f32)
                square_sum = square_sum + tilted * tilted
                mixed_sum = mixed_sum - direct * tilted
            square.append(square_sum)
            mixed.append(mixed_sum)
    moments = jnp.concatenate([jnp.concatenate(square, 1), jnp.concatenate(mixed, 1)], 0)
    contrast = jnp.concatenate([ctf[:, 0, :], ctf[:, 1, :]], 1)
    flat[...] = contrast
    product = lax.dot_general(
        contrast * contrast, moments, NT, precision=lax.Precision.HIGHEST, preferred_element_type=f32
    )
    pairs[...] = jnp.concatenate(split3(product), 1)


def particle_kernel(width, mine, n_gz, n_dom, final, *refs):
    blocks = refs[:n_gz]
    if final:
        ctf, slope, pairs, before, weighted, bins_row, parts = refs[n_gz:]
    else:
        ctf, slope, pairs, weighted, bins_row, parts = refs[n_gz:]
    size = blocks[0].shape[0]
    joined = max(1, CHUNK // size)
    both = slope.shape[0]
    bins = both // 2
    flat = ctf[...]
    ctf_hi = flat.astype(bf16)
    ctf_lo = (flat - ctf_hi.astype(f32)).astype(bf16)
    upper = jnp.where(lanes_of((8, both), 1) >= bins, 1.0, 0.0)
    select = jnp.where(lanes_of((8, both), 0) == upper, 1.0, 0.0).astype(bf16)
    select = jnp.concatenate([select] * 3, 1)
    slopes = slope[...]
    scalars = [[], []]

    for i in range(0, n_gz, joined):
        packed = jnp.concatenate([ref[...] for ref in blocks[i : i + joined]], 0)
        count = packed.shape[0]
        span = slice(i * size, i * size + count)
        ids = packed[:, width:]
        classes = ids[:, 0:1].astype(f32)
        onehot_class = jnp.where(lanes_of((count, NCTF), 1) == classes, 1.0, 0.0).astype(bf16)
        bin_of = ids[:, 1:2].astype(f32)
        lane = lanes_of((count, both), 1)
        chosen = (lane == bin_of) | (lane == bin_of + bins)
        contrast = jnp.dot(onehot_class, ctf_hi, preferred_element_type=f32) + jnp.dot(
            onehot_class, ctf_lo, preferred_element_type=f32
        )
        contrast = jnp.concatenate([contrast, contrast], 1)
        w = contrast * packed[:, :width].astype(f32)
        whi = w.astype(bf16)
        wlo = (w - whi.astype(f32)).astype(bf16)
        weighted[span, :] = whi
        along = lax.dot_general(whi, slopes, NT, preferred_element_type=f32) + lax.dot_general(
            wlo, slopes, NT, preferred_element_type=f32
        )
        tables = jnp.dot(onehot_class, pairs[...], preferred_element_type=f32)
        tables = tables[:, :both] + tables[:, both : 2 * both] + tables[:, 2 * both :]
        terms = jnp.concatenate(split3(jnp.where(chosen, along + tables, 0.0)), 1)
        rows = lax.dot_general(select, terms, NT, preferred_element_type=f32)
        for n in range(2):
            for q in range(count // TILE):
                scalars[n].append(rows[n : n + 1, q * TILE : (q + 1) * TILE])
        pick = jnp.where(lanes_of((8, TILE), 1) == 1.0, 1.0, 0.0).astype(bf16)
        bins_row[:, span] = lax.dot_general(pick, ids, NT, preferred_element_type=f32)[0:1]

    if not final:
        parts[...] = jnp.concatenate(scalars[0] + scalars[1], 0)
        return
    half = before.shape[0] // 2
    scalars = jnp.concatenate(
        [before[:half]] + scalars[0] + [before[half:]] + scalars[1], 0
    )
    scalars = reorder(scalars, position(n_gz, n_dom), mine)
    rows = scalars.shape[0]
    for n in range(parts.shape[0] // rows):
        parts[n * rows : (n + 1) * rows, :] = scalars


class Codes:
    def __init__(self, ref, start):
        self.ref, self.start = ref, start

    def __getitem__(self, at):
        return self.ref[self.start + at].astype(jnp.int32)


def weight_kernel(groups, length, bins, planes, n_dom, edge_samples, trig, right, edges):
    table = Codes(trig, 2 * bins)
    device = lax.axis_index("gz") * n_dom + lax.axis_index("dom")
    row = device * length
    uu = lanes_of((TILE, TILE), 0)

    def step(j, carry):
        xx = lanes_of((1, TILE), 1) + (table[row + 1 + j] * TILE).astype(f32)
        for k in range(SPREAD_GROUP):
            at = row + 1 + groups + j * SPREAD_GROUP + k
            _, _, _, c, base = block_of(table, trig, at, bins)
            for n, part in enumerate(bump((xx - base * c) - uu * c)):
                right[j, (2 * k + n) * TILE : (2 * k + n + 1) * TILE, :] = part.astype(bf16)
        return carry

    lax.fori_loop(0, table[row], step, 0)
    tail = row + 1 + groups * (1 + SPREAD_GROUP)

    def edge(j, carry):
        for k in range(EDGE_GROUP):
            at = j * EDGE_GROUP + k
            _, _, _, c, _ = block_of(table, trig, tail + 1 + at, bins)
            uu = lanes_of((edge_samples, TILE), 0)
            for n, part in enumerate(bump(lanes_of((1, TILE), 1) - uu * c)):
                edges[at, n * edge_samples : (n + 1) * edge_samples, :] = part.astype(bf16)
        return carry

    lax.fori_loop(0, table[tail], edge, 0)


def spread_kernel(
    groups, length, planes, samples, edge_samples, mine, n_gz, n_dom,
    table, trig, right, edges, parts, bins_own, weighted_own, bins_row, weighted,
    pose, out, sums, total, poses,
):
    tiles, bins = sums.shape[0] // 2, sums.shape[1]
    ut_count = samples // TILE
    depth = total.shape[1] // 4
    half = bins_row.shape[1]
    count = 2 * half
    chunk = min(CHUNK, half)
    device = lax.axis_index("gz") * n_dom + lax.axis_index("dom")
    row = device * length
    z0 = (device * planes).astype(f32)

    rows = count // TILE
    scalars = jnp.sum(parts[...].reshape(parts.shape[0] // (2 * rows), 2 * rows, TILE), axis=0)
    square, pull = scalars[:rows], scalars[rows:]
    curvature = square + EPS
    shift = jnp.zeros_like(square)
    for _ in range(ITERS):
        shift = shift + 0.5 * (pull - shift * square) / curvature
    here = position(n_gz, n_dom)
    poses[...] = shift * jnp.sqrt(curvature)
    first = here * mine
    line = poses[pl.ds(lax.div(first, TILE), 1), :]
    pose[...] = pltpu.roll(line, TILE - lax.rem(first, TILE), 1)[:, :mine]
    shift = reorder(jnp.concatenate([shift, shift], 0), here, mine)
    shift = jnp.concatenate([shift[q : q + 1] for q in range(rows)], 1)

    bin_sums = jnp.zeros((3 * bins, tiles * TILE), f32)
    for i in range(count // chunk):
        ids, values = (bins_own, weighted_own) if i * chunk < half else (bins_row, weighted)
        span = slice(i * chunk % half, i * chunk % half + chunk)
        belongs = lanes_of((bins, chunk), 0) == ids[:, span]
        scaled = jnp.where(belongs, shift[:, i * chunk : (i + 1) * chunk], 0.0)
        hi = scaled.astype(bf16)
        lo = (scaled - hi.astype(f32)).astype(bf16)
        onehot = jnp.where(belongs, 1.0, 0.0).astype(bf16)
        bin_sums = bin_sums + jnp.dot(
            jnp.concatenate([onehot, hi, lo], 0), values[span, :], preferred_element_type=f32
        )
    plain = bin_sums[:bins]
    slope_sum = bin_sums[bins : 2 * bins] + bin_sums[2 * bins :]
    for q in range(tiles):
        sums[q] = plain[:, q * TILE : (q + 1) * TILE]
        sums[tiles + q] = slope_sum[:, q * TILE : (q + 1) * TILE]
    total[...] = jnp.zeros_like(total)

    def step(j, carry):
        xt = table[row + 1 + j]
        left = []
        for k in range(SPREAD_GROUP):
            at = row + 1 + groups + j * SPREAD_GROUP + k
            b, ut, s, c, base = block_of(table, trig, at, bins)
            u = lanes_of((1, TILE), 1) + base
            _, kz, kzd, z_factor, x_factor = row_weights(z0, depth, u, s, c, samples)
            first, second = [], []
            for r in range(4):
                direct = sums[r * ut_count + ut, pl.ds(b, 1), :]
                tilted = sums[tiles + r * ut_count + ut, pl.ds(b, 1), :]
                first.append(kz * direct + kzd * (tilted * z_factor))
                second.append(kz * (tilted * x_factor))
            left += [jnp.concatenate(first, 0), jnp.concatenate(second, 0)]
        left = jnp.concatenate(left, 1)
        hi = left.astype(bf16)
        lo = (left - hi.astype(f32)).astype(bf16)
        both = jnp.dot(
            jnp.concatenate([hi, lo], 0), right[j], preferred_element_type=f32
        )
        total[xt] = total[xt] + both[: 4 * depth] + both[4 * depth :]
        return carry

    lax.fori_loop(0, table[row], step, 0)
    tail = row + 1 + groups * (1 + SPREAD_GROUP)

    def edge(j, carry):
        left, below = [], []
        rest = jnp.zeros((TILE - edge_samples, TILE), bf16)
        for k in range(EDGE_GROUP):
            b, _, s, c, _ = block_of(table, trig, tail + 1 + j * EDGE_GROUP + k, bins)
            u = lanes_of((1, TILE), 1)
            _, kz, kzd, z_factor, x_factor = row_weights(z0, 1, u, s, c, samples)
            direct = jnp.concatenate(
                [sums[r * ut_count, pl.ds(b, 1), :] for r in range(4)], 0
            )
            tilted = jnp.concatenate(
                [sums[tiles + r * ut_count, pl.ds(b, 1), :] for r in range(4)], 0
            )
            left += [kz * direct + (kzd * z_factor) * tilted, (kz * x_factor) * tilted]
            part = edges[j * EDGE_GROUP + k]
            below += [part[:edge_samples], rest, part[edge_samples:], rest]
        left = jnp.concatenate(left, 1)
        hi = left.astype(bf16).astype(f32)
        split = jnp.concatenate([hi, left - hi], 0).astype(bf16)
        both = jnp.dot(split, jnp.concatenate(below, 0), preferred_element_type=f32)
        return carry + both[:4] + both[4:]

    extra = lax.fori_loop(0, table[tail], edge, jnp.zeros((4, TILE), f32))
    for xt in range(total.shape[0]):
        for r in range(4):
            out[:, r, xt * TILE : (xt + 1) * TILE] = total[xt, r * depth : r * depth + planes, :]
    out[0, :, :TILE] = out[0, :, :TILE] + extra


def swap(x, axis, size, distance):
    return lax.ppermute(x, axis, [(i, i ^ distance) for i in range(size)])


def local(volume, observed, ctf_table, ctf_class, bin_ids):
    slab, rows, columns = volume.shape
    mine, _, samples = observed.shape
    n_gz, n_dom = lax.axis_size("gz"), lax.axis_size("dom")
    devices = n_gz * n_dom
    bins = NB_DEV * n_dom
    planes = NZ // devices
    count = mine * devices
    width = rows * samples
    xt_count, ut_count = columns // TILE, samples // TILE
    smem = pl.BlockSpec(memory_space=pltpu.SMEM)
    vmem = pl.BlockSpec(memory_space=pltpu.VMEM)
    hbm = pl.BlockSpec(memory_space=pltpu.HBM)
    wide = pltpu.CompilerParams(vmem_limit_bytes=60 * 2**20)
    params = pltpu.CompilerParams(vmem_limit_bytes=min(56, 19 + 37 * count // 4096) * 2**20)
    extract_plan, spread_plan, edge_samples, trig = make_plan(devices, bins, samples, columns)
    trig = jnp.asarray(trig)
    depth_in = round_up(planes + 1, 8)
    packed, plane, field = pl.pallas_call(
        functools.partial(pack_kernel, planes),
        out_shape=[
            jax.ShapeDtypeStruct((mine, width + TILE), bf16),
            jax.ShapeDtypeStruct((1, rows, columns), f32),
            jax.ShapeDtypeStruct((depth_in, rows, columns), f32),
        ],
        in_specs=[hbm] * 4,
        out_specs=[vmem] * 3,
        scratch_shapes=[
            pltpu.VMEM(observed.shape, bf16),
            pltpu.VMEM((1, mine), jnp.int32),
            pltpu.VMEM((1, mine), jnp.int32),
            pltpu.SemaphoreType.DMA((6,)),
        ],
        compiler_params=wide,
        name="pack",
    )(observed, ctf_class.reshape(1, mine), bin_ids.reshape(1, mine), volume)

    n_z = n_dom // 2
    above = lax.ppermute(plane, "gz", [(i, i - 1) for i in range(1, n_gz)])
    column = jnp.concatenate(
        [packed] + [swap(packed, "dom", n_dom, 2 * k) for k in range(1, n_z)], 0
    )
    spread_table, spread_groups = spread_plan
    spread_table_flat = jnp.asarray(spread_table.reshape(-1))
    right, edges = pl.pallas_call(
        functools.partial(
            weight_kernel, spread_groups, spread_table.shape[1], bins, planes, n_dom, edge_samples
        ),
        out_shape=[
            jax.ShapeDtypeStruct((spread_groups, SPREAD_GROUP * 2 * TILE, TILE), bf16),
            jax.ShapeDtypeStruct((bins // 2, 2 * edge_samples, TILE), bf16),
        ],
        in_specs=[smem],
        out_specs=[vmem, vmem],
        compiler_params=params,
        cost_estimate=pl.CostEstimate(flops=3 * 10**9, bytes_accessed=2**21, transcendentals=0),
        name="weights",
    )(jnp.concatenate([trig, spread_table_flat.astype(f32)]))
    column, trig, right, edges = lax.optimization_barrier((column, trig, right, edges))
    planes_of = [column] + [swap(column, "gz", n_gz, j) for j in range(1, n_gz)]


    table, groups = extract_plan
    slope, pairs, flat_ctf = pl.pallas_call(
        functools.partial(
            extract_kernel, groups, table.shape[1], samples, bins, planes, n_dom
        ),
        out_shape=[
            jax.ShapeDtypeStruct((2 * bins, width), bf16),
            jax.ShapeDtypeStruct((NCTF, 6 * bins), bf16),
            jax.ShapeDtypeStruct((NCTF, width // 2), f32),
        ],
        in_specs=[hbm, hbm, vmem, vmem, hbm],
        out_specs=[vmem, vmem, vmem],
        scratch_shapes=[
            pltpu.SMEM((table.size,), jnp.int32),
            pltpu.SMEM(trig.shape, f32),
            pltpu.VMEM(ctf_table.shape, f32),
            pltpu.VMEM((xt_count, rows * depth_in, TILE), bf16),
            pltpu.VMEM((xt_count, rows * depth_in, TILE), bf16),
            pltpu.VMEM((bins * ut_count * 2 * rows, TILE), f32),
            pltpu.SemaphoreType.DMA((3,)),
        ],
        compiler_params=params,
        cost_estimate=pl.CostEstimate(flops=6 * 10**9, bytes_accessed=2**20, transcendentals=0),
        name="extract",
    )(jnp.asarray(table.reshape(-1)), trig, field, above, ctf_table)

    planes_of, slope = lax.optimization_barrier((planes_of, slope))
    others = [swap(part, "dom", n_dom, 1) for part in planes_of]
    per_device = 2 * count // TILE

    def particles(blocks, before):
        final = len(before) > 0
        return pl.pallas_call(
            functools.partial(particle_kernel, width, mine, n_gz, n_dom, final),
            out_shape=[
                jax.ShapeDtypeStruct((count // 2, width), bf16),
                jax.ShapeDtypeStruct((1, count // 2), f32),
                jax.ShapeDtypeStruct(
                    (devices * per_device if final else per_device // 2, TILE), f32
                ),
            ],
            in_specs=[vmem] * (len(blocks) + 3 + len(before)),
            out_specs=[vmem] * 3,
            compiler_params=params,
            cost_estimate=pl.CostEstimate(
                flops=2 * 10**9, bytes_accessed=2**20, transcendentals=0
            ),
            name="particles",
        )(*blocks, flat_ctf, slope, pairs, *before)

    weighted_own, bins_own, before = particles(planes_of, [])
    weighted, bins_row, parts = particles(others, [before])

    parts = lax.all_to_all(parts, ("gz", "dom"), 0, 0, tiled=True)

    depth = round_up(planes, 8)
    pose, spread = pl.pallas_call(
        functools.partial(
            spread_kernel, spread_groups, spread_table.shape[1], planes, samples, edge_samples, mine, n_gz, n_dom
        ),
        out_shape=[
            jax.ShapeDtypeStruct((1, mine), f32),
            jax.ShapeDtypeStruct((planes, rows, columns), f32),
        ],
        in_specs=[smem, smem] + [vmem] * 7,
        out_specs=[vmem, vmem],
        scratch_shapes=[
            pltpu.VMEM((2 * width // TILE, bins, TILE), f32),
            pltpu.VMEM((xt_count, rows * depth, TILE), f32),
            pltpu.VMEM((count // TILE, TILE), f32),
        ],
        compiler_params=params,
        name="spread",
    )(
        spread_table_flat, trig, right, edges, parts, bins_own, weighted_own, bins_row, weighted
    )
    pose = pose.reshape(mine)
    return pose, spread


def solution(mesh):
    return jax.shard_map(
        local,
        mesh=mesh,
        in_specs=(
            P("gz", None, None),
            P(("gz", "dom"), None, None),
            P(),
            P(("gz", "dom")),
            P(("gz", "dom")),
        ),
        out_specs=(P(("gz", "dom")), P(("gz", "dom"), None, None)),
        check_vma=False,
    )
```
